256 devices in a mesh: dp: 32 (over x, z), seq: 8 (over y, core).
Axes of the slice: x: 4, y: 4, z: 8, core: 2. Of those that a mesh axis runs over, the one named last changes fastest.
Arguments:
- hidden: bfloat16 [32, 32, 128, 1152], P('dp', 'seq'), may hold values from -8 to 8
- spatial_qkv: bfloat16 [32, 32, 128, 1728], P('dp', 'seq'), may hold values from -60 to 60
- out_spatial: bfloat16 [576, 1152], P('seq', 'dp'), may hold values from -0.25 to 0.25
- qkv_temporal: bfloat16 [1152, 1728], P('seq', 'dp'), may hold values from -1 to 1
- out_temporal: bfloat16 [576, 1152], P('seq', 'dp'), may hold values from -0.25 to 0.25
- modulation: float32 [32, 3, 1152], P('dp'), may hold values from -2 to 4
- cotangent: bfloat16 [32, 32, 128, 1152], P('dp', 'seq'), may hold values from -6 to 6
- frame_count: int32 [32], P('dp'), may hold values from 16 to 32, as said below
- patch_height: int32 [32], P('dp'), may hold values from 2 to 16, as said below
- patch_width: int32 [32], P('dp'), may hold values from 8 to 32, as said below
Outputs:
- block_out: bfloat16 [32, 32, 128, 1152], P('dp', 'seq')
- hidden_grad: bfloat16 [32, 32, 128, 1152], P('dp', 'seq')
- spatial_qkv_grad: bfloat16 [32, 32, 128, 1728], P('dp', 'seq')
- out_spatial_grad: float32 [576, 1152], P('seq', 'dp')
- qkv_temporal_grad: float32 [1152, 1728], P('seq', 'dp')
- out_temporal_grad: float32 [576, 1152], P('seq', 'dp')
The draws below stay inside these ranges and needn't reach their ends.
Inputs may be any that keep to these rules, and one draw needn't show every extreme that they name: `frame_count`: some sample has 32 frames and some sample 32 // 2. patch_height * patch_width lies between 64 and 128, and equals 128 for some sample. patch_width is 32, 16 or 8.
All inputs are finite; a program needn't handle non-finite values.
Results may differ from the reference program's by a relative error of at most 0.033.
Values may be sent and summed in bfloat16 or wider, within the bound.
No kernel may reach another device: no remote copies, remote signals or barrier semaphores. Data moves between devices by JAX's collectives and lax.ppermute only.
A program may use at most 128 MiB of HBM per device.

```python
import math
import jax
import jax.numpy as jnp
from jax import lax

D = 1152
HEAD_DIM = 72
HEADS = 8
INNER = 576
SP = 128
FRAMES = 32
SAMPLES = 32
N_SEQ = 8


def patch_shape(key):
    key_a, key_b, key_c = jax.random.split(key, 3)
    power = jax.random.randint(key_a, (SAMPLES,), 2, 5)
    breadth = SP // jnp.power(2, power).astype(jnp.int32)
    lower = SP // (2 * breadth)
    upper = SP // breadth + 1
    height = jax.random.randint(key_b, (SAMPLES,), lower, upper)
    order = jax.random.permutation(key_c, SAMPLES)
    breadth = breadth.at[order[0]].set(SP // 16)
    height = height.at[order[0]].set(16)
    breadth = breadth.at[order[1]].set(SP // 4)
    height = height.at[order[1]].set(2)
    return (height.astype(jnp.int32), breadth.astype(jnp.int32))


def draw_patch_height(key, part):
    return patch_shape(key)[0]


def draw_patch_width(key, part):
    return patch_shape(key)[1]


def draw_frame_count(key, part):
    key = jax.random.fold_in(key, 5)
    key_a, key_b = jax.random.split(key)
    counts = jax.random.randint(key_a, (SAMPLES,), FRAMES // 2, FRAMES + 1)
    order = jax.random.permutation(key_b, SAMPLES)
    counts = counts.at[order[0]].set(FRAMES)
    counts = counts.at[order[1]].set(FRAMES // 2)
    return counts.astype(jnp.int32)


def draw_hidden(key, part):
    key = jax.random.fold_in(key, 7)
    key_a = jax.random.fold_in(key, 0)
    shape = (SAMPLES, FRAMES, SP, D)
    value = jnp.clip(jax.random.normal(key_a, shape, jnp.float32), -6.0, 6.0)
    return value.astype(jnp.bfloat16)


def draw_spatial_qkv(key, part):
    key = jax.random.fold_in(key, 11)
    key_a = jax.random.fold_in(key, 0)
    inner = HEADS * HEAD_DIM
    shape = (SAMPLES, FRAMES, SP, 3 * inner)
    value = jnp.clip(jax.random.normal(key_a, shape, jnp.float32), -6.0, 6.0)
    return value.astype(jnp.bfloat16)


def draw_qkv_temporal(key, part):
    key = jax.random.fold_in(key, 13)
    inner = HEADS * HEAD_DIM
    factor = 1.0 / math.sqrt(D)
    value = jnp.clip(jax.random.normal(key, (D, 3 * inner), jnp.float32), -4.0, 4.0) * factor
    return value.astype(jnp.bfloat16)


def draw_modulation(key, part):
    key = jax.random.fold_in(key, 17)
    key_a, key_b, key_c = jax.random.split(key, 3)
    shape = (SAMPLES, 1, D)
    shift_vec = jnp.clip(0.5 * jax.random.normal(key_a, shape, jnp.float32), -2.0, 2.0)
    scale_vec = jnp.clip(0.3 * jax.random.normal(key_b, shape, jnp.float32), -0.9, 0.9)
    gate_vec = jnp.clip(jax.random.normal(key_c, shape, jnp.float32), -2.0, 2.0)
    return jnp.concatenate([shift_vec, scale_vec, gate_vec], axis=1).astype(jnp.float32)


def steps_of(rng, shape, cuts, smallest, high):
    gain, own = 1.0, jax.random.fold_in(rng, 6)
    for dim, blocks in cuts:
        heights = jnp.exp(jax.random.uniform(jax.random.fold_in(own, dim), (blocks,), jnp.float32, smallest / len(cuts), high / len(cuts)))
        gain = gain * jnp.repeat(heights, shape[dim] // blocks).reshape([-1 if axis == dim else 1 for axis in range(len(shape))])
    return gain


def gaussian(stream_key, dims, deviation, bound, shards=(), kind=jnp.bfloat16):
    array = jax.random.normal(stream_key, dims, jnp.float32) * deviation
    if len(shards) > 0:
        array = steps_of(stream_key, dims, shards, -0.22, 0.18) * array
    return jnp.clip(array, min=-bound, max=bound).astype(kind)


def setup_inputs(seed: int = 0) -> dict:
    arg_keys = jax.random.split(jax.random.key(seed), 11)
    return {
        "hidden": draw_hidden(jax.random.fold_in(arg_keys[10], 71), 0),
        "spatial_qkv": draw_spatial_qkv(jax.random.fold_in(arg_keys[10], 71), 0),
        "out_spatial": gaussian(arg_keys[2], (INNER, D), INNER ** -0.5, 0.25, ((0, 8), (1, 32))),
        "qkv_temporal": draw_qkv_temporal(jax.random.fold_in(arg_keys[10], 71), 0),
        "out_temporal": gaussian(arg_keys[4], (INNER, D), INNER ** -0.5, 0.25, ((0, 8), (1, 32))),
        "modulation": draw_modulation(jax.random.fold_in(arg_keys[10], 71), 0),
        "cotangent": gaussian(arg_keys[6], (SAMPLES, FRAMES, SP, D), 1.0, 6.0, ((0, 32), (1, 8))),
        "frame_count": draw_frame_count(jax.random.fold_in(arg_keys[10], 71), 0),
        "patch_height": draw_patch_height(jax.random.fold_in(arg_keys[10], 71), 0),
        "patch_width": draw_patch_width(jax.random.fold_in(arg_keys[10], 71), 0),
    }


EPSILON = 1e-06
NEGATIVE = -1e+30

def attend(query_rows, key_rows, value_rows, key_valid, layout, factor):
    key_layout = layout.replace('l', 'm')
    logits = jnp.einsum(layout + ',' + key_layout + '->ghlm', query_rows.astype(jnp.float32), key_rows.astype(jnp.float32)) * factor
    logits = jnp.where(key_valid, logits, NEGATIVE)
    largest = lax.optimization_barrier(jnp.max(logits, axis=-1, keepdims=True))
    powers = jnp.exp(logits - largest)
    prob_full = powers / lax.optimization_barrier(jnp.sum(powers, axis=-1, keepdims=True))
    prob_half = prob_full.astype(jnp.bfloat16)
    output = jnp.einsum('ghlm,' + key_layout + '->' + layout, prob_half.astype(jnp.float32), value_rows.astype(jnp.float32))
    return (output.astype(jnp.bfloat16), prob_full, prob_half)

def attend_back(query_rows, key_rows, value_rows, output, out_grad, prob_full, prob_half, layout, factor):
    key_layout = layout.replace('l', 'm')
    grad_f = out_grad.astype(jnp.float32)
    prob_grad = jnp.einsum(layout + ',' + key_layout + '->ghlm', grad_f, value_rows.astype(jnp.float32))
    row_delta = jnp.einsum(layout + ',' + layout + '->ghl', grad_f, output.astype(jnp.float32))[..., None]
    logit_grad = (prob_full * (prob_grad - row_delta)).astype(jnp.bfloat16).astype(jnp.float32)
    grad_query = jnp.einsum('ghlm,' + key_layout + '->' + layout, logit_grad, key_rows.astype(jnp.float32)) * factor
    grad_key = jnp.einsum('ghlm,' + layout + '->' + key_layout, logit_grad, query_rows.astype(jnp.float32)) * factor
    grad_value = jnp.einsum('ghlm,' + layout + '->' + key_layout, prob_half.astype(jnp.float32), grad_f)
    return (grad_query.astype(jnp.bfloat16), grad_key.astype(jnp.bfloat16), grad_value.astype(jnp.bfloat16))

def layer_norm(mixed):
    values = mixed.astype(jnp.float32)
    centred = values - lax.optimization_barrier(jnp.mean(values, axis=-1, keepdims=True))
    inv_std = lax.rsqrt(lax.optimization_barrier(jnp.mean(centred * centred, axis=-1, keepdims=True)) + EPSILON)
    return (centred * inv_std, inv_std)

def block_sum(left, right):
    parts = jnp.einsum('nrc,nrd->ncd', left.astype(jnp.float32), right.astype(jnp.float32))
    rounded = lax.optimization_barrier(parts.astype(jnp.bfloat16))
    return lax.optimization_barrier(jnp.sum(rounded.astype(jnp.float32), axis=0))

def slot_blocks(flat, frame_total, slot_total):
    width = flat.shape[-1]
    shaped = flat.reshape(frame_total, N_SEQ, slot_total // N_SEQ, width)
    return jnp.transpose(shaped, (1, 0, 2, 3)).reshape(N_SEQ, -1, width)

def sample_pass(stream, packed, modulation, grad_out, frames, height, breadth, w_spatial, w_qkv, w_temporal):
    frame_total, slot_total, model_width = stream.shape
    inner = w_spatial.shape[0]
    head_count = inner // HEAD_DIM
    factor = 1.0 / math.sqrt(HEAD_DIM)
    frame_ok = jnp.arange(frame_total, dtype=jnp.int32) < frames
    slot_ok = jnp.arange(slot_total, dtype=jnp.int32) < height * breadth
    token_mask = (frame_ok[:, None] & slot_ok[None, :]).astype(jnp.float32)[..., None]
    shaped = packed.reshape(frame_total, slot_total, 3, head_count, HEAD_DIM)
    query_s, key_s, value_s = (shaped[:, :, 0], shaped[:, :, 1], shaped[:, :, 2])
    out_s, full_s, half_s = attend(query_s, key_s, value_s, slot_ok[None, None, None, :], 'glhd', factor)
    flat_s = out_s.reshape(-1, inner)
    branch_s = jnp.dot(flat_s, w_spatial, preferred_element_type=jnp.float32).reshape(frame_total, slot_total, model_width)
    mixed = (stream.astype(jnp.float32) + token_mask * branch_s).astype(jnp.bfloat16)
    normed, inv_std = layer_norm(mixed)
    shift_vec, scale_vec, gate_vec = (modulation[0], modulation[1], modulation[2])
    modulated = (normed * (1.0 + scale_vec) + shift_vec).astype(jnp.bfloat16)
    flat_mod = modulated.reshape(-1, model_width)
    temporal_qkv = jnp.dot(flat_mod, w_qkv, preferred_element_type=jnp.float32).astype(jnp.bfloat16)
    shaped_t = temporal_qkv.reshape(frame_total, slot_total, 3, head_count, HEAD_DIM)
    query_t, key_t, value_t = (shaped_t[:, :, 0], shaped_t[:, :, 1], shaped_t[:, :, 2])
    out_t, full_t, half_t = attend(query_t, key_t, value_t, frame_ok[None, None, None, :], 'lghd', factor)
    flat_t = out_t.reshape(-1, inner)
    branch_t = jnp.dot(flat_t, w_temporal, preferred_element_type=jnp.float32).reshape(frame_total, slot_total, model_width)
    block_out = (mixed.astype(jnp.float32) + token_mask * gate_vec * branch_t).astype(jnp.bfloat16)
    branch_grad = (token_mask * gate_vec * grad_out.astype(jnp.float32)).astype(jnp.bfloat16).reshape(-1, model_width)
    grad_temporal = block_sum(flat_t.reshape(N_SEQ, -1, inner), branch_grad.reshape(N_SEQ, -1, model_width))
    out_t_grad = jnp.dot(branch_grad, w_temporal.T, preferred_element_type=jnp.float32).astype(jnp.bfloat16)
    out_t_grad = out_t_grad.reshape(frame_total, slot_total, head_count, HEAD_DIM)
    grads_t = attend_back(query_t, key_t, value_t, out_t, out_t_grad, full_t, half_t, 'lghd', factor)
    qkv_t_grad = jnp.stack(grads_t, axis=2).reshape(-1, 3 * inner)
    grad_qkv = block_sum(slot_blocks(flat_mod, frame_total, slot_total), slot_blocks(qkv_t_grad, frame_total, slot_total))
    mod_grad = jnp.dot(qkv_t_grad, w_qkv.T, preferred_element_type=jnp.float32).reshape(frame_total, slot_total, model_width)
    norm_grad = mod_grad * (1.0 + scale_vec)
    ln_grad = inv_std * (norm_grad - lax.optimization_barrier(jnp.mean(norm_grad, axis=-1, keepdims=True)) - normed * lax.optimization_barrier(jnp.mean(norm_grad * normed, axis=-1, keepdims=True)))
    ln_grad = ln_grad.astype(jnp.bfloat16)
    hidden_grad = (grad_out.astype(jnp.float32) + ln_grad.astype(jnp.float32)).astype(jnp.bfloat16)
    spatial_branch_grad = (token_mask * hidden_grad.astype(jnp.float32)).astype(jnp.bfloat16).reshape(-1, model_width)
    grad_spatial = block_sum(flat_s.reshape(N_SEQ, -1, inner), spatial_branch_grad.reshape(N_SEQ, -1, model_width))
    out_s_grad = jnp.dot(spatial_branch_grad, w_spatial.T, preferred_element_type=jnp.float32).astype(jnp.bfloat16)
    out_s_grad = out_s_grad.reshape(frame_total, slot_total, head_count, HEAD_DIM)
    grads_s = attend_back(query_s, key_s, value_s, out_s, out_s_grad, full_s, half_s, 'glhd', factor)
    qkv_s_grad = jnp.stack(grads_s, axis=2).reshape(frame_total, slot_total, 3 * inner)
    return (block_out, hidden_grad, qkv_s_grad, grad_spatial, grad_qkv, grad_temporal)

def reference(hidden, spatial_qkv, out_spatial, qkv_temporal, out_temporal, modulation, cotangent, frame_count, patch_height, patch_width):

    def one_sample(running, sample_item):
        stream, packed, mod_row, grad_out, frames, height, breadth = sample_item
        results = sample_pass(stream, packed, mod_row, grad_out, frames, height, breadth, out_spatial, qkv_temporal, out_temporal)
        summed = (running[0] + results[3], running[1] + results[4], running[2] + results[5])
        return (summed, (results[0], results[1], results[2]))
    zero_grads = (jnp.zeros(out_spatial.shape, jnp.float32), jnp.zeros(qkv_temporal.shape, jnp.float32), jnp.zeros(out_temporal.shape, jnp.float32))
    items = (hidden, spatial_qkv, modulation, cotangent, frame_count, patch_height, patch_width)
    grads, stacked = lax.scan(one_sample, zero_grads, items)
    return (stacked[0], stacked[1], stacked[2], grads[0], grads[1], grads[2])
```

```python
import math

import jax
import jax.numpy as jnp
from jax import lax
from jax.sharding import Mesh
from jax.sharding import PartitionSpec as P

HEAD_DIM = 72


EPSILON = 1e-06
NEGATIVE = -1e30


def attend(query_rows, key_rows, value_rows, key_valid, layout, factor):
    key_layout = layout.replace("l", "m")
    logits = (
        jnp.einsum(
            layout + "," + key_layout + "->ghlm",
            query_rows,
            key_rows,
            preferred_element_type=jnp.float32,
        )
        * factor
    )
    logits = jnp.where(key_valid, logits, NEGATIVE)
    largest = jnp.max(logits, axis=-1, keepdims=True)
    powers = jnp.exp(logits - largest)
    prob_full = powers / jnp.sum(powers, axis=-1, keepdims=True)
    prob_half = prob_full.astype(jnp.bfloat16)
    output = jnp.einsum(
        "ghlm," + key_layout + "->" + layout,
        prob_half,
        value_rows,
        preferred_element_type=jnp.float32,
    )
    return (output.astype(jnp.bfloat16), prob_full, prob_half)


def attend_back(
    query_rows, key_rows, value_rows, output, out_grad, prob_full, prob_half, layout, factor
):
    key_layout = layout.replace("l", "m")
    prob_grad = jnp.einsum(
        layout + "," + key_layout + "->ghlm",
        out_grad,
        value_rows,
        preferred_element_type=jnp.float32,
    )
    row_delta = jnp.einsum(
        layout + "," + layout + "->ghl", out_grad, output, preferred_element_type=jnp.float32
    )[..., None]
    logit_grad = (prob_full * (prob_grad - row_delta)).astype(jnp.bfloat16)
    grad_query = (
        jnp.einsum(
            "ghlm," + key_layout + "->" + layout,
            logit_grad,
            key_rows,
            preferred_element_type=jnp.float32,
        )
        * factor
    )
    grad_key = (
        jnp.einsum(
            "ghlm," + layout + "->" + key_layout,
            logit_grad,
            query_rows,
            preferred_element_type=jnp.float32,
        )
        * factor
    )
    grad_value = jnp.einsum(
        "ghlm," + layout + "->" + key_layout,
        prob_half,
        out_grad,
        preferred_element_type=jnp.float32,
    )
    return (
        grad_query.astype(jnp.bfloat16),
        grad_key.astype(jnp.bfloat16),
        grad_value.astype(jnp.bfloat16),
    )


def layer_norm(mixed):
    values = mixed.astype(jnp.float32)
    centred = values - jnp.mean(values, axis=-1, keepdims=True)
    inv_std = lax.rsqrt(jnp.mean(centred * centred, axis=-1, keepdims=True) + EPSILON)
    return (centred * inv_std, inv_std)


def transposed_product(left, right):
    return jnp.einsum("rc,rd->cd", left, right, preferred_element_type=jnp.float32)


def product_by_transpose(left, right):
    return jnp.einsum("rd,cd->rc", left, right, preferred_element_type=jnp.float32)


def weight_rows(out_spatial, qkv_temporal, out_temporal):
    packed = jnp.concatenate(
        [jnp.concatenate([out_spatial.T, out_temporal.T], axis=1), qkv_temporal.T], axis=0
    )
    near = lax.all_gather(packed, ("y", "c"), axis=0, tiled=False)
    narrow = out_spatial.shape[1]
    half = out_spatial.shape[0]
    pair = jnp.transpose(near[:, :narrow], (1, 0, 2))
    first = pair[:, :, :half].reshape(narrow, -1)
    second = pair[:, :, half:].reshape(narrow, -1)
    wide = jnp.transpose(near[:, narrow:], (1, 0, 2)).reshape(near.shape[1] - narrow, -1)
    rows = jnp.concatenate([jnp.concatenate([first, second], axis=1), wide], axis=0)
    far = lax.all_gather(rows, ("x", "z"), axis=0, tiled=False)
    inner = first.shape[1]
    w_pair = far[:, :narrow].reshape(-1, 2 * inner)
    w_wide = far[:, narrow:].reshape(-1, far.shape[2])
    return (w_pair[:, :inner], w_wide, w_pair[:, inner:])


def exchange(rows, axes):
    return lax.all_to_all(rows, axes, 0, 0, tiled=True)


def halve_and_quarter(terms):
    split = terms.reshape((4, 2) + terms.shape[1:])
    split = jnp.transpose(split, (1, 0, 2, 3))
    pairs = exchange(split, "c").astype(jnp.float32)
    pairs = (pairs[0] + pairs[1]).astype(jnp.bfloat16)
    quads = exchange(pairs, "y").astype(jnp.float32)
    return ((quads[0] + quads[1]) + (quads[2] + quads[3])).astype(jnp.bfloat16)


def on_device(
    hidden,
    spatial_qkv,
    out_spatial,
    qkv_temporal,
    out_temporal,
    modulation,
    cotangent,
    frame_count,
    patch_height,
    patch_width,
):
    seq_count = lax.axis_size(("y", "c"))
    seq_place = lax.axis_index(("y", "c"))
    stream = hidden[0]
    grad_out = cotangent[0]
    frame_dev, slot_total, model_width = stream.shape
    frame_total = frame_dev * seq_count
    slot_dev = slot_total // seq_count
    factor = 1.0 / math.sqrt(HEAD_DIM)

    def to_slots(rows):
        width = rows.shape[-1]
        split = rows.reshape(frame_dev, seq_count, slot_dev, width)
        moved = exchange(jnp.transpose(split, (1, 0, 2, 3)), ("y", "c"))
        return moved.reshape(frame_total, slot_dev, width)

    def to_frames(rows):
        width = rows.shape[-1]
        split = rows.reshape(seq_count, frame_dev, slot_dev, width)
        moved = jnp.transpose(exchange(split, ("y", "c")), (1, 0, 2, 3))
        return moved.reshape(frame_dev, slot_total, width)

    w_spatial, w_qkv, w_temporal = weight_rows(out_spatial, qkv_temporal, out_temporal)
    inner = w_spatial.shape[1]
    head_count = inner // HEAD_DIM
    frames = frame_count[0]
    slot_limit = patch_height[0] * patch_width[0]
    frame_here = seq_place * frame_dev + jnp.arange(frame_dev, dtype=jnp.int32)
    slot_here = seq_place * slot_dev + jnp.arange(slot_dev, dtype=jnp.int32)
    slot_ok = jnp.arange(slot_total, dtype=jnp.int32) < slot_limit
    frame_ok = jnp.arange(frame_total, dtype=jnp.int32) < frames
    mask_f = ((frame_here < frames)[:, None] & slot_ok[None, :]).astype(jnp.float32)[..., None]
    mask_s = (frame_ok[:, None] & (slot_here < slot_limit)[None, :]).astype(jnp.float32)[..., None]
    shift_vec, scale_vec, gate_vec = (modulation[0, 0], modulation[0, 1], modulation[0, 2])

    stream_s = to_slots(stream)
    grad_out_s = to_slots(grad_out)
    shaped = spatial_qkv[0].reshape(frame_dev, slot_total, 3, head_count, HEAD_DIM)
    query_s, key_s, value_s = (shaped[:, :, 0], shaped[:, :, 1], shaped[:, :, 2])
    out_s, full_s, half_s = attend(
        query_s, key_s, value_s, slot_ok[None, None, None, :], "glhd", factor
    )
    rows_s = out_s.reshape(frame_dev, slot_total, inner)
    flat_s = to_slots(rows_s).reshape(-1, inner)

    branch_s = product_by_transpose(flat_s, w_spatial).reshape(frame_total, slot_dev, model_width)
    mixed_s = (stream_s.astype(jnp.float32) + mask_s * branch_s).astype(jnp.bfloat16)
    normed, inv_std = layer_norm(mixed_s)
    modulated = (normed * (1.0 + scale_vec) + shift_vec).astype(jnp.bfloat16)
    flat_mod = modulated.reshape(-1, model_width)
    temporal_qkv = product_by_transpose(flat_mod, w_qkv).astype(jnp.bfloat16)
    shaped_t = temporal_qkv.reshape(frame_total, slot_dev, 3, head_count, HEAD_DIM)
    query_t, key_t, value_t = (shaped_t[:, :, 0], shaped_t[:, :, 1], shaped_t[:, :, 2])
    out_t, full_t, half_t = attend(
        query_t, key_t, value_t, frame_ok[None, None, None, :], "lghd", factor
    )
    rows_t = out_t.reshape(frame_total, slot_dev, inner)
    flat_t = rows_t.reshape(-1, inner)

    branch_grad = (
        (mask_s * gate_vec * grad_out_s.astype(jnp.float32))
        .astype(jnp.bfloat16)
        .reshape(-1, model_width)
    )
    grad_temporal = transposed_product(flat_t, branch_grad).astype(jnp.bfloat16)
    out_t_grad = jnp.dot(branch_grad, w_temporal, preferred_element_type=jnp.float32)
    out_t_grad = out_t_grad.astype(jnp.bfloat16).reshape(
        frame_total, slot_dev, head_count, HEAD_DIM
    )
    grads_t = attend_back(
        query_t, key_t, value_t, out_t, out_t_grad, full_t, half_t, "lghd", factor
    )
    qkv_t_grad = jnp.stack(grads_t, axis=2).reshape(-1, 3 * inner)
    grad_qkv = transposed_product(flat_mod, qkv_t_grad).astype(jnp.bfloat16)
    mod_grad = jnp.dot(qkv_t_grad, w_qkv, preferred_element_type=jnp.float32)
    norm_grad = mod_grad.reshape(frame_total, slot_dev, model_width) * (1.0 + scale_vec)
    ln_grad = inv_std * (
        norm_grad
        - jnp.mean(norm_grad, axis=-1, keepdims=True)
        - normed * jnp.mean(norm_grad * normed, axis=-1, keepdims=True)
    )
    ln_grad = ln_grad.astype(jnp.bfloat16)
    hidden_grad_s = (grad_out_s.astype(jnp.float32) + ln_grad.astype(jnp.float32)).astype(
        jnp.bfloat16
    )
    branch_grad_s = (
        (mask_s * hidden_grad_s.astype(jnp.float32)).astype(jnp.bfloat16).reshape(-1, model_width)
    )
    grad_spatial = transposed_product(flat_s, branch_grad_s).astype(jnp.bfloat16)
    ln_frames = to_frames(ln_grad)

    sum_qkv = halve_and_quarter(grad_qkv.reshape(seq_count, -1, 3 * inner))
    grad_pair = jnp.concatenate(
        [grad_spatial.reshape(seq_count, -1, model_width), grad_temporal.reshape(seq_count, -1, model_width)],
        axis=1,
    )
    sum_pair = halve_and_quarter(grad_pair)
    dp_count = lax.axis_size(("x", "z"))
    chunks = jnp.concatenate(
        [
            sum_pair.T.reshape(dp_count, -1, sum_pair.shape[0]),
            sum_qkv.T.reshape(dp_count, -1, sum_qkv.shape[0]),
        ],
        axis=1,
    )
    total = jnp.sum(exchange(chunks, ("x", "z")).astype(jnp.float32), axis=0)
    narrow = out_spatial.shape[1]
    half = out_spatial.shape[0]
    summed = (total[:narrow, :half].T, total[narrow:].T, total[:narrow, half:].T)

    frames_t = to_frames(rows_t).reshape(-1, inner)
    branch_t = product_by_transpose(frames_t, w_temporal).reshape(
        frame_dev, slot_total, model_width
    )
    branch_f = product_by_transpose(rows_s.reshape(-1, inner), w_spatial).reshape(
        frame_dev, slot_total, model_width
    )
    mixed = (stream.astype(jnp.float32) + mask_f * branch_f).astype(jnp.bfloat16)
    block_out = (mixed.astype(jnp.float32) + mask_f * gate_vec * branch_t).astype(jnp.bfloat16)
    hidden_grad = (grad_out.astype(jnp.float32) + ln_frames.astype(jnp.float32)).astype(
        jnp.bfloat16
    )
    spatial_branch_grad = (
        (mask_f * hidden_grad.astype(jnp.float32)).astype(jnp.bfloat16).reshape(-1, model_width)
    )
    out_s_grad = jnp.dot(spatial_branch_grad, w_spatial, preferred_element_type=jnp.float32)
    out_s_grad = out_s_grad.astype(jnp.bfloat16).reshape(
        frame_dev, slot_total, head_count, HEAD_DIM
    )
    grads_s = attend_back(
        query_s, key_s, value_s, out_s, out_s_grad, full_s, half_s, "glhd", factor
    )
    qkv_s_grad = jnp.stack(grads_s, axis=2).reshape(frame_dev, slot_total, 3 * inner)
    return (block_out[None], hidden_grad[None], qkv_s_grad[None], summed[0], summed[1], summed[2])


def solution(mesh):
    torus = Mesh(mesh.devices.reshape(4, 8, 4, 2), ("x", "z", "y", "c"))
    dp, seq = ("x", "z"), ("y", "c")
    tokens = P(dp, seq, None, None)
    weight = P(seq, dp)
    placed = (
        tokens,
        tokens,
        weight,
        weight,
        weight,
        P(dp, None, None),
        tokens,
        P(dp),
        P(dp),
        P(dp),
    )
    return jax.shard_map(
        on_device,
        mesh=torus,
        in_specs=placed,
        out_specs=(tokens, tokens, tokens, weight, weight, weight),
        check_vma=False,
    )
```

```python
import functools
import math

import jax
import jax.numpy as jnp
from jax import lax
from jax.experimental import pallas as pl
from jax.experimental.pallas import tpu as pltpu
from jax.sharding import Mesh
from jax.sharding import PartitionSpec as P

HEAD_DIM = 72
EPSILON = 1e-06
NEGATIVE = -1e30
LANES = 128
VMEM_BYTES = 56 * 1024 * 1024
F32 = jnp.float32
BF16 = jnp.bfloat16


def dot_nn(left, right):
    return lax.dot_general(left, right, (((1,), (0,)), ((), ())), preferred_element_type=F32)


def dot_nt(left, right):
    return lax.dot_general(left, right, (((1,), (1,)), ((), ())), preferred_element_type=F32)


def dot_tn(left, right):
    return lax.dot_general(left, right, (((0,), (0,)), ((), ())), preferred_element_type=F32)


def head_windows(inner):
    windows = []
    for head in range(inner // HEAD_DIM):
        low = head * HEAD_DIM
        start = low // LANES * LANES
        stop = min(-(-(low + HEAD_DIM) // LANES) * LANES, inner)
        windows.append((start, stop, low - start))
    return windows


def own_lanes(window):
    start, stop, offset = window
    lane = lax.broadcasted_iota(jnp.int32, (1, stop - start), 1)
    return (lane >= offset) & (lane < offset + HEAD_DIM)


def only(lanes, rows):
    return jnp.where(lanes, rows, jnp.zeros((), rows.dtype))


def softmax_rows(query, key, allowed):
    logits = dot_nt(query, key) * (1.0 / math.sqrt(HEAD_DIM))
    logits = jnp.where(allowed, logits, NEGATIVE)
    powers = jnp.exp(logits - jnp.max(logits, axis=1, keepdims=True))
    return powers * (1.0 / jnp.sum(powers, axis=1, keepdims=True))


def attend_heads(query, key, value, allowed, out_acc):
    out_acc[...] = jnp.zeros(out_acc.shape, F32)
    for window in head_windows(query.shape[1]):
        start, stop, _ = window
        lanes = own_lanes(window)
        probs = softmax_rows(query[:, start:stop], only(lanes, key[:, start:stop]), allowed)
        out_acc[:, start:stop] += dot_nn(probs.astype(BF16), only(lanes, value[:, start:stop]))


def attend_heads_back(query, key, value, out, out_grad, allowed, q_acc, k_acc, v_acc):
    factor = 1.0 / math.sqrt(HEAD_DIM)
    for acc in (q_acc, k_acc, v_acc):
        acc[...] = jnp.zeros(acc.shape, F32)
    for window in head_windows(query.shape[1]):
        start, stop, _ = window
        lanes = own_lanes(window)
        key_h = only(lanes, key[:, start:stop])
        grad_h = only(lanes, out_grad[:, start:stop])
        probs = softmax_rows(query[:, start:stop], key_h, allowed)
        prob_grad = dot_nt(grad_h, value[:, start:stop])
        row_delta = jnp.sum(
            grad_h.astype(F32) * out[:, start:stop].astype(F32), axis=1, keepdims=True
        )
        logit_grad = (probs * (prob_grad - row_delta)).astype(BF16)
        q_acc[:, start:stop] += dot_nn(logit_grad, key_h) * factor
        k_acc[:, start:stop] += dot_tn(logit_grad, only(lanes, query[:, start:stop])) * factor
        v_acc[:, start:stop] += dot_tn(probs.astype(BF16), grad_h)


def slot_masks(info_ref, rows, slots):
    frames, limit, first = info_ref[0], info_ref[1], info_ref[2]
    group = pl.program_id(0)
    row = lax.broadcasted_iota(jnp.int32, (rows, 1), 0)
    slot = first + group * slots + row % slots
    token = (row // slots < frames) & (slot < limit)
    col = lax.broadcasted_iota(jnp.int32, (1, rows), 1)
    allowed = (row % slots == col % slots) & (col // slots < frames)
    return token.astype(F32), allowed


def normalised(mixed):
    values = mixed.astype(F32)
    centred = values - jnp.mean(values, axis=1, keepdims=True)
    inv_std = lax.rsqrt(jnp.mean(centred * centred, axis=1, keepdims=True) + EPSILON)
    return centred * inv_std, inv_std


def temporal_forward(
    info, mod, stream, out_s, w_spatial, w_qkv, mixed_ref, mod_ref, qkv_ref, out_ref, acc, slots
):
    rows, inner = acc.shape
    width = w_spatial.shape[0]
    token, allowed = slot_masks(info, rows, slots)
    branch = dot_nt(out_s[...].reshape(rows, inner), w_spatial[...])
    mixed = (stream[...].reshape(rows, width).astype(F32) + token * branch).astype(BF16)
    mixed_ref[...] = mixed.reshape(mixed_ref.shape)
    normed, _ = normalised(mixed)
    modulated = (normed * (1.0 + mod[0, 1:2]) + mod[0, 0:1]).astype(BF16)
    mod_ref[...] = modulated.reshape(mod_ref.shape)
    qkv = dot_nt(modulated, w_qkv[...]).astype(BF16)
    qkv_ref[...] = qkv.reshape(qkv_ref.shape)
    attend_heads(
        qkv[:, :inner], qkv[:, inner : 2 * inner], qkv[:, 2 * inner :], allowed, acc
    )
    out_ref[...] = acc[...].astype(BF16).reshape(out_ref.shape)


def temporal_backward(
    info, mod, grad, qkv_ref, out_t, modulated, w_temporal, dqkv_ref, g_temporal, g_qkv,
    q_acc, k_acc, v_acc, sum_t, sum_q, slots
):
    rows, inner = q_acc.shape
    width = w_temporal.shape[0]
    token, allowed = slot_masks(info, rows, slots)
    branch_grad = (token * mod[0, 2:3] * grad[...].reshape(rows, width).astype(F32)).astype(BF16)
    out_grad = dot_nn(branch_grad, w_temporal[...]).astype(BF16)
    qkv = qkv_ref[...].reshape(rows, 3 * inner)
    out = out_t[...].reshape(rows, inner)
    attend_heads_back(
        qkv[:, :inner], qkv[:, inner : 2 * inner], qkv[:, 2 * inner :], out, out_grad, allowed,
        q_acc, k_acc, v_acc,
    )
    dqkv = jnp.concatenate([q_acc[...], k_acc[...], v_acc[...]], axis=1).astype(BF16)
    dqkv_ref[...] = dqkv.reshape(dqkv_ref.shape)
    part_t = dot_tn(out, branch_grad)
    part_q = dot_tn(modulated[...].reshape(rows, width), dqkv)

    @pl.when(pl.program_id(0) == 0)
    def _():
        sum_t[...] = part_t
        sum_q[...] = part_q

    @pl.when(pl.program_id(0) > 0)
    def _():
        sum_t[...] += part_t
        sum_q[...] += part_q

    @pl.when(pl.program_id(0) == pl.num_programs(0) - 1)
    def _():
        g_temporal[...] = sum_t[...].astype(BF16)
        g_qkv[...] = sum_q[...].astype(BF16)


def norm_backward(
    info, mod, grad, mixed, out_s, dqkv, w_qkv, ln_ref, g_spatial, sum_s, slots
):
    rows = dqkv.shape[1]
    width = w_qkv.shape[1]
    token, _ = slot_masks(info, rows, slots)
    norm_grad = dot_nn(dqkv[...].reshape(rows, -1), w_qkv[...]) * (1.0 + mod[0, 1:2])
    normed, inv_std = normalised(mixed[...].reshape(rows, width))
    first = jnp.mean(norm_grad, axis=1, keepdims=True)
    second = jnp.mean(norm_grad * normed, axis=1, keepdims=True)
    ln_grad = (inv_std * (norm_grad - first - normed * second)).astype(BF16)
    ln_ref[...] = ln_grad.reshape(ln_ref.shape)
    grad_f = grad[...].reshape(rows, width).astype(F32)
    hidden_grad = (grad_f + ln_grad.astype(F32)).astype(BF16)
    branch_grad = (token * hidden_grad.astype(F32)).astype(BF16)
    part = dot_tn(out_s[...].reshape(rows, -1), branch_grad)

    @pl.when(pl.program_id(0) == 0)
    def _():
        sum_s[...] = part

    @pl.when(pl.program_id(0) > 0)
    def _():
        sum_s[...] += part

    @pl.when(pl.program_id(0) == pl.num_programs(0) - 1)
    def _():
        g_spatial[...] = sum_s[...].astype(BF16)


def frame_keys(info_ref, rows):
    return lax.broadcasted_iota(jnp.int32, (1, rows), 1) < info_ref[1]


def frame_tokens(info_ref, rows):
    row = lax.broadcasted_iota(jnp.int32, (rows, 1), 0)
    alive = info_ref[3] + pl.program_id(0) < info_ref[0]
    return ((row < info_ref[1]) & alive).astype(F32)


def spatial_forward(info, qkv_ref, out_ref, acc):
    rows, inner = acc.shape
    qkv = qkv_ref[0]
    attend_heads(
        qkv[:, :inner], qkv[:, inner : 2 * inner], qkv[:, 2 * inner :], frame_keys(info, rows), acc
    )
    out_ref[0] = acc[...].astype(BF16)


def block_forward(info, mod, stream, out_s, out_t, w_spatial, w_temporal, block_ref):
    rows = stream.shape[1]
    token = frame_tokens(info, rows)
    mixed = (stream[0].astype(F32) + token * dot_nt(out_s[0], w_spatial[...])).astype(BF16)
    branch = dot_nt(out_t[0], w_temporal[...])
    block_ref[0] = (mixed.astype(F32) + token * mod[0, 2:3] * branch).astype(BF16)


def spatial_backward(
    info, grad, ln_grad, qkv_ref, out_s, w_spatial, hidden_ref, dqkv_ref, q_acc, k_acc, v_acc
):
    rows, inner = q_acc.shape
    hidden_grad = (grad[0].astype(F32) + ln_grad[0].astype(F32)).astype(BF16)
    hidden_ref[0] = hidden_grad
    branch_grad = (frame_tokens(info, rows) * hidden_grad.astype(F32)).astype(BF16)
    out_grad = dot_nn(branch_grad, w_spatial[...]).astype(BF16)
    qkv = qkv_ref[0]
    attend_heads_back(
        qkv[:, :inner], qkv[:, inner : 2 * inner], qkv[:, 2 * inner :], out_s[0], out_grad,
        frame_keys(info, rows), q_acc, k_acc, v_acc,
    )
    dqkv_ref[0] = jnp.concatenate([q_acc[...], k_acc[...], v_acc[...]], axis=1).astype(BF16)


def whole(array):
    return pl.BlockSpec(array.shape, lambda step: (0,) * array.ndim)


def per_frame(array):
    return pl.BlockSpec((1,) + array.shape[1:], lambda step: (step, 0, 0))


def per_group(array):
    return pl.BlockSpec(
        (array.shape[0], 1) + array.shape[2:], lambda step: (0, step, 0, 0)
    )


SCALARS = pl.BlockSpec(memory_space=pltpu.SMEM)


def run(body, steps, operands, specs, results, result_specs, scratch, flops):
    leaves = operands + jax.tree.leaves(results)
    moved = sum(math.prod(a.shape) * a.dtype.itemsize for a in leaves)
    return pl.pallas_call(
        body,
        grid=(steps,),
        in_specs=specs,
        out_specs=result_specs,
        out_shape=results,
        scratch_shapes=scratch,
        compiler_params=pltpu.CompilerParams(vmem_limit_bytes=VMEM_BYTES),
        cost_estimate=pl.CostEstimate(flops=flops, bytes_accessed=moved, transcendentals=0),
    )(*operands)


def shape_of(*dims, dtype=BF16):
    return jax.ShapeDtypeStruct(dims, dtype)


def weight_rows(out_spatial, qkv_temporal, out_temporal):
    packed = jnp.concatenate(
        [jnp.concatenate([out_spatial.T, out_temporal.T], axis=1), qkv_temporal.T], axis=0
    )
    near = lax.all_gather(packed, ("y", "c"), axis=0, tiled=False)
    narrow = out_spatial.shape[1]
    half = out_spatial.shape[0]
    pair = jnp.transpose(near[:, :narrow], (1, 0, 2))
    first = pair[:, :, :half].reshape(narrow, -1)
    second = pair[:, :, half:].reshape(narrow, -1)
    wide = jnp.transpose(near[:, narrow:], (1, 0, 2)).reshape(near.shape[1] - narrow, -1)
    rows = jnp.concatenate([jnp.concatenate([first, second], axis=1), wide], axis=0)
    far = lax.all_gather(rows, ("x", "z"), axis=0, tiled=False)
    inner = first.shape[1]
    w_pair = far[:, :narrow].reshape(-1, 2 * inner)
    w_wide = far[:, narrow:].reshape(-1, far.shape[2])
    return (w_pair[:, :inner], w_wide, w_pair[:, inner:])


def exchange(rows, axes):
    return lax.all_to_all(rows, axes, 0, 0, tiled=True)


def halve_and_quarter(terms):
    split = terms.reshape((4, 2) + terms.shape[1:])
    split = jnp.transpose(split, (1, 0, 2, 3))
    pairs = exchange(split, "c").astype(F32)
    pairs = (pairs[0] + pairs[1]).astype(BF16)
    quads = exchange(pairs, "y").astype(F32)
    return ((quads[0] + quads[1]) + (quads[2] + quads[3])).astype(BF16)


def reduce_grads(g_spatial, g_qkv, g_temporal):
    seq_count = lax.axis_size(("y", "c"))
    dp_count = lax.axis_size(("x", "z"))
    width = g_spatial.shape[1]
    sum_qkv = halve_and_quarter(g_qkv.reshape(seq_count, -1, g_qkv.shape[1]))
    pair = [g.reshape(seq_count, -1, width) for g in (g_spatial, g_temporal)]
    sum_pair = halve_and_quarter(jnp.concatenate(pair, axis=1))
    chunks = jnp.concatenate(
        [
            sum_pair.T.reshape(dp_count, -1, sum_pair.shape[0]),
            sum_qkv.T.reshape(dp_count, -1, sum_qkv.shape[0]),
        ],
        axis=1,
    )
    total = jnp.sum(exchange(chunks, ("x", "z")).astype(F32), axis=0)
    narrow = width // dp_count
    half = sum_pair.shape[0] // 2
    return (total[:narrow, :half].T, total[narrow:].T, total[:narrow, half:].T)


def on_device(
    hidden,
    spatial_qkv,
    out_spatial,
    qkv_temporal,
    out_temporal,
    modulation,
    cotangent,
    frame_count,
    patch_height,
    patch_width,
):
    seq_count = lax.axis_size(("y", "c"))
    seq_place = lax.axis_index(("y", "c"))
    stream = hidden[0]
    grad_out = cotangent[0]
    packed_qkv = spatial_qkv[0]
    frame_dev, slot_total, width = stream.shape
    slot_dev = slot_total // seq_count
    inner = out_spatial.shape[0] * seq_count
    slots = 8
    groups = slot_dev // slots
    rows = frame_dev * seq_count * slots
    info = jnp.stack(
        [
            frame_count[0],
            patch_height[0] * patch_width[0],
            seq_place * slot_dev,
            seq_place * frame_dev,
        ]
    ).astype(jnp.int32)

    def to_slots(tokens):
        split = tokens.reshape(frame_dev, seq_count, groups, slots, -1)
        split = jnp.transpose(split, (1, 2, 0, 3, 4))
        return exchange(split.reshape(seq_count, groups, frame_dev * slots, -1), ("y", "c"))

    def to_frames(tokens):
        moved = exchange(tokens, ("y", "c")).reshape(seq_count, groups, frame_dev, slots, -1)
        return jnp.transpose(moved, (2, 0, 1, 3, 4)).reshape(frame_dev, slot_total, -1)

    stream_s = to_slots(stream)
    frame_acc = pltpu.VMEM((slot_total, inner), F32)
    out_s = shape_of(frame_dev, slot_total, inner)
    out_s = run(
        spatial_forward,
        frame_dev,
        [info, packed_qkv],
        [SCALARS, per_frame(packed_qkv)],
        out_s,
        per_frame(out_s),
        [frame_acc],
        4 * frame_dev * slot_total * slot_total * inner,
    )
    out_s_s = to_slots(out_s)
    grad_s = to_slots(grad_out)
    w_spatial, w_qkv, w_temporal = weight_rows(out_spatial, qkv_temporal, out_temporal)

    group_acc = pltpu.VMEM((rows, inner), F32)
    result = (
        shape_of(groups, rows, width),
        shape_of(groups, rows, width),
        shape_of(groups, rows, 3 * inner),
        shape_of(seq_count, groups, rows // seq_count, inner),
    )
    tokens = groups * rows
    mixed_s, modulated, qkv_t, out_t = run(
        functools.partial(temporal_forward, slots=slots),
        groups,
        [info, modulation, stream_s, out_s_s, w_spatial, w_qkv],
        [SCALARS, whole(modulation), per_group(stream_s), per_group(out_s_s), whole(w_spatial), whole(w_qkv)],
        result,
        [per_frame(result[0]), per_frame(result[1]), per_frame(result[2]), per_group(result[3])],
        [group_acc],
        8 * tokens * width * inner + 4 * tokens * rows * inner,
    )
    out_t_f = to_frames(out_t)

    result = (
        shape_of(groups, rows, 3 * inner),
        shape_of(inner, width),
        shape_of(width, 3 * inner),
    )
    dqkv_t, g_temporal, g_qkv = run(
        functools.partial(temporal_backward, slots=slots),
        groups,
        [info, modulation, grad_s, qkv_t, out_t, modulated, w_temporal],
        [SCALARS, whole(modulation), per_group(grad_s), per_frame(qkv_t), per_group(out_t), per_frame(modulated), whole(w_temporal)],
        result,
        [per_frame(result[0]), whole(result[1]), whole(result[2])],
        [group_acc, group_acc, group_acc, pltpu.VMEM((inner, width), F32), pltpu.VMEM((width, 3 * inner), F32)],
        10 * tokens * width * inner + 10 * tokens * rows * inner,
    )
    result = (
        shape_of(seq_count, groups, rows // seq_count, width),
        shape_of(inner, width),
    )
    ln_grad, g_spatial = run(
        functools.partial(norm_backward, slots=slots),
        groups,
        [info, modulation, grad_s, mixed_s, out_s_s, dqkv_t, w_qkv],
        [SCALARS, whole(modulation), per_group(grad_s), per_frame(mixed_s), per_group(out_s_s), per_frame(dqkv_t), whole(w_qkv)],
        result,
        [per_group(result[0]), whole(result[1])],
        [pltpu.VMEM((inner, width), F32)],
        8 * tokens * width * inner,
    )
    ln_frames = to_frames(ln_grad)
    summed = reduce_grads(g_spatial, g_qkv, g_temporal)

    block_out = shape_of(frame_dev, slot_total, width)
    block_out = run(
        block_forward,
        frame_dev,
        [info, modulation, stream, out_s, out_t_f, w_spatial, w_temporal],
        [SCALARS, whole(modulation), per_frame(stream), per_frame(out_s), per_frame(out_t_f), whole(w_spatial), whole(w_temporal)],
        block_out,
        per_frame(block_out),
        [],
        4 * tokens * width * inner,
    )
    result = (shape_of(frame_dev, slot_total, width), shape_of(frame_dev, slot_total, 3 * inner))
    hidden_grad, qkv_s_grad = run(
        spatial_backward,
        frame_dev,
        [info, grad_out, ln_frames, packed_qkv, out_s, w_spatial],
        [SCALARS, per_frame(grad_out), per_frame(ln_frames), per_frame(packed_qkv), per_frame(out_s), whole(w_spatial)],
        result,
        [per_frame(result[0]), per_frame(result[1])],
        [frame_acc, frame_acc, frame_acc],
        2 * tokens * width * inner + 10 * tokens * slot_total * inner,
    )
    return (block_out[None], hidden_grad[None], qkv_s_grad[None], summed[0], summed[1], summed[2])


def solution(mesh):
    torus = Mesh(mesh.devices.reshape(4, 8, 4, 2), ("x", "z", "y", "c"))
    dp, seq = ("x", "z"), ("y", "c")
    tokens = P(dp, seq, None, None)
    weight = P(seq, dp)
    placed = (
        tokens,
        tokens,
        weight,
        weight,
        weight,
        P(dp, None, None),
        tokens,
        P(dp),
        P(dp),
        P(dp),
    )
    return jax.shard_map(
        on_device,
        mesh=torus,
        in_specs=placed,
        out_specs=(tokens, tokens, tokens, weight, weight, weight),
        check_vma=False,
    )
```

```python
import functools
import math

import jax
import jax.numpy as jnp
from jax import lax
from jax.experimental import pallas as pl
from jax.experimental.pallas import tpu as pltpu
from jax.sharding import Mesh
from jax.sharding import PartitionSpec as P

HEAD_DIM = 72
EPSILON = 1e-06
NEGATIVE = -1e30
LANES = 128
VMEM_BYTES = 56 * 1024 * 1024
F32 = jnp.float32
BF16 = jnp.bfloat16


def dot_nn(left, right):
    return lax.dot_general(left, right, (((1,), (0,)), ((), ())), preferred_element_type=F32)


def dot_nt(left, right):
    return lax.dot_general(left, right, (((1,), (1,)), ((), ())), preferred_element_type=F32)


def dot_tn(left, right):
    return lax.dot_general(left, right, (((0,), (0,)), ((), ())), preferred_element_type=F32)


def head_windows(inner):
    windows = []
    for head in range(inner // HEAD_DIM):
        low = head * HEAD_DIM
        start = low // LANES * LANES
        stop = min(-(-(low + HEAD_DIM) // LANES) * LANES, inner)
        windows.append((start, stop, low - start))
    return windows


def own_lanes(window):
    start, stop, offset = window
    lane = lax.broadcasted_iota(jnp.int32, (1, stop - start), 1)
    return (lane >= offset) & (lane < offset + HEAD_DIM)


def only(lanes, rows):
    return jnp.where(lanes, rows, jnp.zeros((), rows.dtype))


def softmax_rows(query, key, allowed):
    logits = dot_nt(query, key) * (1.0 / math.sqrt(HEAD_DIM))
    logits = jnp.where(allowed, logits, NEGATIVE)
    powers = jnp.exp(logits - jnp.max(logits, axis=1, keepdims=True))
    return powers * (1.0 / jnp.sum(powers, axis=1, keepdims=True))


def attend_heads(query, key, value, allowed, out_acc):
    out_acc[...] = jnp.zeros(out_acc.shape, F32)
    for window in head_windows(query.shape[1]):
        start, stop, _ = window
        lanes = own_lanes(window)
        probs = softmax_rows(query[:, start:stop], only(lanes, key[:, start:stop]), allowed)
        out_acc[:, start:stop] += dot_nn(probs.astype(BF16), only(lanes, value[:, start:stop]))


def attend_heads_back(query, key, value, out, out_grad, allowed, q_acc, k_acc, v_acc):
    factor = 1.0 / math.sqrt(HEAD_DIM)
    for acc in (q_acc, k_acc, v_acc):
        acc[...] = jnp.zeros(acc.shape, F32)
    for window in head_windows(query.shape[1]):
        start, stop, _ = window
        lanes = own_lanes(window)
        key_h = only(lanes, key[:, start:stop])
        grad_h = only(lanes, out_grad[:, start:stop])
        probs = softmax_rows(query[:, start:stop], key_h, allowed)
        prob_grad = dot_nt(grad_h, value[:, start:stop])
        row_delta = jnp.sum(
            grad_h.astype(F32) * out[:, start:stop].astype(F32), axis=1, keepdims=True
        )
        logit_grad = (probs * (prob_grad - row_delta)).astype(BF16)
        q_acc[:, start:stop] += dot_nn(logit_grad, key_h) * factor
        k_acc[:, start:stop] += dot_tn(logit_grad, only(lanes, query[:, start:stop])) * factor
        v_acc[:, start:stop] += dot_tn(probs.astype(BF16), grad_h)


def slot_masks(info_ref, rows, slots):
    frames, limit, first = info_ref[0], info_ref[1], info_ref[2]
    group = pl.program_id(0)
    row = lax.broadcasted_iota(jnp.int32, (rows, 1), 0)
    slot = first + group * slots + row % slots
    token = (row // slots < frames) & (slot < limit)
    col = lax.broadcasted_iota(jnp.int32, (1, rows), 1)
    allowed = (row % slots == col % slots) & (col // slots < frames)
    return token.astype(F32), allowed


def normalised(mixed):
    values = mixed.astype(F32)
    centred = values - jnp.mean(values, axis=1, keepdims=True)
    inv_std = lax.rsqrt(jnp.mean(centred * centred, axis=1, keepdims=True) + EPSILON)
    return centred * inv_std, inv_std


def temporal_forward(
    info, mod, stream, out_s, w_spatial, w_qkv, mixed_ref, mod_ref, qkv_ref, out_ref, acc, slots
):
    rows, inner = acc.shape
    width = w_spatial.shape[0]
    token, allowed = slot_masks(info, rows, slots)
    branch = dot_nt(out_s[...].reshape(rows, inner), w_spatial[...])
    mixed = (stream[...].reshape(rows, width).astype(F32) + token * branch).astype(BF16)
    mixed_ref[...] = mixed.reshape(mixed_ref.shape)
    normed, _ = normalised(mixed)
    modulated = (normed * (1.0 + mod[0, 1:2]) + mod[0, 0:1]).astype(BF16)
    mod_ref[...] = modulated.reshape(mod_ref.shape)
    qkv = dot_nt(modulated, w_qkv[...]).astype(BF16)
    qkv_ref[...] = qkv.reshape(qkv_ref.shape)
    attend_heads(
        qkv[:, :inner], qkv[:, inner : 2 * inner], qkv[:, 2 * inner :], allowed, acc
    )
    out_ref[...] = acc[...].astype(BF16).reshape(out_ref.shape)


def temporal_backward(
    info, mod, grad, qkv_ref, out_t, modulated, w_temporal, dqkv_ref, g_temporal, g_qkv,
    q_acc, k_acc, v_acc, sum_t, sum_q, slots, y_count
):
    rows, inner = q_acc.shape
    width = w_temporal.shape[0]
    token, allowed = slot_masks(info, rows, slots)
    branch_grad = (token * mod[0, 2:3] * grad[...].reshape(rows, width).astype(F32)).astype(BF16)
    out_grad = dot_nn(branch_grad, w_temporal[...]).astype(BF16)
    qkv = qkv_ref[...].reshape(rows, 3 * inner)
    out = out_t[...].reshape(rows, inner)
    attend_heads_back(
        qkv[:, :inner], qkv[:, inner : 2 * inner], qkv[:, 2 * inner :], out, out_grad, allowed,
        q_acc, k_acc, v_acc,
    )
    dqkv = jnp.concatenate([q_acc[...], k_acc[...], v_acc[...]], axis=1).astype(BF16)
    dqkv_ref[...] = dqkv.reshape(dqkv_ref.shape)
    part_t = dot_tn(out, branch_grad)
    left = modulated[...].reshape(rows, width)
    step = width // (2 * y_count)
    cores = [
        jnp.concatenate(
            [left[:, (2 * y + c) * step : (2 * y + c + 1) * step] for y in range(y_count)], axis=1
        )
        for c in range(2)
    ]
    parts_q = [dot_tn(dqkv, core) for core in cores]

    @pl.when(pl.program_id(0) == 0)
    def _():
        sum_t[...] = part_t
        for c in range(2):
            sum_q[c] = parts_q[c]

    @pl.when(pl.program_id(0) > 0)
    def _():
        sum_t[...] += part_t
        for c in range(2):
            sum_q[c] += parts_q[c]

    @pl.when(pl.program_id(0) == pl.num_programs(0) - 1)
    def _():
        store_by_core(sum_t, g_temporal)
        g_qkv[...] = sum_q[...].astype(BF16)


def store_by_core(total, out):
    _, y_count, step, _ = out.shape
    for y in range(y_count):
        for c in range(2):
            start = (2 * y + c) * step
            out[c, y] = total[start : start + step].astype(BF16)


def norm_backward(
    info, mod, grad, mixed, out_s, dqkv, w_qkv, ln_ref, g_spatial, sum_s, slots
):
    rows = dqkv.shape[1]
    width = w_qkv.shape[1]
    token, _ = slot_masks(info, rows, slots)
    norm_grad = dot_nn(dqkv[...].reshape(rows, -1), w_qkv[...]) * (1.0 + mod[0, 1:2])
    normed, inv_std = normalised(mixed[...].reshape(rows, width))
    first = jnp.mean(norm_grad, axis=1, keepdims=True)
    second = jnp.mean(norm_grad * normed, axis=1, keepdims=True)
    ln_grad = (inv_std * (norm_grad - first - normed * second)).astype(BF16)
    ln_ref[...] = ln_grad.reshape(ln_ref.shape)
    grad_f = grad[...].reshape(rows, width).astype(F32)
    hidden_grad = (grad_f + ln_grad.astype(F32)).astype(BF16)
    branch_grad = (token * hidden_grad.astype(F32)).astype(BF16)
    part = dot_tn(out_s[...].reshape(rows, -1), branch_grad)

    @pl.when(pl.program_id(0) == 0)
    def _():
        sum_s[...] = part

    @pl.when(pl.program_id(0) > 0)
    def _():
        sum_s[...] += part

    @pl.when(pl.program_id(0) == pl.num_programs(0) - 1)
    def _():
        store_by_core(sum_s, g_spatial)


def frame_keys(info_ref, rows):
    return lax.broadcasted_iota(jnp.int32, (1, rows), 1) < info_ref[1]


def frame_tokens(info_ref, rows):
    row = lax.broadcasted_iota(jnp.int32, (rows, 1), 0)
    alive = info_ref[3] + pl.program_id(0) < info_ref[0]
    return ((row < info_ref[1]) & alive).astype(F32)


def spatial_forward(info, qkv_ref, out_ref, acc):
    rows, inner = acc.shape
    qkv = qkv_ref[0]
    attend_heads(
        qkv[:, :inner], qkv[:, inner : 2 * inner], qkv[:, 2 * inner :], frame_keys(info, rows), acc
    )
    out_ref[0] = acc[...].astype(BF16)


def block_forward(info, mod, stream, out_s, out_t, w_spatial, w_temporal, block_ref):
    rows = stream.shape[1]
    token = frame_tokens(info, rows)
    mixed = (stream[0].astype(F32) + token * dot_nt(out_s[0], w_spatial[...])).astype(BF16)
    branch = dot_nt(out_t[0], w_temporal[...])
    block_ref[0] = (mixed.astype(F32) + token * mod[0, 2:3] * branch).astype(BF16)


def spatial_backward(
    info, grad, ln_grad, qkv_ref, out_s, w_spatial, hidden_ref, dqkv_ref, q_acc, k_acc, v_acc
):
    rows, inner = q_acc.shape
    hidden_grad = (grad[0].astype(F32) + ln_grad[0].astype(F32)).astype(BF16)
    hidden_ref[0] = hidden_grad
    branch_grad = (frame_tokens(info, rows) * hidden_grad.astype(F32)).astype(BF16)
    out_grad = dot_nn(branch_grad, w_spatial[...]).astype(BF16)
    qkv = qkv_ref[0]
    attend_heads_back(
        qkv[:, :inner], qkv[:, inner : 2 * inner], qkv[:, 2 * inner :], out_s[0], out_grad,
        frame_keys(info, rows), q_acc, k_acc, v_acc,
    )
    dqkv_ref[0] = jnp.concatenate([q_acc[...], k_acc[...], v_acc[...]], axis=1).astype(BF16)


def whole(array):
    return pl.BlockSpec(array.shape, lambda step: (0,) * array.ndim)


def per_frame(array):
    return pl.BlockSpec((1,) + array.shape[1:], lambda step: (step, 0, 0))


def per_group(array):
    return pl.BlockSpec(
        (array.shape[0], 1) + array.shape[2:], lambda step: (0, step, 0, 0)
    )


SCALARS = pl.BlockSpec(memory_space=pltpu.SMEM)


def run(body, steps, operands, specs, results, result_specs, scratch, flops):
    leaves = operands + jax.tree.leaves(results)
    moved = sum(math.prod(a.shape) * a.dtype.itemsize for a in leaves)
    return pl.pallas_call(
        body,
        grid=(steps,),
        in_specs=specs,
        out_specs=result_specs,
        out_shape=results,
        scratch_shapes=scratch,
        compiler_params=pltpu.CompilerParams(vmem_limit_bytes=VMEM_BYTES),
        cost_estimate=pl.CostEstimate(flops=flops, bytes_accessed=moved, transcendentals=0),
    )(*operands)


def shape_of(*dims, dtype=BF16):
    return jax.ShapeDtypeStruct(dims, dtype)


def exchange(rows, axes):
    return lax.all_to_all(rows, axes, 0, 0, tiled=True)


def shift(rows, axis, hops):
    count = lax.axis_size(axis)
    return lax.ppermute(rows, axis, [(at, (at + hops) % count) for at in range(count)])


def shift_both(rows, axis, hops):
    count = lax.axis_size(axis)
    pairs = []
    for at in range(count):
        pairs.append((2 * at, 2 * ((at - hops) % count)))
        pairs.append((2 * at + 1, 2 * ((at + hops) % count) + 1))
    return lax.ppermute(rows, (axis, "c"), pairs)


def swap(rows):
    return shift(rows, "c", 1)


def copy_all(copies):
    for copy in copies:
        copy.start()
    for copy in copies:
        copy.wait()


def place_along_z(info, own, near, mid, far, last, near_p, mid_p, far_p, out, sems):
    place, count = info[1], out.shape[0]
    sign = 1 - 2 * info[3]
    moves = [(own, place), (last, lax.rem(place + count // 2, count))]
    for hops, mine, other in ((1, near, near_p), (2, mid, mid_p), (3, far, far_p)):
        moves.append((mine, lax.rem(place + sign * hops + count, count)))
        moves.append((other, lax.rem(place - sign * hops + count, count)))
    copy_all(
        [
            pltpu.make_async_copy(source, out.at[index], sems.at[number])
            for number, (source, index) in enumerate(moves)
        ]
    )


def place_along_x(info, own, near, near_p, part, part_p, out_s, out_q, sems):
    place, count = info[0], out_s.shape[0]
    sign = 1 - 2 * info[3]
    thin = out_s.shape[1]
    half = part.shape[0]
    opposite = lax.rem(place + count // 2, count)
    copies = []

    def move(source, target):
        copies.append(pltpu.make_async_copy(source, target, sems.at[len(copies)]))

    for block, index in (
        (own, place),
        (near, lax.rem(place + sign + count, count)),
        (near_p, lax.rem(place - sign + count, count)),
    ):
        move(block.at[pl.ds(0, thin)], out_s.at[index])
        move(block.at[pl.ds(thin, 2 * half - thin)], out_q.at[index])
    copy_all(copies)

    def halves(first, second):
        copies.clear()
        move(first.at[pl.ds(0, thin)], out_s.at[opposite])
        move(first.at[pl.ds(thin, half - thin)], out_q.at[opposite, pl.ds(0, half - thin)])
        move(second, out_q.at[opposite, pl.ds(half - thin, half)])
        copy_all(copies)

    @pl.when(info[3] == 0)
    def _():
        halves(part, part_p)

    @pl.when(info[3] != 0)
    def _():
        halves(part_p, part)


def place_blocks(body, info, blocks, results, copies):
    anywhere = pl.BlockSpec(memory_space=pl.ANY)
    return pl.pallas_call(
        body,
        in_specs=[SCALARS] + [anywhere] * len(blocks),
        out_specs=jax.tree.map(lambda _: anywhere, results),
        out_shape=results,
        scratch_shapes=[pltpu.SemaphoreType.DMA((copies,))],
    )(info, *blocks)


def weight_rows(out_spatial, qkv_temporal, out_temporal):
    half, narrow = out_spatial.shape
    packed = jnp.concatenate(
        [jnp.concatenate([out_spatial.T, out_temporal.T], axis=1), qkv_temporal.T], axis=0
    )
    near = jnp.transpose(lax.all_gather(packed, ("y", "c"), axis=0, tiled=False), (1, 0, 2))
    thin = near[:narrow, :, :half].reshape(narrow, -1)
    inner = thin.shape[1]
    wide = near[narrow:].reshape(near.shape[0] - narrow, -1)
    w_temporal = lax.all_gather(near[:narrow, :, half:].reshape(narrow, -1), ("x", "z"), axis=0)
    w_temporal = w_temporal.reshape(-1, inner)

    coords = jnp.stack([lax.axis_index(name) for name in ("x", "z", "y", "c")]).astype(jnp.int32)
    cut = narrow // 2
    rows = jnp.concatenate([jnp.concatenate([thin[:cut], thin[cut:]], axis=1), wide], axis=0)
    arrived = [shift_both(rows, "z", hops) for hops in (1, 2, 3)] + [shift(rows, "z", 4)]
    swapped = [swap(block) for block in arrived[:3]]
    z_count, x_count = lax.axis_size("z"), lax.axis_size("x")
    stack = place_blocks(
        place_along_z, coords, [rows] + arrived + swapped, shape_of(z_count, *rows.shape), z_count
    )
    thin = jnp.concatenate([stack[:, :cut, :inner], stack[:, :cut, inner:]], axis=1)
    thin = thin.reshape(-1, inner)
    cut = thin.shape[0] // 2
    wide = stack[:, narrow // 2 :].reshape(-1, stack.shape[2])
    rows = jnp.concatenate([jnp.concatenate([thin[:cut], thin[cut:]], axis=1), wide], axis=0)
    first = shift_both(rows, "x", 1)
    size = rows.shape[0] // 2
    onward = lax.dynamic_slice_in_dim(first, lax.axis_index("c") * size, size, 0)
    second = shift_both(onward, "x", 1)
    w_thin, w_wide = place_blocks(
        place_along_x,
        coords,
        [rows, first, swap(first), second, swap(second)],
        (
            shape_of(x_count, cut, rows.shape[1]),
            shape_of(x_count, wide.shape[0], rows.shape[1]),
        ),
        6,
    )
    w_thin = jnp.concatenate([w_thin[:, :, :inner], w_thin[:, :, inner:]], axis=1)
    return (w_thin.reshape(-1, inner), w_wide.reshape(-1, rows.shape[1]), w_temporal)


def summed_halves(terms):
    pair = exchange(terms, "c").astype(F32)
    return pair[0] + pair[1]


def scatter_sum(blocks, axis):
    count, place = lax.axis_size(axis), lax.axis_index(axis)
    total = lax.dynamic_index_in_dim(blocks, place, 0, keepdims=False).astype(F32)
    for hops in range(1, count):
        block = lax.dynamic_index_in_dim(blocks, (place + hops) % count, 0, keepdims=False)
        total = total + shift(block, axis, hops).astype(F32)
    return total


def reduce_grads(g_spatial, g_qkv, g_temporal):
    x_count, z_count = lax.axis_size("x"), lax.axis_size("z")
    y_count = lax.axis_size("y")
    wide = summed_halves(g_qkv).astype(BF16)
    wide = scatter_sum(wide.reshape(x_count, -1, wide.shape[1]), "x").astype(BF16)
    wide = jnp.transpose(wide.reshape(wide.shape[0], y_count, -1), (1, 0, 2))
    wide = scatter_sum(wide, "y").astype(BF16)

    pair = jnp.concatenate([summed_halves(g_spatial), summed_halves(g_temporal)], axis=1)
    pair = jnp.sum(exchange(pair.astype(BF16), "y").astype(F32), axis=0).astype(BF16)
    pair = scatter_sum(pair.T.reshape(x_count, -1, pair.shape[0]), "x").astype(BF16)

    chunks = jnp.concatenate(
        [pair.reshape(z_count, -1, pair.shape[1]), wide.reshape(z_count, -1, wide.shape[1])],
        axis=1,
    )
    total = jnp.sum(exchange(chunks, "z").astype(F32), axis=0)
    narrow = pair.shape[0] // z_count
    half = pair.shape[1] // 2
    return (total[:narrow, :half].T, total[narrow:].T, total[:narrow, half:].T)


def on_device(
    hidden,
    spatial_qkv,
    out_spatial,
    qkv_temporal,
    out_temporal,
    modulation,
    cotangent,
    frame_count,
    patch_height,
    patch_width,
):
    seq_count = lax.axis_size(("y", "c"))
    seq_place = lax.axis_index(("y", "c"))
    y_count = lax.axis_size("y")
    stream = hidden[0]
    grad_out = cotangent[0]
    packed_qkv = spatial_qkv[0]
    frame_dev, slot_total, width = stream.shape
    slot_dev = slot_total // seq_count
    inner = out_spatial.shape[0] * seq_count
    slots = 8
    groups = slot_dev // slots
    rows = frame_dev * seq_count * slots
    info = jnp.stack(
        [
            frame_count[0],
            patch_height[0] * patch_width[0],
            seq_place * slot_dev,
            seq_place * frame_dev,
        ]
    ).astype(jnp.int32)

    def to_slots(tokens):
        split = tokens.reshape(frame_dev, seq_count, groups, slots, -1)
        split = jnp.transpose(split, (1, 2, 0, 3, 4))
        return exchange(split.reshape(seq_count, groups, frame_dev * slots, -1), ("y", "c"))

    def to_frames(tokens):
        moved = exchange(tokens, ("y", "c")).reshape(seq_count, groups, frame_dev, slots, -1)
        return jnp.transpose(moved, (2, 0, 1, 3, 4)).reshape(frame_dev, slot_total, -1)

    stream_s = to_slots(stream)
    frame_acc = pltpu.VMEM((slot_total, inner), F32)
    out_s = shape_of(frame_dev, slot_total, inner)
    out_s = run(
        spatial_forward,
        frame_dev,
        [info, packed_qkv],
        [SCALARS, per_frame(packed_qkv)],
        out_s,
        per_frame(out_s),
        [frame_acc],
        4 * frame_dev * slot_total * slot_total * inner,
    )
    out_s_s = to_slots(out_s)
    grad_s = to_slots(grad_out)
    w_spatial, w_qkv, w_temporal = weight_rows(out_spatial, qkv_temporal, out_temporal)

    group_acc = pltpu.VMEM((rows, inner), F32)
    result = (
        shape_of(groups, rows, width),
        shape_of(groups, rows, width),
        shape_of(groups, rows, 3 * inner),
        shape_of(seq_count, groups, rows // seq_count, inner),
    )
    tokens = groups * rows
    mixed_s, modulated, qkv_t, out_t = run(
        functools.partial(temporal_forward, slots=slots),
        groups,
        [info, modulation, stream_s, out_s_s, w_spatial, w_qkv],
        [SCALARS, whole(modulation), per_group(stream_s), per_group(out_s_s), whole(w_spatial), whole(w_qkv)],
        result,
        [per_frame(result[0]), per_frame(result[1]), per_frame(result[2]), per_group(result[3])],
        [group_acc],
        8 * tokens * width * inner + 4 * tokens * rows * inner,
    )
    out_t_f = to_frames(out_t)

    result = (
        shape_of(groups, rows, 3 * inner),
        shape_of(2, y_count, inner // seq_count, width),
        shape_of(2, 3 * inner, width // 2),
    )
    dqkv_t, g_temporal, g_qkv = run(
        functools.partial(temporal_backward, slots=slots, y_count=y_count),
        groups,
        [info, modulation, grad_s, qkv_t, out_t, modulated, w_temporal],
        [SCALARS, whole(modulation), per_group(grad_s), per_frame(qkv_t), per_group(out_t), per_frame(modulated), whole(w_temporal)],
        result,
        [per_frame(result[0]), whole(result[1]), whole(result[2])],
        [group_acc, group_acc, group_acc, pltpu.VMEM((inner, width), F32), pltpu.VMEM((2, 3 * inner, width // 2), F32)],
        10 * tokens * width * inner + 10 * tokens * rows * inner,
    )
    result = (
        shape_of(seq_count, groups, rows // seq_count, width),
        shape_of(2, y_count, inner // seq_count, width),
    )
    ln_grad, g_spatial = run(
        functools.partial(norm_backward, slots=slots),
        groups,
        [info, modulation, grad_s, mixed_s, out_s_s, dqkv_t, w_qkv],
        [SCALARS, whole(modulation), per_group(grad_s), per_frame(mixed_s), per_group(out_s_s), per_frame(dqkv_t), whole(w_qkv)],
        result,
        [per_group(result[0]), whole(result[1])],
        [pltpu.VMEM((inner, width), F32)],
        8 * tokens * width * inner,
    )
    ln_frames = to_frames(ln_grad)
    summed = reduce_grads(g_spatial, g_qkv, g_temporal)

    block_out = shape_of(frame_dev, slot_total, width)
    block_out = run(
        block_forward,
        frame_dev,
        [info, modulation, stream, out_s, out_t_f, w_spatial, w_temporal],
        [SCALARS, whole(modulation), per_frame(stream), per_frame(out_s), per_frame(out_t_f), whole(w_spatial), whole(w_temporal)],
        block_out,
        per_frame(block_out),
        [],
        4 * tokens * width * inner,
    )
    result = (shape_of(frame_dev, slot_total, width), shape_of(frame_dev, slot_total, 3 * inner))
    hidden_grad, qkv_s_grad = run(
        spatial_backward,
        frame_dev,
        [info, grad_out, ln_frames, packed_qkv, out_s, w_spatial],
        [SCALARS, per_frame(grad_out), per_frame(ln_frames), per_frame(packed_qkv), per_frame(out_s), whole(w_spatial)],
        result,
        [per_frame(result[0]), per_frame(result[1])],
        [frame_acc, frame_acc, frame_acc],
        2 * tokens * width * inner + 10 * tokens * slot_total * inner,
    )
    return (block_out[None], hidden_grad[None], qkv_s_grad[None], summed[0], summed[1], summed[2])


def solution(mesh):
    torus = Mesh(mesh.devices.reshape(4, 8, 4, 2), ("x", "z", "y", "c"))
    dp, seq = ("x", "z"), ("y", "c")
    tokens = P(dp, seq, None, None)
    weight = P(seq, dp)
    placed = (
        tokens,
        tokens,
        weight,
        weight,
        weight,
        P(dp, None, None),
        tokens,
        P(dp),
        P(dp),
        P(dp),
    )
    return jax.shard_map(
        on_device,
        mesh=torus,
        in_specs=placed,
        out_specs=(tokens, tokens, tokens, weight, weight, weight),
        check_vma=False,
    )
```

```python
import functools
import math

import jax
import jax.numpy as jnp
from jax import lax
from jax.experimental import pallas as pl
from jax.experimental.pallas import tpu as pltpu
from jax.sharding import Mesh
from jax.sharding import PartitionSpec as P

HEAD_DIM = 72
EPSILON = 1e-06
NEGATIVE = -1e30
LANES = 128
VMEM_BYTES = 56 * 1024 * 1024
F32 = jnp.float32
BF16 = jnp.bfloat16


def dot_nn(left, right):
    return lax.dot_general(left, right, (((1,), (0,)), ((), ())), preferred_element_type=F32)


def dot_nt(left, right):
    return lax.dot_general(left, right, (((1,), (1,)), ((), ())), preferred_element_type=F32)


def dot_tn(left, right):
    return lax.dot_general(left, right, (((0,), (0,)), ((), ())), preferred_element_type=F32)


def head_windows(inner):
    windows = []
    for head in range(inner // HEAD_DIM):
        low = head * HEAD_DIM
        start = low // LANES * LANES
        stop = min(-(-(low + HEAD_DIM) // LANES) * LANES, inner)
        windows.append((start, stop, low - start))
    return windows


def own_lanes(window):
    start, stop, offset = window
    lane = lax.broadcasted_iota(jnp.int32, (1, stop - start), 1)
    return (lane >= offset) & (lane < offset + HEAD_DIM)


def only(lanes, rows):
    return jnp.where(lanes, rows, jnp.zeros((), rows.dtype))


def softmax_rows(query, key, allowed):
    logits = dot_nt(query, key) * (1.0 / math.sqrt(HEAD_DIM))
    logits = jnp.where(allowed, logits, NEGATIVE)
    powers = jnp.exp(logits - jnp.max(logits, axis=1, keepdims=True))
    return powers * (1.0 / jnp.sum(powers, axis=1, keepdims=True))


def attend_heads(query, key, value, allowed, out_acc):
    out_acc[...] = jnp.zeros(out_acc.shape, F32)
    for window in head_windows(query.shape[1]):
        start, stop, _ = window
        lanes = own_lanes(window)
        probs = softmax_rows(query[:, start:stop], only(lanes, key[:, start:stop]), allowed)
        out_acc[:, start:stop] += dot_nn(probs.astype(BF16), only(lanes, value[:, start:stop]))


def attend_heads_back(query, key, value, out, out_grad, allowed, q_acc, k_acc, v_acc):
    factor = 1.0 / math.sqrt(HEAD_DIM)
    for acc in (q_acc, k_acc, v_acc):
        acc[...] = jnp.zeros(acc.shape, F32)
    for window in head_windows(query.shape[1]):
        start, stop, _ = window
        lanes = own_lanes(window)
        key_h = only(lanes, key[:, start:stop])
        grad_h = only(lanes, out_grad[:, start:stop])
        probs = softmax_rows(query[:, start:stop], key_h, allowed)
        prob_grad = dot_nt(grad_h, value[:, start:stop])
        row_delta = jnp.sum(
            grad_h.astype(F32) * out[:, start:stop].astype(F32), axis=1, keepdims=True
        )
        logit_grad = (probs * (prob_grad - row_delta)).astype(BF16)
        q_acc[:, start:stop] += dot_nn(logit_grad, key_h) * factor
        k_acc[:, start:stop] += dot_tn(logit_grad, only(lanes, query[:, start:stop])) * factor
        v_acc[:, start:stop] += dot_tn(probs.astype(BF16), grad_h)


def slot_masks(info_ref, rows, slots):
    frames, limit, first = info_ref[0], info_ref[1], info_ref[2]
    group = pl.program_id(0)
    row = lax.broadcasted_iota(jnp.int32, (rows, 1), 0)
    slot = first + group * slots + row % slots
    token = (row // slots < frames) & (slot < limit)
    col = lax.broadcasted_iota(jnp.int32, (1, rows), 1)
    allowed = (row % slots == col % slots) & (col // slots < frames)
    return token.astype(F32), allowed


def normalised(mixed):
    values = mixed.astype(F32)
    centred = values - jnp.mean(values, axis=1, keepdims=True)
    inv_std = lax.rsqrt(jnp.mean(centred * centred, axis=1, keepdims=True) + EPSILON)
    return centred * inv_std, inv_std


def temporal_forward(
    info, mod, stream, out_s, w_spatial, w_qkv, mixed_ref, mod_ref, qkv_ref, out_ref, acc, slots
):
    rows, inner = acc.shape
    width = w_spatial.shape[0]
    token, allowed = slot_masks(info, rows, slots)
    branch = dot_nt(out_s[...].reshape(rows, inner), w_spatial[...])
    mixed = (stream[...].reshape(rows, width).astype(F32) + token * branch).astype(BF16)
    mixed_ref[...] = mixed.reshape(mixed_ref.shape)
    normed, _ = normalised(mixed)
    modulated = (normed * (1.0 + mod[0, 1:2]) + mod[0, 0:1]).astype(BF16)
    mod_ref[...] = modulated.reshape(mod_ref.shape)
    qkv = dot_nt(modulated, w_qkv[...]).astype(BF16)
    qkv_ref[...] = qkv.reshape(qkv_ref.shape)
    attend_heads(
        qkv[:, :inner], qkv[:, inner : 2 * inner], qkv[:, 2 * inner :], allowed, acc
    )
    out_ref[...] = acc[...].astype(BF16).reshape(out_ref.shape)


def temporal_backward(
    info, mod, grad, mixed, out_s, qkv_ref, out_t, modulated, w_temporal, w_qkv, ln_ref, terms,
    q_acc, k_acc, v_acc, sum_s, sum_t, sum_q, slots, y_count, x_count,
):
    rows, inner = q_acc.shape
    width = w_temporal.shape[0]
    token, allowed = slot_masks(info, rows, slots)

    @pl.when(pl.program_id(0) == 0)
    def _():
        for total in (sum_s, sum_t, sum_q):
            total[...] = jnp.zeros(total.shape, F32)

    grad_f = grad[...].reshape(rows, width).astype(F32)
    branch_grad = (token * mod[0, 2:3] * grad_f).astype(BF16)
    out_grad = dot_nn(branch_grad, w_temporal[...]).astype(BF16)
    qkv = qkv_ref[...].reshape(rows, 3 * inner)
    out = out_t[...].reshape(rows, inner)
    attend_heads_back(
        qkv[:, :inner], qkv[:, inner : 2 * inner], qkv[:, 2 * inner :], out, out_grad, allowed,
        q_acc, k_acc, v_acc,
    )
    dqkv = jnp.concatenate([q_acc[...], k_acc[...], v_acc[...]], axis=1).astype(BF16)

    norm_grad = dot_nn(dqkv, w_qkv[...]) * (1.0 + mod[0, 1:2])
    normed, inv_std = normalised(mixed[...].reshape(rows, width))
    first = jnp.mean(norm_grad, axis=1, keepdims=True)
    second = jnp.mean(norm_grad * normed, axis=1, keepdims=True)
    ln_grad = (inv_std * (norm_grad - first - normed * second)).astype(BF16)
    ln_ref[...] = ln_grad.reshape(ln_ref.shape)
    hidden_grad = (grad_f + ln_grad.astype(F32)).astype(BF16)
    spatial_grad = (token * hidden_grad.astype(F32)).astype(BF16)

    sum_t[...] += dot_tn(out, branch_grad)
    sum_s[...] += dot_tn(out_s[...].reshape(rows, inner), spatial_grad)
    left = modulated[...].reshape(rows, width)
    step = width // (2 * y_count)
    for c in range(2):
        pieces = [left[:, (2 * y + c) * step : (2 * y + c + 1) * step] for y in range(y_count)]
        sum_q[c] += dot_tn(dqkv, jnp.concatenate(pieces, axis=1))

    @pl.when(pl.program_id(0) == pl.num_programs(0) - 1)
    def _():
        store_terms(sum_s, sum_t, sum_q, terms, y_count, x_count)


def term_rows(inner, width, y_count, x_count):
    tiles = -(-(width // 2) // LANES)
    return tiles * (3 * inner // x_count), width // LANES * (inner // y_count)


def store_terms(sum_s, sum_t, sum_q, terms, y_count, x_count):
    inner, width = sum_s.shape
    span, step = 3 * inner // x_count, inner // (2 * y_count)
    wide, pair = term_rows(inner, width, y_count, x_count)
    half = width // 2
    for c in range(2):
        for x in range(x_count):
            for tile in range(wide // span):
                low, high = tile * LANES, min((tile + 1) * LANES, half)
                block = sum_q[c, x * span : (x + 1) * span, low:high]
                if high - low < LANES:
                    rest = jnp.zeros((span, LANES - (high - low)), F32)
                    block = jnp.concatenate([block, rest], axis=1)
                start = x * wide + tile * span
                terms[c, start : start + span] = block.astype(BF16)
        for y in range(y_count):
            place = (2 * y + c) * step
            for tile in range(width // LANES):
                lanes = slice(tile * LANES, (tile + 1) * LANES)
                block = jnp.concatenate(
                    [sum_s[place : place + step, lanes], sum_t[place : place + step, lanes]],
                    axis=0,
                )
                start = x_count * wide + y * pair + tile * 2 * step
                terms[c, start : start + 2 * step] = block.astype(BF16)


def frame_keys(info_ref, rows):
    return lax.broadcasted_iota(jnp.int32, (1, rows), 1) < info_ref[1]


def frame_tokens(info_ref, rows):
    row = lax.broadcasted_iota(jnp.int32, (rows, 1), 0)
    alive = info_ref[3] + pl.program_id(0) < info_ref[0]
    return ((row < info_ref[1]) & alive).astype(F32)


def spatial_forward(info, qkv_ref, out_ref, acc):
    rows, inner = acc.shape
    qkv = qkv_ref[0]
    attend_heads(
        qkv[:, :inner], qkv[:, inner : 2 * inner], qkv[:, 2 * inner :], frame_keys(info, rows), acc
    )
    out_ref[0] = acc[...].astype(BF16)


def block_forward(info, mod, stream, out_s, out_t, w_spatial, w_temporal, block_ref):
    rows = stream.shape[1]
    token = frame_tokens(info, rows)
    mixed = (stream[0].astype(F32) + token * dot_nt(out_s[0], w_spatial[...])).astype(BF16)
    branch = dot_nt(out_t[0], w_temporal[...])
    block_ref[0] = (mixed.astype(F32) + token * mod[0, 2:3] * branch).astype(BF16)


def spatial_backward(
    info, grad, ln_grad, qkv_ref, out_s, w_spatial, hidden_ref, dqkv_ref, q_acc, k_acc, v_acc
):
    rows, inner = q_acc.shape
    hidden_grad = (grad[0].astype(F32) + ln_grad[0].astype(F32)).astype(BF16)
    hidden_ref[0] = hidden_grad
    branch_grad = (frame_tokens(info, rows) * hidden_grad.astype(F32)).astype(BF16)
    out_grad = dot_nn(branch_grad, w_spatial[...]).astype(BF16)
    qkv = qkv_ref[0]
    attend_heads_back(
        qkv[:, :inner], qkv[:, inner : 2 * inner], qkv[:, 2 * inner :], out_s[0], out_grad,
        frame_keys(info, rows), q_acc, k_acc, v_acc,
    )
    dqkv_ref[0] = jnp.concatenate([q_acc[...], k_acc[...], v_acc[...]], axis=1).astype(BF16)


def whole(array):
    return pl.BlockSpec(
        array.shape, lambda step: (0,) * array.ndim, pipeline_mode=pl.Buffered(1)
    )


def per_frame(array):
    return pl.BlockSpec((1,) + array.shape[1:], lambda step: (step, 0, 0))


def per_group(array):
    return pl.BlockSpec(
        (array.shape[0], 1) + array.shape[2:], lambda step: (0, step, 0, 0)
    )


SCALARS = pl.BlockSpec(memory_space=pltpu.SMEM)


def run(body, steps, operands, specs, results, result_specs, scratch, flops):
    leaves = operands + jax.tree.leaves(results)
    moved = sum(math.prod(a.shape) * a.dtype.itemsize for a in leaves)
    return pl.pallas_call(
        body,
        grid=(steps,),
        in_specs=specs,
        out_specs=result_specs,
        out_shape=results,
        scratch_shapes=scratch,
        compiler_params=pltpu.CompilerParams(vmem_limit_bytes=VMEM_BYTES),
        cost_estimate=pl.CostEstimate(flops=flops, bytes_accessed=moved, transcendentals=0),
    )(*operands)


def shape_of(*dims, dtype=BF16):
    return jax.ShapeDtypeStruct(dims, dtype)


def exchange(rows, axes):
    return lax.all_to_all(rows, axes, 0, 0, tiled=True)


def shift(rows, axis, hops):
    count = lax.axis_size(axis)
    return lax.ppermute(rows, axis, [(at, (at + hops) % count) for at in range(count)])


def shift_both(rows, axis, hops):
    count = lax.axis_size(axis)
    pairs = []
    for at in range(count):
        pairs.append((2 * at, 2 * ((at - hops) % count)))
        pairs.append((2 * at + 1, 2 * ((at + hops) % count) + 1))
    return lax.ppermute(rows, (axis, "c"), pairs)


def swap(rows):
    return shift(rows, "c", 1)


def place_along_z(info, own, near, mid, far, last, near_p, mid_p, far_p, out):
    place, count = info[1], out.shape[0]
    sign = 1 - 2 * info[3]
    out[place] = own[...]
    out[lax.rem(place + count // 2, count)] = last[...]
    for hops, mine, other in ((1, near, near_p), (2, mid, mid_p), (3, far, far_p)):
        out[lax.rem(place + sign * hops + count, count)] = mine[...]
        out[lax.rem(place - sign * hops + count, count)] = other[...]


def place_along_x(info, own, near, near_p, part, part_p, out_s, out_q):
    place, count = info[0], out_s.shape[0]
    sign = 1 - 2 * info[3]
    thin = out_s.shape[1]
    half = part.shape[0]
    opposite = lax.rem(place + count // 2, count)
    for block, index in (
        (own, place),
        (near, lax.rem(place + sign + count, count)),
        (near_p, lax.rem(place - sign + count, count)),
    ):
        out_s[index] = block[:thin]
        out_q[index] = block[thin:]

    def halves(first, second):
        out_s[opposite] = first[:thin]
        out_q[opposite, : half - thin] = first[thin:]
        out_q[opposite, half - thin :] = second[...]

    @pl.when(info[3] == 0)
    def _():
        halves(part, part_p)

    @pl.when(info[3] != 0)
    def _():
        halves(part_p, part)


def in_vmem(body, info, blocks, results):
    vmem = pl.BlockSpec(memory_space=pltpu.VMEM)
    return pl.pallas_call(
        body,
        in_specs=[SCALARS] + [vmem] * len(blocks),
        out_specs=jax.tree.map(lambda _: vmem, results),
        out_shape=results,
        compiler_params=pltpu.CompilerParams(vmem_limit_bytes=VMEM_BYTES),
    )(info, *blocks)


def weight_rows(coords, out_spatial, qkv_temporal, out_temporal):
    half, narrow = out_spatial.shape
    packed = jnp.concatenate(
        [jnp.concatenate([out_spatial.T, out_temporal.T], axis=1), qkv_temporal.T], axis=0
    )
    near = jnp.transpose(lax.all_gather(packed, ("y", "c"), axis=0, tiled=False), (1, 0, 2))
    thin = near[:narrow, :, :half].reshape(narrow, -1)
    inner = thin.shape[1]
    wide = near[narrow:].reshape(near.shape[0] - narrow, -1)
    w_temporal = lax.all_gather(near[:narrow, :, half:].reshape(narrow, -1), ("x", "z"), axis=0)
    w_temporal = w_temporal.reshape(-1, inner)

    cut = narrow // 2
    rows = jnp.concatenate([jnp.concatenate([thin[:cut], thin[cut:]], axis=1), wide], axis=0)
    arrived = [shift_both(rows, "z", hops) for hops in (1, 2, 3)] + [shift(rows, "z", 4)]
    swapped = [swap(block) for block in arrived[:3]]
    z_count, x_count = lax.axis_size("z"), lax.axis_size("x")
    stack = in_vmem(
        place_along_z, coords, [rows] + arrived + swapped, shape_of(z_count, *rows.shape)
    )
    thin = jnp.concatenate([stack[:, :cut, :inner], stack[:, :cut, inner:]], axis=1)
    thin = thin.reshape(-1, inner)
    cut = thin.shape[0] // 2
    wide = stack[:, narrow // 2 :].reshape(-1, stack.shape[2])
    rows = jnp.concatenate([jnp.concatenate([thin[:cut], thin[cut:]], axis=1), wide], axis=0)
    first = shift_both(rows, "x", 1)
    size = rows.shape[0] // 2
    onward = lax.dynamic_slice_in_dim(first, lax.axis_index("c") * size, size, 0)
    second = shift_both(onward, "x", 1)
    w_thin, w_wide = in_vmem(
        place_along_x,
        coords,
        [rows, first, swap(first), second, swap(second)],
        (
            shape_of(x_count, cut, rows.shape[1]),
            shape_of(x_count, wide.shape[0], rows.shape[1]),
        ),
    )
    w_thin = jnp.concatenate([w_thin[:, :, :inner], w_thin[:, :, inner:]], axis=1)
    return (w_thin.reshape(-1, inner), w_wide.reshape(-1, rows.shape[1]), w_temporal)


def scatter(blocks, axis):
    count, place = lax.axis_size(axis), lax.axis_index(axis)
    arrived = []
    for hops in range(1, count):
        block = lax.dynamic_index_in_dim(blocks, (place + hops) % count, 0, keepdims=False)
        arrived.append(shift(block, axis, hops))
    return arrived


def scatter_sum(blocks, axis):
    place = lax.axis_index(axis)
    total = lax.dynamic_index_in_dim(blocks, place, 0, keepdims=False).astype(F32)
    for block in scatter(blocks, axis):
        total = total + block.astype(F32)
    return total


def regroup_wide(info, blocks, first, second, third, out):
    y_count, span, lanes = out.shape
    total = blocks[info[0]].astype(F32)
    for block in (first, second, third):
        total = total + block[...].astype(F32)
    tiles = [total[at : at + span] for at in range(0, total.shape[0], span)]
    flat = jnp.concatenate(tiles, axis=1)
    step = (flat.shape[1] - LANES // 2) // y_count
    for y in range(y_count):
        block = flat[:, y * step : (y + 1) * step]
        rest = jnp.zeros((span, lanes - step), F32)
        out[y] = jnp.concatenate([block, rest], axis=1).astype(BF16)


def regroup_pair(info, blocks, out):
    x_count, span, lanes = out.shape
    total = blocks[0].astype(F32)
    for y in range(1, blocks.shape[0]):
        total = total + blocks[y].astype(F32)
    width = x_count * span
    step = total.shape[0] // (width // LANES)
    tiles = [total[at : at + step].T for at in range(0, total.shape[0], step)]
    flat = jnp.concatenate(tiles, axis=0)
    flat = jnp.concatenate([flat, jnp.zeros((width, lanes - step), F32)], axis=1)
    for x in range(x_count):
        out[x] = flat[x * span : (x + 1) * span].astype(BF16)


def reduce_grads(coords, terms, inner, width):
    x_count, z_count = lax.axis_size("x"), lax.axis_size("z")
    y_count = lax.axis_size("y")
    wide_rows, pair_rows = term_rows(inner, width, y_count, x_count)
    halves = exchange(terms, "c")
    total = (halves[0].astype(F32) + halves[1].astype(F32)).astype(BF16)
    wide = total[: x_count * wide_rows].reshape(x_count, wide_rows, LANES)
    pair = total[x_count * wide_rows :].reshape(y_count, pair_rows, LANES)

    step = width // (2 * y_count)
    wide = in_vmem(
        regroup_wide,
        coords,
        [wide] + scatter(wide, "x"),
        shape_of(y_count, 3 * inner // x_count, 2 * LANES),
    )
    pair = in_vmem(
        regroup_pair, coords, [exchange(pair, "y")], shape_of(x_count, width // x_count, 2 * LANES)
    )
    wide = scatter_sum(wide, "y").astype(BF16).reshape(z_count, -1, 2 * LANES)
    pair = scatter_sum(pair, "x").astype(BF16).reshape(z_count, -1, 2 * LANES)
    total = jnp.sum(exchange(jnp.concatenate([pair, wide], axis=1), "z").astype(F32), axis=0)
    narrow = pair.shape[1]
    half = step // 2
    return (total[:narrow, :half].T, total[narrow:, :step].T, total[:narrow, half:step].T)


def on_device(
    hidden,
    spatial_qkv,
    out_spatial,
    qkv_temporal,
    out_temporal,
    modulation,
    cotangent,
    frame_count,
    patch_height,
    patch_width,
):
    seq_count = lax.axis_size(("y", "c"))
    seq_place = lax.axis_index(("y", "c"))
    y_count = lax.axis_size("y")
    stream = hidden[0]
    grad_out = cotangent[0]
    packed_qkv = spatial_qkv[0]
    frame_dev, slot_total, width = stream.shape
    slot_dev = slot_total // seq_count
    inner = out_spatial.shape[0] * seq_count
    slots = 8
    groups = slot_dev // slots
    rows = frame_dev * seq_count * slots
    coords = jnp.stack([lax.axis_index(name) for name in ("x", "z", "y", "c")]).astype(jnp.int32)
    info = jnp.stack(
        [
            frame_count[0],
            patch_height[0] * patch_width[0],
            seq_place * slot_dev,
            seq_place * frame_dev,
        ]
    ).astype(jnp.int32)

    def to_slots(tokens):
        split = tokens.reshape(frame_dev, seq_count, groups, slots, -1)
        split = jnp.transpose(split, (1, 2, 0, 3, 4))
        return exchange(split.reshape(seq_count, groups, frame_dev * slots, -1), ("y", "c"))

    def to_frames(tokens):
        moved = exchange(tokens, ("y", "c")).reshape(seq_count, groups, frame_dev, slots, -1)
        return jnp.transpose(moved, (2, 0, 1, 3, 4)).reshape(frame_dev, slot_total, -1)

    stream_s = to_slots(stream)
    frame_acc = pltpu.VMEM((slot_total, inner), F32)
    out_s = shape_of(frame_dev, slot_total, inner)
    out_s = run(
        spatial_forward,
        frame_dev,
        [info, packed_qkv],
        [SCALARS, per_frame(packed_qkv)],
        out_s,
        per_frame(out_s),
        [frame_acc],
        4 * frame_dev * slot_total * slot_total * inner,
    )
    out_s_s = to_slots(out_s)
    grad_s = to_slots(grad_out)
    w_spatial, w_qkv, w_temporal = weight_rows(coords, out_spatial, qkv_temporal, out_temporal)

    group_acc = pltpu.VMEM((rows, inner), F32)
    result = (
        shape_of(groups, rows, width),
        shape_of(groups, rows, width),
        shape_of(groups, rows, 3 * inner),
        shape_of(seq_count, groups, rows // seq_count, inner),
    )
    tokens = groups * rows
    mixed_s, modulated, qkv_t, out_t = run(
        functools.partial(temporal_forward, slots=slots),
        groups,
        [info, modulation, stream_s, out_s_s, w_spatial, w_qkv],
        [SCALARS, whole(modulation), per_group(stream_s), per_group(out_s_s), whole(w_spatial), whole(w_qkv)],
        result,
        [per_frame(result[0]), per_frame(result[1]), per_frame(result[2]), per_group(result[3])],
        [group_acc],
        8 * tokens * width * inner + 4 * tokens * rows * inner,
    )
    out_t_f = to_frames(out_t)

    x_count = lax.axis_size("x")
    wide_rows, pair_rows = term_rows(inner, width, y_count, x_count)
    result = (
        shape_of(seq_count, groups, rows // seq_count, width),
        shape_of(2, x_count * wide_rows + y_count * pair_rows, LANES),
    )
    total = pltpu.VMEM((inner, width), F32)
    ln_grad, terms = run(
        functools.partial(temporal_backward, slots=slots, y_count=y_count, x_count=x_count),
        groups,
        [info, modulation, grad_s, mixed_s, out_s_s, qkv_t, out_t, modulated, w_temporal, w_qkv],
        [
            SCALARS,
            whole(modulation),
            per_group(grad_s),
            per_frame(mixed_s),
            per_group(out_s_s),
            per_frame(qkv_t),
            per_group(out_t),
            per_frame(modulated),
            whole(w_temporal),
            whole(w_qkv),
        ],
        result,
        [per_group(result[0]), whole(result[1])],
        [group_acc, group_acc, group_acc, total, total, pltpu.VMEM((2, 3 * inner, width // 2), F32)],
        18 * tokens * width * inner + 10 * tokens * rows * inner,
    )
    terms, out_t_f = lax.optimization_barrier((terms, out_t_f))
    ln_frames = to_frames(ln_grad)
    summed = reduce_grads(coords, terms, inner, width)

    block_out = shape_of(frame_dev, slot_total, width)
    block_out = run(
        block_forward,
        frame_dev,
        [info, modulation, stream, out_s, out_t_f, w_spatial, w_temporal],
        [SCALARS, whole(modulation), per_frame(stream), per_frame(out_s), per_frame(out_t_f), whole(w_spatial), whole(w_temporal)],
        block_out,
        per_frame(block_out),
        [],
        4 * tokens * width * inner,
    )
    result = (shape_of(frame_dev, slot_total, width), shape_of(frame_dev, slot_total, 3 * inner))
    hidden_grad, qkv_s_grad = run(
        spatial_backward,
        frame_dev,
        [info, grad_out, ln_frames, packed_qkv, out_s, w_spatial],
        [SCALARS, per_frame(grad_out), per_frame(ln_frames), per_frame(packed_qkv), per_frame(out_s), whole(w_spatial)],
        result,
        [per_frame(result[0]), per_frame(result[1])],
        [frame_acc, frame_acc, frame_acc],
        2 * tokens * width * inner + 10 * tokens * slot_total * inner,
    )
    return (block_out[None], hidden_grad[None], qkv_s_grad[None], summed[0], summed[1], summed[2])


def solution(mesh):
    torus = Mesh(mesh.devices.reshape(4, 8, 4, 2), ("x", "z", "y", "c"))
    dp, seq = ("x", "z"), ("y", "c")
    tokens = P(dp, seq, None, None)
    weight = P(seq, dp)
    placed = (
        tokens,
        tokens,
        weight,
        weight,
        weight,
        P(dp, None, None),
        tokens,
        P(dp),
        P(dp),
        P(dp),
    )
    return jax.shard_map(
        on_device,
        mesh=torus,
        in_specs=placed,
        out_specs=(tokens, tokens, tokens, weight, weight, weight),
        check_vma=False,
    )
```

```python
import functools
import math

import jax
import jax.numpy as jnp
from jax import lax
from jax.experimental import pallas as pl
from jax.experimental.pallas import tpu as pltpu
from jax.sharding import Mesh
from jax.sharding import PartitionSpec as P

HEAD_DIM = 72
EPSILON = 1e-06
NEGATIVE = -1e30
LANES = 128
VMEM_BYTES = 56 * 1024 * 1024
F32 = jnp.float32
BF16 = jnp.bfloat16


def dot_nn(left, right):
    return lax.dot_general(left, right, (((1,), (0,)), ((), ())), preferred_element_type=F32)


def dot_nt(left, right):
    return lax.dot_general(left, right, (((1,), (1,)), ((), ())), preferred_element_type=F32)


def dot_tn(left, right):
    return lax.dot_general(left, right, (((0,), (0,)), ((), ())), preferred_element_type=F32)


def head_windows(inner):
    windows = []
    for head in range(inner // HEAD_DIM):
        low = head * HEAD_DIM
        start = low // LANES * LANES
        stop = min(-(-(low + HEAD_DIM) // LANES) * LANES, inner)
        windows.append((start, stop, low - start))
    return windows


def own_lanes(window):
    start, stop, offset = window
    lane = lax.broadcasted_iota(jnp.int32, (1, stop - start), 1)
    return (lane >= offset) & (lane < offset + HEAD_DIM)


def only(lanes, rows):
    return jnp.where(lanes, rows, jnp.zeros((), rows.dtype))


def softmax_rows(query, key, allowed):
    logits = dot_nt(query, key) * (1.0 / math.sqrt(HEAD_DIM))
    logits = jnp.where(allowed, logits, NEGATIVE)
    powers = jnp.exp(logits - jnp.max(logits, axis=1, keepdims=True))
    return powers * (1.0 / jnp.sum(powers, axis=1, keepdims=True))


def attend_heads(query, key, value, allowed, out_acc):
    out_acc[...] = jnp.zeros(out_acc.shape, F32)
    for window in head_windows(query.shape[1]):
        start, stop, _ = window
        lanes = own_lanes(window)
        probs = softmax_rows(query[:, start:stop], only(lanes, key[:, start:stop]), allowed)
        out_acc[:, start:stop] += dot_nn(probs.astype(BF16), only(lanes, value[:, start:stop]))


def attend_heads_back(query, key, value, out, out_grad, allowed, q_acc, k_acc, v_acc):
    factor = 1.0 / math.sqrt(HEAD_DIM)
    for acc in (q_acc, k_acc, v_acc):
        acc[...] = jnp.zeros(acc.shape, F32)
    for window in head_windows(query.shape[1]):
        start, stop, _ = window
        lanes = own_lanes(window)
        key_h = only(lanes, key[:, start:stop])
        grad_h = only(lanes, out_grad[:, start:stop])
        probs = softmax_rows(query[:, start:stop], key_h, allowed)
        prob_grad = dot_nt(grad_h, value[:, start:stop])
        row_delta = jnp.sum(
            grad_h.astype(F32) * out[:, start:stop].astype(F32), axis=1, keepdims=True
        )
        logit_grad = (probs * (prob_grad - row_delta)).astype(BF16)
        q_acc[:, start:stop] += dot_nn(logit_grad, key_h) * factor
        k_acc[:, start:stop] += dot_tn(logit_grad, only(lanes, query[:, start:stop])) * factor
        v_acc[:, start:stop] += dot_tn(probs.astype(BF16), grad_h)


def slot_masks(info_ref, rows, slots):
    frames, limit, first = info_ref[0], info_ref[1], info_ref[2]
    group = pl.program_id(0)
    row = lax.broadcasted_iota(jnp.int32, (rows, 1), 0)
    slot = first + group * slots + row % slots
    token = (row // slots < frames) & (slot < limit)
    col = lax.broadcasted_iota(jnp.int32, (1, rows), 1)
    allowed = (row % slots == col % slots) & (col // slots < frames)
    return token.astype(F32), allowed


def normalised(mixed):
    values = mixed.astype(F32)
    centred = values - jnp.mean(values, axis=1, keepdims=True)
    inv_std = lax.rsqrt(jnp.mean(centred * centred, axis=1, keepdims=True) + EPSILON)
    return centred * inv_std, inv_std


def narrow_rows(w_main, inner):
    count, _, width = w_main.shape
    cut = width // count // 2
    blocks = []
    for x in range(count):
        blocks += [w_main[x, :cut, :inner], w_main[x, :cut, inner:]]
    return jnp.concatenate(blocks, axis=0)


def wide_rows(w_main, inner):
    count, _, width = w_main.shape
    cut = width // count // 2
    return jnp.concatenate([w_main[x, cut:] for x in range(count)], axis=0)


def temporal_forward(
    info, mod, stream, out_s, w_main, mixed_ref, mod_ref, qkv_ref, out_ref, acc, slots
):
    rows, inner = acc.shape
    width = stream.shape[-1]
    token, allowed = slot_masks(info, rows, slots)
    branch = dot_nt(out_s[...].reshape(rows, inner), narrow_rows(w_main, inner))
    mixed = (stream[...].reshape(rows, width).astype(F32) + token * branch).astype(BF16)
    mixed_ref[...] = mixed.reshape(mixed_ref.shape)
    normed, _ = normalised(mixed)
    modulated = (normed * (1.0 + mod[0, 1:2]) + mod[0, 0:1]).astype(BF16)
    mod_ref[...] = modulated.reshape(mod_ref.shape)
    qkv = dot_nt(modulated, wide_rows(w_main, inner)).astype(BF16)
    qkv_ref[...] = qkv.reshape(qkv_ref.shape)
    attend_heads(
        qkv[:, :inner], qkv[:, inner : 2 * inner], qkv[:, 2 * inner :], allowed, acc
    )
    out_ref[...] = acc[...].astype(BF16).reshape(out_ref.shape)


def temporal_backward(
    info, mod, grad, mixed, out_s, qkv_ref, out_t, modulated, w_other, w_main, ln_ref, terms,
    q_acc, k_acc, v_acc, sum_s, sum_t, sum_q, slots, y_count, x_count,
):
    rows, inner = q_acc.shape
    width = grad.shape[-1]
    token, allowed = slot_masks(info, rows, slots)

    @pl.when(pl.program_id(0) == 0)
    def _():
        for total in (sum_s, sum_t, sum_q):
            total[...] = jnp.zeros(total.shape, F32)

    grad_f = grad[...].reshape(rows, width).astype(F32)
    branch_grad = (token * mod[0, 2:3] * grad_f).astype(BF16)
    out_grad = dot_nn(branch_grad, narrow_rows(w_other, inner)).astype(BF16)
    qkv = qkv_ref[...].reshape(rows, 3 * inner)
    out = out_t[...].reshape(rows, inner)
    attend_heads_back(
        qkv[:, :inner], qkv[:, inner : 2 * inner], qkv[:, 2 * inner :], out, out_grad, allowed,
        q_acc, k_acc, v_acc,
    )
    dqkv = jnp.concatenate([q_acc[...], k_acc[...], v_acc[...]], axis=1).astype(BF16)

    norm_grad = dot_nn(dqkv, wide_rows(w_main, inner)) * (1.0 + mod[0, 1:2])
    normed, inv_std = normalised(mixed[...].reshape(rows, width))
    first = jnp.mean(norm_grad, axis=1, keepdims=True)
    second = jnp.mean(norm_grad * normed, axis=1, keepdims=True)
    ln_grad = (inv_std * (norm_grad - first - normed * second)).astype(BF16)
    ln_ref[...] = ln_grad.reshape(ln_ref.shape)
    hidden_grad = (grad_f + ln_grad.astype(F32)).astype(BF16)
    spatial_grad = (token * hidden_grad.astype(F32)).astype(BF16)

    sum_t[...] += dot_tn(out, branch_grad)
    sum_s[...] += dot_tn(out_s[...].reshape(rows, inner), spatial_grad)
    left = modulated[...].reshape(rows, width)
    step = width // (2 * y_count)
    for c in range(2):
        pieces = [left[:, (2 * y + c) * step : (2 * y + c + 1) * step] for y in range(y_count)]
        sum_q[c] += dot_tn(dqkv, jnp.concatenate(pieces, axis=1))

    @pl.when(pl.program_id(0) == pl.num_programs(0) - 1)
    def _():
        store_terms(sum_s, sum_t, sum_q, terms, y_count, x_count)


def term_rows(inner, width, y_count, x_count):
    tiles = -(-(width // 2) // LANES)
    return tiles * (3 * inner // x_count), width // LANES * (inner // y_count)


def store_terms(sum_s, sum_t, sum_q, terms, y_count, x_count):
    inner, width = sum_s.shape
    span, step = 3 * inner // x_count, inner // (2 * y_count)
    wide, pair = term_rows(inner, width, y_count, x_count)
    half = width // 2
    for c in range(2):
        for x in range(x_count):
            for tile in range(wide // span):
                low, high = tile * LANES, min((tile + 1) * LANES, half)
                block = sum_q[c, x * span : (x + 1) * span, low:high]
                if high - low < LANES:
                    rest = jnp.zeros((span, LANES - (high - low)), F32)
                    block = jnp.concatenate([block, rest], axis=1)
                start = x * wide + tile * span
                terms[c, start : start + span] = block.astype(BF16)
        for y in range(y_count):
            place = (2 * y + c) * step
            for tile in range(width // LANES):
                lanes = slice(tile * LANES, (tile + 1) * LANES)
                block = jnp.concatenate(
                    [sum_s[place : place + step, lanes], sum_t[place : place + step, lanes]],
                    axis=0,
                )
                start = x_count * wide + y * pair + tile * 2 * step
                terms[c, start : start + 2 * step] = block.astype(BF16)


def frame_keys(info_ref, rows):
    return lax.broadcasted_iota(jnp.int32, (1, rows), 1) < info_ref[1]


def frame_tokens(info_ref, rows):
    row = lax.broadcasted_iota(jnp.int32, (rows, 1), 0)
    alive = info_ref[3] + pl.program_id(0) < info_ref[0]
    return ((row < info_ref[1]) & alive).astype(F32)


def spatial_forward(info, qkv_ref, out_ref, acc):
    rows, inner = acc.shape
    qkv = qkv_ref[0]
    attend_heads(
        qkv[:, :inner], qkv[:, inner : 2 * inner], qkv[:, 2 * inner :], frame_keys(info, rows), acc
    )
    out_ref[0] = acc[...].astype(BF16)


def block_forward(info, mod, stream, out_s, out_t, w_main, w_other, block_ref):
    rows, inner = out_s.shape[1:]
    token = frame_tokens(info, rows)
    spatial = dot_nt(out_s[0], narrow_rows(w_main, inner))
    mixed = (stream[0].astype(F32) + token * spatial).astype(BF16)
    branch = dot_nt(out_t[0], narrow_rows(w_other, inner))
    block_ref[0] = (mixed.astype(F32) + token * mod[0, 2:3] * branch).astype(BF16)


def spatial_backward(
    info, grad, ln_grad, qkv_ref, out_s, w_main, hidden_ref, dqkv_ref, q_acc, k_acc, v_acc
):
    rows, inner = q_acc.shape
    hidden_grad = (grad[0].astype(F32) + ln_grad[0].astype(F32)).astype(BF16)
    hidden_ref[0] = hidden_grad
    branch_grad = (frame_tokens(info, rows) * hidden_grad.astype(F32)).astype(BF16)
    out_grad = dot_nn(branch_grad, narrow_rows(w_main, inner)).astype(BF16)
    qkv = qkv_ref[0]
    attend_heads_back(
        qkv[:, :inner], qkv[:, inner : 2 * inner], qkv[:, 2 * inner :], out_s[0], out_grad,
        frame_keys(info, rows), q_acc, k_acc, v_acc,
    )
    dqkv_ref[0] = jnp.concatenate([q_acc[...], k_acc[...], v_acc[...]], axis=1).astype(BF16)


def whole(array):
    return pl.BlockSpec(
        array.shape, lambda step: (0,) * array.ndim, pipeline_mode=pl.Buffered(1)
    )


def per_frame(array):
    return pl.BlockSpec((1,) + array.shape[1:], lambda step: (step, 0, 0))


def per_group(array):
    return pl.BlockSpec(
        (array.shape[0], 1) + array.shape[2:], lambda step: (0, step, 0, 0)
    )


SCALARS = pl.BlockSpec(memory_space=pltpu.SMEM)


def run(body, steps, operands, specs, results, result_specs, scratch, flops):
    leaves = operands + jax.tree.leaves(results)
    moved = sum(math.prod(a.shape) * a.dtype.itemsize for a in leaves)
    return pl.pallas_call(
        body,
        grid=(steps,),
        in_specs=specs,
        out_specs=result_specs,
        out_shape=results,
        scratch_shapes=scratch,
        compiler_params=pltpu.CompilerParams(vmem_limit_bytes=VMEM_BYTES),
        cost_estimate=pl.CostEstimate(flops=flops, bytes_accessed=moved, transcendentals=0),
    )(*operands)


def shape_of(*dims, dtype=BF16):
    return jax.ShapeDtypeStruct(dims, dtype)


def exchange(rows, axes):
    return lax.all_to_all(rows, axes, 0, 0, tiled=True)


def shift(rows, axis, hops):
    count = lax.axis_size(axis)
    return lax.ppermute(rows, axis, [(at, (at + hops) % count) for at in range(count)])


def shift_both(rows, axis, hops):
    count = lax.axis_size(axis)
    pairs = []
    for at in range(count):
        pairs.append((2 * at, 2 * ((at - hops) % count)))
        pairs.append((2 * at + 1, 2 * ((at + hops) % count) + 1))
    return lax.ppermute(rows, (axis, "c"), pairs)


def swap(rows):
    return shift(rows, "c", 1)


def place_along_z(info, own, near, mid, far, last, near_p, mid_p, far_p, out):
    place, count = info[1], out.shape[0]
    sign = 1 - 2 * info[3]
    out[place] = own[...]
    out[lax.rem(place + count // 2, count)] = last[...]
    for hops, mine, other in ((1, near, near_p), (2, mid, mid_p), (3, far, far_p)):
        out[lax.rem(place + sign * hops + count, count)] = mine[...]
        out[lax.rem(place - sign * hops + count, count)] = other[...]


def place_along_x(info, own, near, near_p, part, part_p, out):
    place, count = info[0], out.shape[0]
    sign = 1 - 2 * info[3]
    half = part.shape[0]
    opposite = lax.rem(place + count // 2, count)
    out[place] = own[...]
    out[lax.rem(place + sign + count, count)] = near[...]
    out[lax.rem(place - sign + count, count)] = near_p[...]

    @pl.when(info[3] == 0)
    def _():
        out[opposite, :half] = part[...]
        out[opposite, half:] = part_p[...]

    @pl.when(info[3] != 0)
    def _():
        out[opposite, :half] = part_p[...]
        out[opposite, half:] = part[...]


def in_vmem(body, info, blocks, results):
    vmem = pl.BlockSpec(memory_space=pltpu.VMEM)
    return pl.pallas_call(
        body,
        in_specs=[SCALARS] + [vmem] * len(blocks),
        out_specs=jax.tree.map(lambda _: vmem, results),
        out_shape=results,
        compiler_params=pltpu.CompilerParams(vmem_limit_bytes=VMEM_BYTES),
    )(info, *blocks)


def tie(*values):
    return lax.optimization_barrier(values)


def near_rows(out_spatial, qkv_temporal, out_temporal):
    half, narrow = out_spatial.shape
    packed = jnp.concatenate(
        [jnp.concatenate([out_spatial.T, out_temporal.T], axis=1), qkv_temporal.T], axis=0
    )
    near = jnp.transpose(lax.all_gather(packed, ("y", "c"), axis=0, tiled=False), (1, 0, 2))
    thin = near[:narrow, :, :half].reshape(narrow, -1)
    other = near[:narrow, :, half:].reshape(narrow, -1)
    wide = near[narrow:].reshape(near.shape[0] - narrow, -1)
    return (fold(thin), wide, fold(other))


def fold(rows):
    cut = rows.shape[-2] // 2
    return jnp.concatenate([rows[..., :cut, :], rows[..., cut:, :]], axis=-1)


def unfold(rows):
    cut = rows.shape[-1] // 2
    return jnp.concatenate([rows[..., :cut], rows[..., cut:]], axis=-2)


def gather_z(coords, rows):
    arrived = [shift_both(rows, "z", hops) for hops in (1, 2, 3)] + [shift(rows, "z", 4)]
    swapped = [swap(block) for block in arrived[:3]]
    result = shape_of(lax.axis_size("z"), *rows.shape)
    return arrived, lambda tied: in_vmem(place_along_z, coords, [rows] + tied + swapped, result)


def gather_x(coords, rows, first):
    size = rows.shape[0] // 2
    onward = lax.dynamic_slice_in_dim(first, lax.axis_index("c") * size, size, 0)
    second = shift_both(onward, "x", 1)
    result = shape_of(lax.axis_size("x"), *rows.shape)
    return in_vmem(place_along_x, coords, [rows, first, swap(first), second, swap(second)], result)


def scatter(blocks, axis):
    count, place = lax.axis_size(axis), lax.axis_index(axis)
    arrived = []
    for hops in range(1, count):
        block = lax.dynamic_index_in_dim(blocks, (place + hops) % count, 0, keepdims=False)
        arrived.append(shift(block, axis, hops))
    return arrived


def scatter_sum(blocks, axis):
    place = lax.axis_index(axis)
    total = lax.dynamic_index_in_dim(blocks, place, 0, keepdims=False).astype(F32)
    for block in scatter(blocks, axis):
        total = total + block.astype(F32)
    return total


def regroup_wide(info, blocks, first, second, third, out):
    y_count, span, lanes = out.shape
    total = blocks[info[0]].astype(F32)
    for block in (first, second, third):
        total = total + block[...].astype(F32)
    tiles = [total[at : at + span] for at in range(0, total.shape[0], span)]
    flat = jnp.concatenate(tiles, axis=1)
    step = (flat.shape[1] - LANES // 2) // y_count
    for y in range(y_count):
        block = flat[:, y * step : (y + 1) * step]
        rest = jnp.zeros((span, lanes - step), F32)
        out[y] = jnp.concatenate([block, rest], axis=1).astype(BF16)


def regroup_pair(info, blocks, out):
    x_count, span, lanes = out.shape
    total = blocks[0].astype(F32)
    for y in range(1, blocks.shape[0]):
        total = total + blocks[y].astype(F32)
    width = x_count * span
    step = total.shape[0] // (width // LANES)
    tiles = [total[at : at + step].T for at in range(0, total.shape[0], step)]
    flat = jnp.concatenate(tiles, axis=0)
    flat = jnp.concatenate([flat, jnp.zeros((width, lanes - step), F32)], axis=1)
    for x in range(x_count):
        out[x] = flat[x * span : (x + 1) * span].astype(BF16)


def reduce_start(coords, terms, inner, width, beside):
    x_count, y_count = lax.axis_size("x"), lax.axis_size("y")
    wide_rows, pair_rows = term_rows(inner, width, y_count, x_count)
    halves = exchange(terms, "c")
    total = (halves[0].astype(F32) + halves[1].astype(F32)).astype(BF16)
    wide = total[: x_count * wide_rows].reshape(x_count, wide_rows, LANES)
    pair = total[x_count * wide_rows :].reshape(y_count, pair_rows, LANES)

    arrived = scatter(wide, "x")
    pair = exchange(pair, "y")
    arrived[2], beside = tie(arrived[2], beside)
    wide = in_vmem(
        regroup_wide,
        coords,
        [wide] + arrived,
        shape_of(y_count, 3 * inner // x_count, 2 * LANES),
    )
    blocks = in_vmem(
        regroup_pair, coords, [pair], shape_of(x_count, width // x_count, 2 * LANES)
    )
    return (wide, blocks), beside, pair


def reduce_end(reduced, inner, width):
    wide, pair = reduced
    z_count = lax.axis_size("z")
    step = width // (2 * lax.axis_size("y"))
    wide = scatter_sum(wide, "y").astype(BF16).reshape(z_count, -1, 2 * LANES)
    pair = scatter_sum(pair, "x").astype(BF16).reshape(z_count, -1, 2 * LANES)
    total = jnp.sum(exchange(jnp.concatenate([pair, wide], axis=1), "z").astype(F32), axis=0)
    narrow = pair.shape[1]
    half = step // 2
    return (total[:narrow, :half].T, total[narrow:, :step].T, total[:narrow, half:step].T)


def on_device(
    hidden,
    spatial_qkv,
    out_spatial,
    qkv_temporal,
    out_temporal,
    modulation,
    cotangent,
    frame_count,
    patch_height,
    patch_width,
):
    seq_count = lax.axis_size(("y", "c"))
    seq_place = lax.axis_index(("y", "c"))
    y_count = lax.axis_size("y")
    stream = hidden[0]
    grad_out = cotangent[0]
    packed_qkv = spatial_qkv[0]
    frame_dev, slot_total, width = stream.shape
    slot_dev = slot_total // seq_count
    inner = out_spatial.shape[0] * seq_count
    slots = 8
    groups = slot_dev // slots
    rows = frame_dev * seq_count * slots
    coords = jnp.stack([lax.axis_index(name) for name in ("x", "z", "y", "c")]).astype(jnp.int32)
    info = jnp.stack(
        [
            frame_count[0],
            patch_height[0] * patch_width[0],
            seq_place * slot_dev,
            seq_place * frame_dev,
        ]
    ).astype(jnp.int32)

    def to_slots(tokens):
        split = tokens.reshape(frame_dev, seq_count, groups, slots, -1)
        split = jnp.transpose(split, (1, 2, 0, 3, 4))
        return exchange(split.reshape(seq_count, groups, frame_dev * slots, -1), ("y", "c"))

    def to_frames(tokens):
        moved = exchange(tokens, ("y", "c")).reshape(seq_count, groups, frame_dev, slots, -1)
        return jnp.transpose(moved, (2, 0, 1, 3, 4)).reshape(frame_dev, slot_total, -1)

    stream_s = to_slots(stream)
    frame_acc = pltpu.VMEM((slot_total, inner), F32)
    out_s = shape_of(frame_dev, slot_total, inner)
    out_s = run(
        spatial_forward,
        frame_dev,
        [info, packed_qkv],
        [SCALARS, per_frame(packed_qkv)],
        out_s,
        per_frame(out_s),
        [frame_acc],
        4 * frame_dev * slot_total * slot_total * inner,
    )
    thin, wide, other = near_rows(out_spatial, qkv_temporal, out_temporal)
    cut = thin.shape[0]
    rows_z = jnp.concatenate([thin, wide], axis=0)
    arrived, finish = gather_z(coords, rows_z)
    arrived[3], stream_s, out_s = tie(arrived[3], stream_s, out_s)
    stack = finish(arrived)
    grad_out_tied, _ = tie(grad_out, stream_s)
    grad_s = to_slots(grad_out_tied)
    thin = fold(unfold(stack[:, :cut]).reshape(-1, inner))
    wide = stack[:, cut:].reshape(-1, width)
    rows_x = jnp.concatenate([thin, wide], axis=0)
    first = shift_both(rows_x, "x", 1)
    other, _ = tie(other, stack)
    arrived, finish = gather_z(coords, other)
    first, grad_s, arrived[3] = tie(first, grad_s, arrived[3])
    other = fold(unfold(finish(arrived)).reshape(-1, inner))
    out_s_sent, _ = tie(out_s, grad_s)
    out_s_s = to_slots(out_s_sent)
    w_main = gather_x(coords, rows_x, first)
    other, _ = tie(other, w_main)
    w_other = gather_x(coords, other, shift_both(other, "x", 1))

    group_acc = pltpu.VMEM((rows, inner), F32)
    result = (
        shape_of(groups, rows, width),
        shape_of(groups, rows, width),
        shape_of(groups, rows, 3 * inner),
        shape_of(seq_count, groups, rows // seq_count, inner),
    )
    tokens = groups * rows
    mixed_s, modulated, qkv_t, out_t = run(
        functools.partial(temporal_forward, slots=slots),
        groups,
        [info, modulation, stream_s, out_s_s, w_main],
        [SCALARS, whole(modulation), per_group(stream_s), per_group(out_s_s), whole(w_main)],
        result,
        [per_frame(result[0]), per_frame(result[1]), per_frame(result[2]), per_group(result[3])],
        [group_acc],
        8 * tokens * width * inner + 4 * tokens * rows * inner,
    )
    out_t_f = to_frames(out_t)

    x_count = lax.axis_size("x")
    wide_rows, pair_rows = term_rows(inner, width, y_count, x_count)
    result = (
        shape_of(seq_count, groups, rows // seq_count, width),
        shape_of(2, x_count * wide_rows + y_count * pair_rows, LANES),
    )
    total = pltpu.VMEM((inner, width), F32)
    ln_grad, terms = run(
        functools.partial(temporal_backward, slots=slots, y_count=y_count, x_count=x_count),
        groups,
        [info, modulation, grad_s, mixed_s, out_s_s, qkv_t, out_t, modulated, w_other, w_main],
        [
            SCALARS,
            whole(modulation),
            per_group(grad_s),
            per_frame(mixed_s),
            per_group(out_s_s),
            per_frame(qkv_t),
            per_group(out_t),
            per_frame(modulated),
            whole(w_other),
            whole(w_main),
        ],
        result,
        [per_group(result[0]), whole(result[1])],
        [group_acc, group_acc, group_acc, total, total, pltpu.VMEM((2, 3 * inner, width // 2), F32)],
        18 * tokens * width * inner + 10 * tokens * rows * inner,
    )
    terms, out_t_f = lax.optimization_barrier((terms, out_t_f))
    block_out = shape_of(frame_dev, slot_total, width)
    block_out = run(
        block_forward,
        frame_dev,
        [info, modulation, stream, out_s, out_t_f, w_main, w_other],
        [
            SCALARS,
            whole(modulation),
            per_frame(stream),
            per_frame(out_s),
            per_frame(out_t_f),
            whole(w_main),
            whole(w_other),
        ],
        block_out,
        per_frame(block_out),
        [],
        4 * tokens * width * inner,
    )
    reduced, block_out, pair_ready = reduce_start(coords, terms, inner, width, block_out)
    ln_grad, _ = tie(ln_grad, pair_ready)
    ln_frames = to_frames(ln_grad)

    result = (shape_of(frame_dev, slot_total, width), shape_of(frame_dev, slot_total, 3 * inner))
    hidden_grad, qkv_s_grad = run(
        spatial_backward,
        frame_dev,
        [info, grad_out, ln_frames, packed_qkv, out_s, w_main],
        [
            SCALARS,
            per_frame(grad_out),
            per_frame(ln_frames),
            per_frame(packed_qkv),
            per_frame(out_s),
            whole(w_main),
        ],
        result,
        [per_frame(result[0]), per_frame(result[1])],
        [frame_acc, frame_acc, frame_acc],
        2 * tokens * width * inner + 10 * tokens * slot_total * inner,
    )
    summed = reduce_end(reduced, inner, width)
    return (block_out[None], hidden_grad[None], qkv_s_grad[None], summed[0], summed[1], summed[2])


def solution(mesh):
    torus = Mesh(mesh.devices.reshape(4, 8, 4, 2), ("x", "z", "y", "c"))
    dp, seq = ("x", "z"), ("y", "c")
    tokens = P(dp, seq, None, None)
    weight = P(seq, dp)
    placed = (
        tokens,
        tokens,
        weight,
        weight,
        weight,
        P(dp, None, None),
        tokens,
        P(dp),
        P(dp),
        P(dp),
    )
    return jax.shard_map(
        on_device,
        mesh=torus,
        in_specs=placed,
        out_specs=(tokens, tokens, tokens, weight, weight, weight),
        check_vma=False,
    )
```

```python
import functools
import math

import jax
import jax.numpy as jnp
from jax import lax
from jax.experimental import pallas as pl
from jax.experimental.pallas import tpu as pltpu
from jax.sharding import Mesh
from jax.sharding import PartitionSpec as P

HEAD_DIM = 72
EPSILON = 1e-06
NEGATIVE = -1e30
LANES = 128
VMEM_BYTES = 56 * 1024 * 1024
F32 = jnp.float32
BF16 = jnp.bfloat16


def dot_nn(left, right):
    return lax.dot_general(left, right, (((1,), (0,)), ((), ())), preferred_element_type=F32)


def dot_nt(left, right):
    return lax.dot_general(left, right, (((1,), (1,)), ((), ())), preferred_element_type=F32)


def dot_tn(left, right):
    return lax.dot_general(left, right, (((0,), (0,)), ((), ())), preferred_element_type=F32)


def head_windows(inner):
    windows = []
    for head in range(inner // HEAD_DIM):
        low = head * HEAD_DIM
        start = low // LANES * LANES
        stop = min(-(-(low + HEAD_DIM) // LANES) * LANES, inner)
        windows.append((start, stop, low - start))
    return windows


def own_lanes(window):
    start, stop, offset = window
    lane = lax.broadcasted_iota(jnp.int32, (1, stop - start), 1)
    return (lane >= offset) & (lane < offset + HEAD_DIM)


def only(lanes, rows):
    return jnp.where(lanes, rows, jnp.zeros((), rows.dtype))


def softmax_rows(query, key, allowed):
    logits = dot_nt(query, key) * (1.0 / math.sqrt(HEAD_DIM))
    logits = jnp.where(allowed, logits, NEGATIVE)
    powers = jnp.exp(logits - jnp.max(logits, axis=1, keepdims=True))
    return powers * (1.0 / jnp.sum(powers, axis=1, keepdims=True))


def attend_heads(query, key, value, allowed, out_acc):
    out_acc[...] = jnp.zeros(out_acc.shape, F32)
    for window in head_windows(query.shape[1]):
        start, stop, _ = window
        lanes = own_lanes(window)
        probs = softmax_rows(query[:, start:stop], only(lanes, key[:, start:stop]), allowed)
        out_acc[:, start:stop] += dot_nn(probs.astype(BF16), only(lanes, value[:, start:stop]))


def attend_heads_back(query, key, value, out, out_grad, allowed, q_acc, k_acc, v_acc):
    factor = 1.0 / math.sqrt(HEAD_DIM)
    for acc in (q_acc, k_acc, v_acc):
        acc[...] = jnp.zeros(acc.shape, F32)
    for window in head_windows(query.shape[1]):
        start, stop, _ = window
        lanes = own_lanes(window)
        key_h = only(lanes, key[:, start:stop])
        grad_h = only(lanes, out_grad[:, start:stop])
        probs = softmax_rows(query[:, start:stop], key_h, allowed)
        prob_grad = dot_nt(grad_h, value[:, start:stop])
        row_delta = jnp.sum(
            grad_h.astype(F32) * out[:, start:stop].astype(F32), axis=1, keepdims=True
        )
        logit_grad = (probs * (prob_grad - row_delta)).astype(BF16)
        q_acc[:, start:stop] += dot_nn(logit_grad, key_h) * factor
        k_acc[:, start:stop] += dot_tn(logit_grad, only(lanes, query[:, start:stop])) * factor
        v_acc[:, start:stop] += dot_tn(probs.astype(BF16), grad_h)


def slot_masks(info_ref, rows, slots):
    frames, limit, first = info_ref[0], info_ref[1], info_ref[2]
    group = pl.program_id(0)
    row = lax.broadcasted_iota(jnp.int32, (rows, 1), 0)
    slot = first + group * slots + row % slots
    token = (row // slots < frames) & (slot < limit)
    col = lax.broadcasted_iota(jnp.int32, (1, rows), 1)
    allowed = (row % slots == col % slots) & (col // slots < frames)
    return token.astype(F32), allowed


def normalised(mixed):
    values = mixed.astype(F32)
    centred = values - jnp.mean(values, axis=1, keepdims=True)
    inv_std = lax.rsqrt(jnp.mean(centred * centred, axis=1, keepdims=True) + EPSILON)
    return centred * inv_std, inv_std


def temporal_forward(
    info, mod, stream, out_s, w_spatial, w_qkv, mixed_ref, mod_ref, qkv_ref, out_ref, acc, slots
):
    rows, inner = acc.shape
    width = stream.shape[-1]
    token, allowed = slot_masks(info, rows, slots)
    branch = dot_nt(out_s[...].reshape(rows, inner), w_spatial[...])
    mixed = (stream[...].reshape(rows, width).astype(F32) + token * branch).astype(BF16)
    mixed_ref[...] = mixed.reshape(mixed_ref.shape)
    normed, _ = normalised(mixed)
    modulated = (normed * (1.0 + mod[0, 1:2]) + mod[0, 0:1]).astype(BF16)
    mod_ref[...] = modulated.reshape(mod_ref.shape)
    qkv = dot_nt(modulated, w_qkv[...]).astype(BF16)
    qkv_ref[...] = qkv.reshape(qkv_ref.shape)
    attend_heads(
        qkv[:, :inner], qkv[:, inner : 2 * inner], qkv[:, 2 * inner :], allowed, acc
    )
    out_ref[...] = acc[...].astype(BF16).reshape(out_ref.shape)


def temporal_backward(
    info, mod, grad, mixed, out_s, qkv_ref, out_t, modulated, w_temporal, w_qkv, ln_ref, terms,
    q_acc, k_acc, v_acc, sum_s, sum_t, sum_q, slots, y_count, x_count,
):
    rows, inner = q_acc.shape
    width = grad.shape[-1]
    token, allowed = slot_masks(info, rows, slots)

    @pl.when(pl.program_id(0) == 0)
    def _():
        for total in (sum_s, sum_t, sum_q):
            total[...] = jnp.zeros(total.shape, F32)

    grad_f = grad[...].reshape(rows, width).astype(F32)
    branch_grad = (token * mod[0, 2:3] * grad_f).astype(BF16)
    out_grad = dot_nn(branch_grad, w_temporal[...]).astype(BF16)
    qkv = qkv_ref[...].reshape(rows, 3 * inner)
    out = out_t[...].reshape(rows, inner)
    attend_heads_back(
        qkv[:, :inner], qkv[:, inner : 2 * inner], qkv[:, 2 * inner :], out, out_grad, allowed,
        q_acc, k_acc, v_acc,
    )
    dqkv = jnp.concatenate([q_acc[...], k_acc[...], v_acc[...]], axis=1).astype(BF16)

    norm_grad = dot_nn(dqkv, w_qkv[...]) * (1.0 + mod[0, 1:2])
    normed, inv_std = normalised(mixed[...].reshape(rows, width))
    first = jnp.mean(norm_grad, axis=1, keepdims=True)
    second = jnp.mean(norm_grad * normed, axis=1, keepdims=True)
    ln_grad = (inv_std * (norm_grad - first - normed * second)).astype(BF16)
    ln_ref[...] = ln_grad.reshape(ln_ref.shape)
    hidden_grad = (grad_f + ln_grad.astype(F32)).astype(BF16)
    spatial_grad = (token * hidden_grad.astype(F32)).astype(BF16)

    sum_t[...] += dot_tn(out, branch_grad)
    sum_s[...] += dot_tn(out_s[...].reshape(rows, inner), spatial_grad)
    left = modulated[...].reshape(rows, width)
    step = width // (2 * y_count)
    for c in range(2):
        pieces = [left[:, (2 * y + c) * step : (2 * y + c + 1) * step] for y in range(y_count)]
        sum_q[c] += dot_tn(dqkv, jnp.concatenate(pieces, axis=1))

    @pl.when(pl.program_id(0) == pl.num_programs(0) - 1)
    def _():
        store_terms(sum_s, sum_t, sum_q, terms, y_count, x_count)


def term_rows(inner, width, y_count, x_count):
    tiles = -(-(width // 2) // LANES)
    return tiles * (3 * inner // x_count), width // LANES * (inner // y_count)


def store_terms(sum_s, sum_t, sum_q, terms, y_count, x_count):
    inner, width = sum_s.shape
    span, step = 3 * inner // x_count, inner // (2 * y_count)
    wide, pair = term_rows(inner, width, y_count, x_count)
    half = width // 2
    for c in range(2):
        for x in range(x_count):
            for tile in range(wide // span):
                low, high = tile * LANES, min((tile + 1) * LANES, half)
                block = sum_q[c, x * span : (x + 1) * span, low:high]
                if high - low < LANES:
                    rest = jnp.zeros((span, LANES - (high - low)), F32)
                    block = jnp.concatenate([block, rest], axis=1)
                start = x * wide + tile * span
                terms[c, start : start + span] = block.astype(BF16)
        for y in range(y_count):
            place = (2 * y + c) * step
            for tile in range(width // LANES):
                lanes = slice(tile * LANES, (tile + 1) * LANES)
                block = jnp.concatenate(
                    [sum_s[place : place + step, lanes], sum_t[place : place + step, lanes]],
                    axis=0,
                )
                start = x_count * wide + y * pair + tile * 2 * step
                terms[c, start : start + 2 * step] = block.astype(BF16)


def frame_keys(info_ref, rows):
    return lax.broadcasted_iota(jnp.int32, (1, rows), 1) < info_ref[1]


def frame_tokens(info_ref, rows):
    row = lax.broadcasted_iota(jnp.int32, (rows, 1), 0)
    alive = info_ref[3] + pl.program_id(0) < info_ref[0]
    return ((row < info_ref[1]) & alive).astype(F32)


def spatial_forward(info, qkv_ref, out_ref, acc):
    rows, inner = acc.shape
    qkv = qkv_ref[0]
    attend_heads(
        qkv[:, :inner], qkv[:, inner : 2 * inner], qkv[:, 2 * inner :], frame_keys(info, rows), acc
    )
    out_ref[0] = acc[...].astype(BF16)


def block_forward(info, mod, stream, out_s, out_t, w_spatial, w_temporal, block_ref):
    rows = stream.shape[1]
    token = frame_tokens(info, rows)
    spatial = dot_nt(out_s[0], w_spatial[...])
    mixed = (stream[0].astype(F32) + token * spatial).astype(BF16)
    branch = dot_nt(out_t[0], w_temporal[...])
    block_ref[0] = (mixed.astype(F32) + token * mod[0, 2:3] * branch).astype(BF16)


def spatial_backward(
    info, grad, ln_grad, qkv_ref, out_s, w_spatial, hidden_ref, dqkv_ref, q_acc, k_acc, v_acc
):
    rows, inner = q_acc.shape
    hidden_grad = (grad[0].astype(F32) + ln_grad[0].astype(F32)).astype(BF16)
    hidden_ref[0] = hidden_grad
    branch_grad = (frame_tokens(info, rows) * hidden_grad.astype(F32)).astype(BF16)
    out_grad = dot_nn(branch_grad, w_spatial[...]).astype(BF16)
    qkv = qkv_ref[0]
    attend_heads_back(
        qkv[:, :inner], qkv[:, inner : 2 * inner], qkv[:, 2 * inner :], out_s[0], out_grad,
        frame_keys(info, rows), q_acc, k_acc, v_acc,
    )
    dqkv_ref[0] = jnp.concatenate([q_acc[...], k_acc[...], v_acc[...]], axis=1).astype(BF16)


def whole(array):
    return pl.BlockSpec(
        array.shape, lambda step: (0,) * array.ndim, pipeline_mode=pl.Buffered(1)
    )


def per_frame(array):
    return pl.BlockSpec((1,) + array.shape[1:], lambda step: (step, 0, 0))


def per_group(array):
    return pl.BlockSpec(
        (array.shape[0], 1) + array.shape[2:], lambda step: (0, step, 0, 0)
    )


SCALARS = pl.BlockSpec(memory_space=pltpu.SMEM)


def run(body, steps, operands, specs, results, result_specs, scratch, flops):
    leaves = operands + jax.tree.leaves(results)
    moved = sum(math.prod(a.shape) * a.dtype.itemsize for a in leaves)
    return pl.pallas_call(
        body,
        grid=(steps,),
        in_specs=specs,
        out_specs=result_specs,
        out_shape=results,
        scratch_shapes=scratch,
        compiler_params=pltpu.CompilerParams(vmem_limit_bytes=VMEM_BYTES),
        cost_estimate=pl.CostEstimate(flops=flops, bytes_accessed=moved, transcendentals=0),
    )(*operands)


def shape_of(*dims, dtype=BF16):
    return jax.ShapeDtypeStruct(dims, dtype)


def exchange(rows, axes):
    return lax.all_to_all(rows, axes, 0, 0, tiled=True)


def shift(rows, axis, hops):
    count = lax.axis_size(axis)
    return lax.ppermute(rows, axis, [(at, (at + hops) % count) for at in range(count)])


def shift_both(rows, axis, hops):
    count = lax.axis_size(axis)
    pairs = []
    for at in range(count):
        pairs.append((2 * at, 2 * ((at - hops) % count)))
        pairs.append((2 * at + 1, 2 * ((at + hops) % count) + 1))
    return lax.ppermute(rows, (axis, "c"), pairs)


def swap(rows):
    return shift(rows, "c", 1)


def place_along_z(info, own, near, mid, far, last, near_p, mid_p, far_p, out):
    place, count = info[1], out.shape[0]
    sign = 1 - 2 * info[3]
    out[place] = own[...]
    out[lax.rem(place + count // 2, count)] = last[...]
    for hops, mine, other in ((1, near, near_p), (2, mid, mid_p), (3, far, far_p)):
        out[lax.rem(place + sign * hops + count, count)] = mine[...]
        out[lax.rem(place - sign * hops + count, count)] = other[...]


def place_along_x(info, own, near, near_p, part, part_p, spatial, temporal, wide, out):
    place, count = info[0], out.shape[0]
    sign = 1 - 2 * info[3]
    half = part.shape[0]
    opposite = lax.rem(place + count // 2, count)
    out[place] = own[...]
    out[lax.rem(place + sign + count, count)] = near[...]
    out[lax.rem(place - sign + count, count)] = near_p[...]

    @pl.when(info[3] == 0)
    def _():
        out[opposite, :half] = part[...]
        out[opposite, half:] = part_p[...]

    @pl.when(info[3] != 0)
    def _():
        out[opposite, :half] = part_p[...]
        out[opposite, half:] = part[...]

    cut, inner = out.shape[2] // count // 2, out.shape[2] // 2
    span = wide.shape[0] // count
    for x in range(count):
        for number, result in ((0, spatial), (1, temporal)):
            block = out[x, number * cut : (number + 1) * cut]
            result[2 * x * cut : (2 * x + 1) * cut] = block[:, :inner]
            result[(2 * x + 1) * cut : (2 * x + 2) * cut] = block[:, inner:]
        wide[x * span : (x + 1) * span] = out[x, 2 * cut :]


def in_vmem(body, info, blocks, results, scratch=()):
    vmem = pl.BlockSpec(memory_space=pltpu.VMEM)
    return pl.pallas_call(
        body,
        in_specs=[SCALARS] + [vmem] * len(blocks),
        out_specs=jax.tree.map(lambda _: vmem, results),
        out_shape=results,
        scratch_shapes=list(scratch),
        compiler_params=pltpu.CompilerParams(vmem_limit_bytes=VMEM_BYTES),
    )(info, *blocks)


def tie(*values):
    return lax.optimization_barrier(values)


def near_rows(out_spatial, qkv_temporal, out_temporal):
    half, narrow = out_spatial.shape
    packed = jnp.concatenate(
        [jnp.concatenate([out_spatial.T, out_temporal.T], axis=1), qkv_temporal.T], axis=0
    )
    near = jnp.transpose(lax.all_gather(packed, ("y", "c"), axis=0, tiled=False), (1, 0, 2))
    thin = near[:narrow, :, :half].reshape(narrow, -1)
    other = near[:narrow, :, half:].reshape(narrow, -1)
    wide = near[narrow:].reshape(near.shape[0] - narrow, -1)
    return (fold(thin), wide, fold(other))


def fold(rows):
    cut = rows.shape[-2] // 2
    return jnp.concatenate([rows[..., :cut, :], rows[..., cut:, :]], axis=-1)


def unfold(rows):
    cut = rows.shape[-1] // 2
    return jnp.concatenate([rows[..., :cut], rows[..., cut:]], axis=-2)


def gather_z(coords, rows):
    arrived = [shift_both(rows, "z", hops) for hops in (1, 2, 3)] + [shift(rows, "z", 4)]
    swapped = [swap(block) for block in arrived[:3]]
    result = shape_of(lax.axis_size("z"), *rows.shape)
    return in_vmem(place_along_z, coords, [rows] + arrived + swapped, result)


def scatter(blocks, axis):
    count, place = lax.axis_size(axis), lax.axis_index(axis)
    arrived = []
    for hops in range(1, count):
        block = lax.dynamic_index_in_dim(blocks, (place + hops) % count, 0, keepdims=False)
        arrived.append(shift(block, axis, hops))
    return arrived


def scatter_sum(blocks, axis):
    place = lax.axis_index(axis)
    total = lax.dynamic_index_in_dim(blocks, place, 0, keepdims=False).astype(F32)
    for block in scatter(blocks, axis):
        total = total + block.astype(F32)
    return total


def regroup_wide(info, blocks, first, second, third, out):
    y_count, span, lanes = out.shape
    total = blocks[info[0]].astype(F32)
    for block in (first, second, third):
        total = total + block[...].astype(F32)
    tiles = [total[at : at + span] for at in range(0, total.shape[0], span)]
    flat = jnp.concatenate(tiles, axis=1)
    step = (flat.shape[1] - LANES // 2) // y_count
    for y in range(y_count):
        block = flat[:, y * step : (y + 1) * step]
        rest = jnp.zeros((span, lanes - step), F32)
        out[y] = jnp.concatenate([block, rest], axis=1).astype(BF16)


def regroup_pair(info, blocks, out):
    x_count, span, lanes = out.shape
    total = blocks[0].astype(F32)
    for y in range(1, blocks.shape[0]):
        total = total + blocks[y].astype(F32)
    width = x_count * span
    step = total.shape[0] // (width // LANES)
    tiles = [total[at : at + step].T for at in range(0, total.shape[0], step)]
    flat = jnp.concatenate(tiles, axis=0)
    flat = jnp.concatenate([flat, jnp.zeros((width, lanes - step), F32)], axis=1)
    for x in range(x_count):
        out[x] = flat[x * span : (x + 1) * span].astype(BF16)


def reduce_start(coords, terms, inner, width, beside):
    x_count, y_count = lax.axis_size("x"), lax.axis_size("y")
    wide_rows, pair_rows = term_rows(inner, width, y_count, x_count)
    halves = exchange(terms, "c")
    total = (halves[0].astype(F32) + halves[1].astype(F32)).astype(BF16)
    wide = total[: x_count * wide_rows].reshape(x_count, wide_rows, LANES)
    pair = total[x_count * wide_rows :].reshape(y_count, pair_rows, LANES)

    arrived = scatter(wide, "x")
    pair = exchange(pair, "y")
    arrived[2], beside = tie(arrived[2], beside)
    wide = in_vmem(
        regroup_wide,
        coords,
        [wide] + arrived,
        shape_of(y_count, 3 * inner // x_count, 2 * LANES),
    )
    blocks = in_vmem(
        regroup_pair, coords, [pair], shape_of(x_count, width // x_count, 2 * LANES)
    )
    return (wide, blocks), beside, pair


def reduce_end(reduced, inner, width, beside):
    wide, pair = reduced
    z_count = lax.axis_size("z")
    step = width // (2 * lax.axis_size("y"))
    wide = scatter_sum(wide, "y").astype(BF16).reshape(z_count, -1, 2 * LANES)
    wide, beside = tie(wide, beside)
    pair = scatter_sum(pair, "x").astype(BF16).reshape(z_count, -1, 2 * LANES)
    total = jnp.sum(exchange(jnp.concatenate([pair, wide], axis=1), "z").astype(F32), axis=0)
    narrow = pair.shape[1]
    half = step // 2
    summed = (total[:narrow, :half].T, total[narrow:, :step].T, total[:narrow, half:step].T)
    return summed, beside


def on_device(
    hidden,
    spatial_qkv,
    out_spatial,
    qkv_temporal,
    out_temporal,
    modulation,
    cotangent,
    frame_count,
    patch_height,
    patch_width,
):
    seq_count = lax.axis_size(("y", "c"))
    seq_place = lax.axis_index(("y", "c"))
    y_count = lax.axis_size("y")
    stream = hidden[0]
    grad_out = cotangent[0]
    packed_qkv = spatial_qkv[0]
    frame_dev, slot_total, width = stream.shape
    slot_dev = slot_total // seq_count
    inner = out_spatial.shape[0] * seq_count
    slots = 8
    groups = slot_dev // slots
    rows = frame_dev * seq_count * slots
    coords = jnp.stack([lax.axis_index(name) for name in ("x", "z", "y", "c")]).astype(jnp.int32)
    info = jnp.stack(
        [
            frame_count[0],
            patch_height[0] * patch_width[0],
            seq_place * slot_dev,
            seq_place * frame_dev,
        ]
    ).astype(jnp.int32)

    def to_slots(tokens):
        split = tokens.reshape(frame_dev, seq_count, groups, slots, -1)
        split = jnp.transpose(split, (1, 2, 0, 3, 4))
        return exchange(split.reshape(seq_count, groups, frame_dev * slots, -1), ("y", "c"))

    def to_frames(tokens):
        moved = exchange(tokens, ("y", "c")).reshape(seq_count, groups, frame_dev, slots, -1)
        return jnp.transpose(moved, (2, 0, 1, 3, 4)).reshape(frame_dev, slot_total, -1)

    frame_acc = pltpu.VMEM((slot_total, inner), F32)
    out_s = shape_of(frame_dev, slot_total, inner)
    out_s = run(
        spatial_forward,
        frame_dev,
        [info, packed_qkv],
        [SCALARS, per_frame(packed_qkv)],
        out_s,
        per_frame(out_s),
        [frame_acc],
        4 * frame_dev * slot_total * slot_total * inner,
    )
    thin, wide, other = near_rows(out_spatial, qkv_temporal, out_temporal)
    rows_z = jnp.concatenate([thin, other, wide], axis=0)
    cut = thin.shape[0]
    stream_tied, _ = tie(stream, rows_z)
    stream_s = to_slots(stream_tied)
    grad_tied, _ = tie(grad_out, stream_s)
    grad_s = to_slots(grad_tied)
    out_s_tied, _ = tie(out_s, grad_s)
    out_s_s = to_slots(out_s_tied)

    stack = gather_z(coords, rows_z)
    thin = fold(unfold(stack[:, :cut]).reshape(-1, inner))
    other = fold(unfold(stack[:, cut : 2 * cut]).reshape(-1, inner))
    wide = stack[:, 2 * cut :].reshape(-1, width)
    rows_x = jnp.concatenate([thin, other, wide], axis=0)
    first = shift_both(rows_x, "x", 1)
    size = rows_x.shape[0] // 2
    onward = lax.dynamic_slice_in_dim(first, lax.axis_index("c") * size, size, 0)
    second = shift_both(onward, "x", 1)
    second_p, grad_s, out_s_s = tie(swap(second), grad_s, out_s_s)
    x_count = lax.axis_size("x")
    w_spatial, w_temporal, w_qkv = in_vmem(
        place_along_x,
        coords,
        [rows_x, first, swap(first), second, second_p],
        (shape_of(width, inner), shape_of(width, inner), shape_of(3 * inner, width)),
        [pltpu.VMEM((x_count,) + rows_x.shape, BF16)],
    )

    group_acc = pltpu.VMEM((rows, inner), F32)
    result = (
        shape_of(groups, rows, width),
        shape_of(groups, rows, width),
        shape_of(groups, rows, 3 * inner),
        shape_of(seq_count, groups, rows // seq_count, inner),
    )
    tokens = groups * rows
    mixed_s, modulated, qkv_t, out_t = run(
        functools.partial(temporal_forward, slots=slots),
        groups,
        [info, modulation, stream_s, out_s_s, w_spatial, w_qkv],
        [SCALARS, whole(modulation), per_group(stream_s), per_group(out_s_s), whole(w_spatial), whole(w_qkv)],
        result,
        [per_frame(result[0]), per_frame(result[1]), per_frame(result[2]), per_group(result[3])],
        [group_acc],
        8 * tokens * width * inner + 4 * tokens * rows * inner,
    )
    out_t_f = to_frames(out_t)

    wide_rows, pair_rows = term_rows(inner, width, y_count, x_count)
    result = (
        shape_of(seq_count, groups, rows // seq_count, width),
        shape_of(2, x_count * wide_rows + y_count * pair_rows, LANES),
    )
    total = pltpu.VMEM((inner, width), F32)
    ln_grad, terms = run(
        functools.partial(temporal_backward, slots=slots, y_count=y_count, x_count=x_count),
        groups,
        [info, modulation, grad_s, mixed_s, out_s_s, qkv_t, out_t, modulated, w_temporal, w_qkv],
        [
            SCALARS,
            whole(modulation),
            per_group(grad_s),
            per_frame(mixed_s),
            per_group(out_s_s),
            per_frame(qkv_t),
            per_group(out_t),
            per_frame(modulated),
            whole(w_temporal),
            whole(w_qkv),
        ],
        result,
        [per_group(result[0]), whole(result[1])],
        [group_acc, group_acc, group_acc, total, total, pltpu.VMEM((2, 3 * inner, width // 2), F32)],
        18 * tokens * width * inner + 10 * tokens * rows * inner,
    )
    terms, out_t_f = lax.optimization_barrier((terms, out_t_f))
    block_out = shape_of(frame_dev, slot_total, width)
    block_out = run(
        block_forward,
        frame_dev,
        [info, modulation, stream, out_s, out_t_f, w_spatial, w_temporal],
        [
            SCALARS,
            whole(modulation),
            per_frame(stream),
            per_frame(out_s),
            per_frame(out_t_f),
            whole(w_spatial),
            whole(w_temporal),
        ],
        block_out,
        per_frame(block_out),
        [],
        4 * tokens * width * inner,
    )
    reduced, block_out, pair_ready = reduce_start(coords, terms, inner, width, block_out)
    ln_grad, _ = tie(ln_grad, pair_ready)
    ln_frames = to_frames(ln_grad)

    result = (shape_of(frame_dev, slot_total, width), shape_of(frame_dev, slot_total, 3 * inner))
    hidden_grad, qkv_s_grad = run(
        spatial_backward,
        frame_dev,
        [info, grad_out, ln_frames, packed_qkv, out_s, w_spatial],
        [
            SCALARS,
            per_frame(grad_out),
            per_frame(ln_frames),
            per_frame(packed_qkv),
            per_frame(out_s),
            whole(w_spatial),
        ],
        result,
        [per_frame(result[0]), per_frame(result[1])],
        [frame_acc, frame_acc, frame_acc],
        2 * tokens * width * inner + 10 * tokens * slot_total * inner,
    )
    summed, qkv_s_grad = reduce_end(reduced, inner, width, qkv_s_grad)
    return (block_out[None], hidden_grad[None], qkv_s_grad[None], summed[0], summed[1], summed[2])


def solution(mesh):
    torus = Mesh(mesh.devices.reshape(4, 8, 4, 2), ("x", "z", "y", "c"))
    dp, seq = ("x", "z"), ("y", "c")
    tokens = P(dp, seq, None, None)
    weight = P(seq, dp)
    placed = (
        tokens,
        tokens,
        weight,
        weight,
        weight,
        P(dp, None, None),
        tokens,
        P(dp),
        P(dp),
        P(dp),
    )
    return jax.shard_map(
        on_device,
        mesh=torus,
        in_specs=placed,
        out_specs=(tokens, tokens, tokens, weight, weight, weight),
        check_vma=False,
    )
```

```python
import functools
import math

import jax
import jax.numpy as jnp
from jax import lax
from jax.experimental import pallas as pl
from jax.experimental.pallas import tpu as pltpu
from jax.sharding import Mesh
from jax.sharding import PartitionSpec as P

HEAD_DIM = 72
EPSILON = 1e-06
NEGATIVE = -1e30
LANES = 128
VMEM_BYTES = 56 * 1024 * 1024
F32 = jnp.float32
BF16 = jnp.bfloat16


def dot_nn(left, right):
    return lax.dot_general(left, right, (((1,), (0,)), ((), ())), preferred_element_type=F32)


def dot_nt(left, right):
    return lax.dot_general(left, right, (((1,), (1,)), ((), ())), preferred_element_type=F32)


def dot_tn(left, right):
    return lax.dot_general(left, right, (((0,), (0,)), ((), ())), preferred_element_type=F32)


def head_windows(inner):
    windows = []
    for head in range(inner // HEAD_DIM):
        low = head * HEAD_DIM
        start = low // LANES * LANES
        stop = min(-(-(low + HEAD_DIM) // LANES) * LANES, inner)
        windows.append((start, stop, low - start))
    return windows


def own_lanes(window):
    start, stop, offset = window
    lane = lax.broadcasted_iota(jnp.int32, (1, stop - start), 1)
    return (lane >= offset) & (lane < offset + HEAD_DIM)


def only(lanes, rows):
    return jnp.where(lanes, rows, jnp.zeros((), rows.dtype))


def softmax_rows(query, key, allowed):
    logits = dot_nt(query, key) * (1.0 / math.sqrt(HEAD_DIM))
    logits = jnp.where(allowed, logits, NEGATIVE)
    powers = jnp.exp(logits - jnp.max(logits, axis=1, keepdims=True))
    return powers * (1.0 / jnp.sum(powers, axis=1, keepdims=True))


def attend_heads(query, key, value, allowed, out_acc):
    out_acc[...] = jnp.zeros(out_acc.shape, F32)
    for window in head_windows(query.shape[1]):
        start, stop, _ = window
        lanes = own_lanes(window)
        probs = softmax_rows(query[:, start:stop], only(lanes, key[:, start:stop]), allowed)
        out_acc[:, start:stop] += dot_nn(probs.astype(BF16), only(lanes, value[:, start:stop]))


def attend_heads_back(query, key, value, out, out_grad, allowed, q_acc, k_acc, v_acc):
    factor = 1.0 / math.sqrt(HEAD_DIM)
    for acc in (q_acc, k_acc, v_acc):
        acc[...] = jnp.zeros(acc.shape, F32)
    for window in head_windows(query.shape[1]):
        start, stop, _ = window
        lanes = own_lanes(window)
        key_h = only(lanes, key[:, start:stop])
        grad_h = only(lanes, out_grad[:, start:stop])
        probs = softmax_rows(query[:, start:stop], key_h, allowed)
        prob_grad = dot_nt(grad_h, value[:, start:stop])
        row_delta = jnp.sum(
            grad_h.astype(F32) * out[:, start:stop].astype(F32), axis=1, keepdims=True
        )
        logit_grad = (probs * (prob_grad - row_delta)).astype(BF16)
        q_acc[:, start:stop] += dot_nn(logit_grad, key_h) * factor
        k_acc[:, start:stop] += dot_tn(logit_grad, only(lanes, query[:, start:stop])) * factor
        v_acc[:, start:stop] += dot_tn(probs.astype(BF16), grad_h)


def slot_masks(info_ref, rows, slots):
    frames, limit, first = info_ref[0], info_ref[1], info_ref[2]
    group = pl.program_id(0)
    row = lax.broadcasted_iota(jnp.int32, (rows, 1), 0)
    slot = first + group * slots + row % slots
    token = (row // slots < frames) & (slot < limit)
    col = lax.broadcasted_iota(jnp.int32, (1, rows), 1)
    allowed = (row % slots == col % slots) & (col // slots < frames)
    return token.astype(F32), allowed


def normalised(mixed):
    values = mixed.astype(F32)
    centred = values - jnp.mean(values, axis=1, keepdims=True)
    inv_std = lax.rsqrt(jnp.mean(centred * centred, axis=1, keepdims=True) + EPSILON)
    return centred * inv_std, inv_std


def temporal_forward(
    info, mod, stream, out_s, w_spatial, w_qkv, mixed_ref, mod_ref, qkv_ref, out_ref, acc, slots
):
    rows, inner = acc.shape
    width = stream.shape[-1]
    token, allowed = slot_masks(info, rows, slots)
    branch = dot_nt(out_s[...].reshape(rows, inner), w_spatial[...])
    mixed = (stream[...].reshape(rows, width).astype(F32) + token * branch).astype(BF16)
    mixed_ref[...] = mixed.reshape(mixed_ref.shape)
    normed, _ = normalised(mixed)
    modulated = (normed * (1.0 + mod[0, 1:2]) + mod[0, 0:1]).astype(BF16)
    mod_ref[...] = modulated.reshape(mod_ref.shape)
    qkv = dot_nt(modulated, w_qkv[...]).astype(BF16)
    qkv_ref[...] = qkv.reshape(qkv_ref.shape)
    attend_heads(
        qkv[:, :inner], qkv[:, inner : 2 * inner], qkv[:, 2 * inner :], allowed, acc
    )
    out_ref[...] = acc[...].astype(BF16).reshape(out_ref.shape)


def temporal_backward(
    info, mod, grad, mixed, out_s, qkv_ref, out_t, modulated, w_temporal, w_qkv, ln_ref, terms,
    q_acc, k_acc, v_acc, sum_s, sum_t, sum_q, slots, y_count, x_count,
):
    rows, inner = q_acc.shape
    width = grad.shape[-1]
    token, allowed = slot_masks(info, rows, slots)

    @pl.when(pl.program_id(0) == 0)
    def _():
        for total in (sum_s, sum_t, sum_q):
            total[...] = jnp.zeros(total.shape, F32)

    grad_f = grad[...].reshape(rows, width).astype(F32)
    branch_grad = (token * mod[0, 2:3] * grad_f).astype(BF16)
    out_grad = dot_nn(branch_grad, w_temporal[...]).astype(BF16)
    qkv = qkv_ref[...].reshape(rows, 3 * inner)
    out = out_t[...].reshape(rows, inner)
    attend_heads_back(
        qkv[:, :inner], qkv[:, inner : 2 * inner], qkv[:, 2 * inner :], out, out_grad, allowed,
        q_acc, k_acc, v_acc,
    )
    dqkv = jnp.concatenate([q_acc[...], k_acc[...], v_acc[...]], axis=1).astype(BF16)

    norm_grad = dot_nn(dqkv, w_qkv[...]) * (1.0 + mod[0, 1:2])
    normed, inv_std = normalised(mixed[...].reshape(rows, width))
    first = jnp.mean(norm_grad, axis=1, keepdims=True)
    second = jnp.mean(norm_grad * normed, axis=1, keepdims=True)
    ln_grad = (inv_std * (norm_grad - first - normed * second)).astype(BF16)
    ln_ref[...] = ln_grad.reshape(ln_ref.shape)
    hidden_grad = (grad_f + ln_grad.astype(F32)).astype(BF16)
    spatial_grad = (token * hidden_grad.astype(F32)).astype(BF16)

    sum_t[...] += dot_tn(out, branch_grad)
    sum_s[...] += dot_tn(out_s[...].reshape(rows, inner), spatial_grad)
    left = modulated[...].reshape(rows, width)
    step = width // (2 * y_count)
    for c in range(2):
        pieces = [left[:, (2 * y + c) * step : (2 * y + c + 1) * step] for y in range(y_count)]
        sum_q[c] += dot_tn(dqkv, jnp.concatenate(pieces, axis=1))

    @pl.when(pl.program_id(0) == pl.num_programs(0) - 1)
    def _():
        store_terms(sum_s, sum_t, sum_q, terms, y_count, x_count)


def term_rows(inner, width, y_count, x_count):
    tiles = -(-(width // 2) // LANES)
    return tiles * (3 * inner // x_count), width // LANES * (inner // y_count)


def store_terms(sum_s, sum_t, sum_q, terms, y_count, x_count):
    inner, width = sum_s.shape
    span, step = 3 * inner // x_count, inner // (2 * y_count)
    wide, pair = term_rows(inner, width, y_count, x_count)
    half = width // 2
    for c in range(2):
        for x in range(x_count):
            for tile in range(wide // span):
                low, high = tile * LANES, min((tile + 1) * LANES, half)
                block = sum_q[c, x * span : (x + 1) * span, low:high]
                if high - low < LANES:
                    rest = jnp.zeros((span, LANES - (high - low)), F32)
                    block = jnp.concatenate([block, rest], axis=1)
                start = x * wide + tile * span
                terms[c, start : start + span] = block.astype(BF16)
        for y in range(y_count):
            place = (2 * y + c) * step
            for tile in range(width // LANES):
                lanes = slice(tile * LANES, (tile + 1) * LANES)
                block = jnp.concatenate(
                    [sum_s[place : place + step, lanes], sum_t[place : place + step, lanes]],
                    axis=0,
                )
                start = x_count * wide + y * pair + tile * 2 * step
                terms[c, start : start + 2 * step] = block.astype(BF16)


def frame_keys(info_ref, rows):
    return lax.broadcasted_iota(jnp.int32, (1, rows), 1) < info_ref[1]


def frame_tokens(info_ref, rows):
    row = lax.broadcasted_iota(jnp.int32, (rows, 1), 0)
    alive = info_ref[3] + pl.program_id(0) < info_ref[0]
    return ((row < info_ref[1]) & alive).astype(F32)


def spatial_forward(info, qkv_ref, out_ref, acc):
    rows, inner = acc.shape
    qkv = qkv_ref[0]
    attend_heads(
        qkv[:, :inner], qkv[:, inner : 2 * inner], qkv[:, 2 * inner :], frame_keys(info, rows), acc
    )
    out_ref[0] = acc[...].astype(BF16)


def block_forward(info, mod, stream, out_s, out_t, w_spatial, w_temporal, block_ref):
    rows = stream.shape[1]
    token = frame_tokens(info, rows)
    spatial = dot_nt(out_s[0], w_spatial[...])
    mixed = (stream[0].astype(F32) + token * spatial).astype(BF16)
    branch = dot_nt(out_t[0], w_temporal[...])
    block_ref[0] = (mixed.astype(F32) + token * mod[0, 2:3] * branch).astype(BF16)


def spatial_backward(
    info, grad, ln_grad, qkv_ref, out_s, w_spatial, hidden_ref, dqkv_ref, q_acc, k_acc, v_acc
):
    rows, inner = q_acc.shape
    hidden_grad = (grad[0].astype(F32) + ln_grad[0].astype(F32)).astype(BF16)
    hidden_ref[0] = hidden_grad
    branch_grad = (frame_tokens(info, rows) * hidden_grad.astype(F32)).astype(BF16)
    out_grad = dot_nn(branch_grad, w_spatial[...]).astype(BF16)
    qkv = qkv_ref[0]
    attend_heads_back(
        qkv[:, :inner], qkv[:, inner : 2 * inner], qkv[:, 2 * inner :], out_s[0], out_grad,
        frame_keys(info, rows), q_acc, k_acc, v_acc,
    )
    dqkv_ref[0] = jnp.concatenate([q_acc[...], k_acc[...], v_acc[...]], axis=1).astype(BF16)


def whole(array):
    return pl.BlockSpec(
        array.shape, lambda step: (0,) * array.ndim, pipeline_mode=pl.Buffered(1)
    )


def per_frame(array):
    return pl.BlockSpec((1,) + array.shape[1:], lambda step: (step, 0, 0))


def per_group(array):
    return pl.BlockSpec(
        (array.shape[0], 1) + array.shape[2:], lambda step: (0, step, 0, 0)
    )


SCALARS = pl.BlockSpec(memory_space=pltpu.SMEM)


def run(body, steps, operands, specs, results, result_specs, scratch, flops):
    leaves = operands + jax.tree.leaves(results)
    moved = sum(math.prod(a.shape) * a.dtype.itemsize for a in leaves)
    return pl.pallas_call(
        body,
        grid=(steps,),
        in_specs=specs,
        out_specs=result_specs,
        out_shape=results,
        scratch_shapes=scratch,
        compiler_params=pltpu.CompilerParams(vmem_limit_bytes=VMEM_BYTES),
        cost_estimate=pl.CostEstimate(flops=flops, bytes_accessed=moved, transcendentals=0),
    )(*operands)


def shape_of(*dims, dtype=BF16):
    return jax.ShapeDtypeStruct(dims, dtype)


def exchange(rows, axes):
    return lax.all_to_all(rows, axes, 0, 0, tiled=True)


def shift(rows, axis, hops):
    count = lax.axis_size(axis)
    return lax.ppermute(rows, axis, [(at, (at + hops) % count) for at in range(count)])


def shift_both(rows, axis, hops):
    count = lax.axis_size(axis)
    pairs = []
    for at in range(count):
        pairs.append((2 * at, 2 * ((at - hops) % count)))
        pairs.append((2 * at + 1, 2 * ((at + hops) % count) + 1))
    return lax.ppermute(rows, (axis, "c"), pairs)


def swap(rows):
    return shift(rows, "c", 1)


def place_along_z(info, own, near, mid, far, last, near_p, mid_p, far_p, out):
    place, count = info[1], out.shape[0]
    sign = 1 - 2 * info[3]
    out[place] = own[...]
    out[lax.rem(place + count // 2, count)] = last[...]
    for hops, mine, other in ((1, near, near_p), (2, mid, mid_p), (3, far, far_p)):
        out[lax.rem(place + sign * hops + count, count)] = mine[...]
        out[lax.rem(place - sign * hops + count, count)] = other[...]


def place_along_x(info, own, near, near_p, part, part_p, spatial, temporal, wide, out):
    place, count = info[0], out.shape[0]
    sign = 1 - 2 * info[3]
    half = part.shape[0]
    opposite = lax.rem(place + count // 2, count)
    out[place] = own[...]
    out[lax.rem(place + sign + count, count)] = near[...]
    out[lax.rem(place - sign + count, count)] = near_p[...]

    @pl.when(info[3] == 0)
    def _():
        out[opposite, :half] = part[...]
        out[opposite, half:] = part_p[...]

    @pl.when(info[3] != 0)
    def _():
        out[opposite, :half] = part_p[...]
        out[opposite, half:] = part[...]

    cut, inner = out.shape[2] // count // 2, out.shape[2] // 2
    span = wide.shape[0] // count
    for x in range(count):
        for number, result in ((0, spatial), (1, temporal)):
            block = out[x, number * cut : (number + 1) * cut]
            result[2 * x * cut : (2 * x + 1) * cut] = block[:, :inner]
            result[(2 * x + 1) * cut : (2 * x + 2) * cut] = block[:, inner:]
        wide[x * span : (x + 1) * span] = out[x, 2 * cut :]


def in_vmem(body, info, blocks, results, scratch=()):
    vmem = pl.BlockSpec(memory_space=pltpu.VMEM)
    return pl.pallas_call(
        body,
        in_specs=[SCALARS] + [vmem] * len(blocks),
        out_specs=jax.tree.map(lambda _: vmem, results),
        out_shape=results,
        scratch_shapes=list(scratch),
        compiler_params=pltpu.CompilerParams(vmem_limit_bytes=VMEM_BYTES),
    )(info, *blocks)


def tie(*values):
    return lax.optimization_barrier(values)


def near_rows(out_spatial, qkv_temporal, out_temporal):
    half, narrow = out_spatial.shape
    packed = jnp.concatenate(
        [jnp.concatenate([out_spatial.T, out_temporal.T], axis=1), qkv_temporal.T], axis=0
    )
    near = jnp.transpose(lax.all_gather(packed, ("y", "c"), axis=0, tiled=False), (1, 0, 2))
    thin = near[:narrow, :, :half].reshape(narrow, -1)
    other = near[:narrow, :, half:].reshape(narrow, -1)
    wide = near[narrow:].reshape(near.shape[0] - narrow, -1)
    return (fold(thin), wide, fold(other))


def fold(rows):
    cut = rows.shape[-2] // 2
    return jnp.concatenate([rows[..., :cut, :], rows[..., cut:, :]], axis=-1)


def unfold(rows):
    cut = rows.shape[-1] // 2
    return jnp.concatenate([rows[..., :cut], rows[..., cut:]], axis=-2)


def gather_z(coords, rows, beside):
    arrived = [shift_both(rows, "z", hops) for hops in (1, 2, 3)] + [shift(rows, "z", 4)]
    arrived, beside = tie(arrived, beside)
    swapped = [swap(block) for block in arrived[:3]]
    result = shape_of(lax.axis_size("z"), *rows.shape)
    return in_vmem(place_along_z, coords, [rows] + arrived + swapped, result), beside


def scatter(blocks, axis):
    count, place = lax.axis_size(axis), lax.axis_index(axis)
    arrived = []
    for hops in range(1, count):
        block = lax.dynamic_index_in_dim(blocks, (place + hops) % count, 0, keepdims=False)
        arrived.append(shift(block, axis, hops))
    return arrived


def sum_with_own(blocks, arrived, axis):
    place = lax.axis_index(axis)
    total = lax.dynamic_index_in_dim(blocks, place, 0, keepdims=False).astype(F32)
    for block in arrived:
        total = total + block.astype(F32)
    return total.astype(BF16)


def regroup_wide(info, blocks, first, second, third, out):
    y_count, span, lanes = out.shape
    total = blocks[info[0]].astype(F32)
    for block in (first, second, third):
        total = total + block[...].astype(F32)
    tiles = [total[at : at + span] for at in range(0, total.shape[0], span)]
    flat = jnp.concatenate(tiles, axis=1)
    step = (flat.shape[1] - LANES // 2) // y_count
    for y in range(y_count):
        block = flat[:, y * step : (y + 1) * step]
        rest = jnp.zeros((span, lanes - step), F32)
        out[y] = jnp.concatenate([block, rest], axis=1).astype(BF16)


def regroup_pair(info, blocks, out):
    x_count, span, lanes = out.shape
    total = blocks[0].astype(F32)
    for y in range(1, blocks.shape[0]):
        total = total + blocks[y].astype(F32)
    width = x_count * span
    step = total.shape[0] // (width // LANES)
    tiles = [total[at : at + step].T for at in range(0, total.shape[0], step)]
    flat = jnp.concatenate(tiles, axis=0)
    flat = jnp.concatenate([flat, jnp.zeros((width, lanes - step), F32)], axis=1)
    for x in range(x_count):
        out[x] = flat[x * span : (x + 1) * span].astype(BF16)


def reduce_start(coords, terms, inner, width, beside):
    x_count, y_count = lax.axis_size("x"), lax.axis_size("y")
    wide_rows, pair_rows = term_rows(inner, width, y_count, x_count)
    halves = exchange(terms, "c")
    total = (halves[0].astype(F32) + halves[1].astype(F32)).astype(BF16)
    wide = total[: x_count * wide_rows].reshape(x_count, wide_rows, LANES)
    pair = total[x_count * wide_rows :].reshape(y_count, pair_rows, LANES)

    arrived = scatter(wide, "x")
    pair = exchange(pair, "y")
    arrived[2], beside = tie(arrived[2], beside)
    wide = in_vmem(
        regroup_wide,
        coords,
        [wide] + arrived,
        shape_of(y_count, 3 * inner // x_count, 2 * LANES),
    )
    blocks = in_vmem(
        regroup_pair, coords, [pair], shape_of(x_count, width // x_count, 2 * LANES)
    )
    return (wide, blocks), beside, pair


def reduce_end(reduced, inner, width, beside):
    wide, pair = reduced
    z_count = lax.axis_size("z")
    step = width // (2 * lax.axis_size("y"))
    wide_in, pair_in, beside = tie(scatter(wide, "y"), scatter(pair, "x"), beside)
    wide = sum_with_own(wide, wide_in, "y").reshape(z_count, -1, 2 * LANES)
    pair = sum_with_own(pair, pair_in, "x").reshape(z_count, -1, 2 * LANES)
    total = jnp.sum(exchange(jnp.concatenate([pair, wide], axis=1), "z").astype(F32), axis=0)
    narrow = pair.shape[1]
    half = step // 2
    summed = (total[:narrow, :half].T, total[narrow:, :step].T, total[:narrow, half:step].T)
    return summed, beside


def on_device(
    hidden,
    spatial_qkv,
    out_spatial,
    qkv_temporal,
    out_temporal,
    modulation,
    cotangent,
    frame_count,
    patch_height,
    patch_width,
):
    seq_count = lax.axis_size(("y", "c"))
    seq_place = lax.axis_index(("y", "c"))
    y_count = lax.axis_size("y")
    stream = hidden[0]
    grad_out = cotangent[0]
    packed_qkv = spatial_qkv[0]
    frame_dev, slot_total, width = stream.shape
    slot_dev = slot_total // seq_count
    inner = out_spatial.shape[0] * seq_count
    slots = 8
    groups = slot_dev // slots
    rows = frame_dev * seq_count * slots
    coords = jnp.stack([lax.axis_index(name) for name in ("x", "z", "y", "c")]).astype(jnp.int32)
    info = jnp.stack(
        [
            frame_count[0],
            patch_height[0] * patch_width[0],
            seq_place * slot_dev,
            seq_place * frame_dev,
        ]
    ).astype(jnp.int32)

    def to_slots(tokens):
        split = tokens.reshape(frame_dev, seq_count, groups, slots, -1)
        split = jnp.transpose(split, (1, 2, 0, 3, 4))
        return exchange(split.reshape(seq_count, groups, frame_dev * slots, -1), ("y", "c"))

    def to_frames(tokens):
        moved = exchange(tokens, ("y", "c")).reshape(seq_count, groups, frame_dev, slots, -1)
        return jnp.transpose(moved, (2, 0, 1, 3, 4)).reshape(frame_dev, slot_total, -1)

    frame_acc = pltpu.VMEM((slot_total, inner), F32)
    out_s = shape_of(frame_dev, slot_total, inner)
    out_s = run(
        spatial_forward,
        frame_dev,
        [info, packed_qkv],
        [SCALARS, per_frame(packed_qkv)],
        out_s,
        per_frame(out_s),
        [frame_acc],
        4 * frame_dev * slot_total * slot_total * inner,
    )
    thin, wide, other = near_rows(out_spatial, qkv_temporal, out_temporal)
    rows_z = jnp.concatenate([thin, other, wide], axis=0)
    cut = thin.shape[0]
    stream_tied, _ = tie(stream, rows_z)
    stream_s = to_slots(stream_tied)
    stack, (stream_s, out_s) = gather_z(coords, rows_z, (stream_s, out_s))
    out_s_s = to_slots(out_s)
    grad_tied, _ = tie(grad_out, out_s_s)
    grad_s = to_slots(grad_tied)

    thin = fold(unfold(stack[:, :cut]).reshape(-1, inner))
    other = fold(unfold(stack[:, cut : 2 * cut]).reshape(-1, inner))
    wide = stack[:, 2 * cut :].reshape(-1, width)
    rows_x = jnp.concatenate([thin, other, wide], axis=0)
    first, out_s_s = tie(shift_both(rows_x, "x", 1), out_s_s)
    size = rows_x.shape[0] // 2
    onward = lax.dynamic_slice_in_dim(first, lax.axis_index("c") * size, size, 0)
    second = shift_both(onward, "x", 1)
    second_p = swap(second)
    x_count = lax.axis_size("x")
    w_spatial, w_temporal, w_qkv = in_vmem(
        place_along_x,
        coords,
        [rows_x, first, swap(first), second, second_p],
        (shape_of(width, inner), shape_of(width, inner), shape_of(3 * inner, width)),
        [pltpu.VMEM((x_count,) + rows_x.shape, BF16)],
    )

    group_acc = pltpu.VMEM((rows, inner), F32)
    result = (
        shape_of(groups, rows, width),
        shape_of(groups, rows, width),
        shape_of(groups, rows, 3 * inner),
        shape_of(seq_count, groups, rows // seq_count, inner),
    )
    tokens = groups * rows
    mixed_s, modulated, qkv_t, out_t = run(
        functools.partial(temporal_forward, slots=slots),
        groups,
        [info, modulation, stream_s, out_s_s, w_spatial, w_qkv],
        [SCALARS, whole(modulation), per_group(stream_s), per_group(out_s_s), whole(w_spatial), whole(w_qkv)],
        result,
        [per_frame(result[0]), per_frame(result[1]), per_frame(result[2]), per_group(result[3])],
        [group_acc],
        8 * tokens * width * inner + 4 * tokens * rows * inner,
    )
    out_t_tied, _ = tie(out_t, grad_s)
    out_t_f = to_frames(out_t_tied)

    wide_rows, pair_rows = term_rows(inner, width, y_count, x_count)
    result = (
        shape_of(seq_count, groups, rows // seq_count, width),
        shape_of(2, x_count * wide_rows + y_count * pair_rows, LANES),
    )
    total = pltpu.VMEM((inner, width), F32)
    ln_grad, terms = run(
        functools.partial(temporal_backward, slots=slots, y_count=y_count, x_count=x_count),
        groups,
        [info, modulation, grad_s, mixed_s, out_s_s, qkv_t, out_t, modulated, w_temporal, w_qkv],
        [
            SCALARS,
            whole(modulation),
            per_group(grad_s),
            per_frame(mixed_s),
            per_group(out_s_s),
            per_frame(qkv_t),
            per_group(out_t),
            per_frame(modulated),
            whole(w_temporal),
            whole(w_qkv),
        ],
        result,
        [per_group(result[0]), whole(result[1])],
        [group_acc, group_acc, group_acc, total, total, pltpu.VMEM((2, 3 * inner, width // 2), F32)],
        18 * tokens * width * inner + 10 * tokens * rows * inner,
    )
    terms, out_t_f = lax.optimization_barrier((terms, out_t_f))
    block_out = shape_of(frame_dev, slot_total, width)
    block_out = run(
        block_forward,
        frame_dev,
        [info, modulation, stream, out_s, out_t_f, w_spatial, w_temporal],
        [
            SCALARS,
            whole(modulation),
            per_frame(stream),
            per_frame(out_s),
            per_frame(out_t_f),
            whole(w_spatial),
            whole(w_temporal),
        ],
        block_out,
        per_frame(block_out),
        [],
        4 * tokens * width * inner,
    )
    reduced, block_out, pair_ready = reduce_start(coords, terms, inner, width, block_out)
    ln_grad, _ = tie(ln_grad, pair_ready)
    ln_frames = to_frames(ln_grad)

    result = (shape_of(frame_dev, slot_total, width), shape_of(frame_dev, slot_total, 3 * inner))
    hidden_grad, qkv_s_grad = run(
        spatial_backward,
        frame_dev,
        [info, grad_out, ln_frames, packed_qkv, out_s, w_spatial],
        [
            SCALARS,
            per_frame(grad_out),
            per_frame(ln_frames),
            per_frame(packed_qkv),
            per_frame(out_s),
            whole(w_spatial),
        ],
        result,
        [per_frame(result[0]), per_frame(result[1])],
        [frame_acc, frame_acc, frame_acc],
        2 * tokens * width * inner + 10 * tokens * slot_total * inner,
    )
    summed, qkv_s_grad = reduce_end(reduced, inner, width, qkv_s_grad)
    return (block_out[None], hidden_grad[None], qkv_s_grad[None], summed[0], summed[1], summed[2])


def solution(mesh):
    torus = Mesh(mesh.devices.reshape(4, 8, 4, 2), ("x", "z", "y", "c"))
    dp, seq = ("x", "z"), ("y", "c")
    tokens = P(dp, seq, None, None)
    weight = P(seq, dp)
    placed = (
        tokens,
        tokens,
        weight,
        weight,
        weight,
        P(dp, None, None),
        tokens,
        P(dp),
        P(dp),
        P(dp),
    )
    return jax.shard_map(
        on_device,
        mesh=torus,
        in_specs=placed,
        out_specs=(tokens, tokens, tokens, weight, weight, weight),
        check_vma=False,
    )
```

```python
import functools
import math

import jax
import jax.numpy as jnp
from jax import lax
from jax.experimental import pallas as pl
from jax.experimental.pallas import tpu as pltpu
from jax.sharding import Mesh
from jax.sharding import PartitionSpec as P

HEAD_DIM = 72
EPSILON = 1e-06
NEGATIVE = -1e30
LANES = 128
VMEM_BYTES = 56 * 1024 * 1024
F32 = jnp.float32
BF16 = jnp.bfloat16


def dot_nn(left, right):
    return lax.dot_general(left, right, (((1,), (0,)), ((), ())), preferred_element_type=F32)


def dot_nt(left, right):
    return lax.dot_general(left, right, (((1,), (1,)), ((), ())), preferred_element_type=F32)


def dot_tn(left, right):
    return lax.dot_general(left, right, (((0,), (0,)), ((), ())), preferred_element_type=F32)


def head_windows(inner):
    windows = []
    for head in range(inner // HEAD_DIM):
        low = head * HEAD_DIM
        start = low // LANES * LANES
        stop = min(-(-(low + HEAD_DIM) // LANES) * LANES, inner)
        windows.append((start, stop, low - start))
    return windows


def own_lanes(window):
    start, stop, offset = window
    lane = lax.broadcasted_iota(jnp.int32, (1, stop - start), 1)
    return (lane >= offset) & (lane < offset + HEAD_DIM)


def only(lanes, rows):
    return jnp.where(lanes, rows, jnp.zeros((), rows.dtype))


def lane_tiles(inner):
    return [(low, min(low + LANES, inner)) for low in range(0, inner, LANES)]


def combine(inner, factors, rows):
    pieces = []
    for low, high in lane_tiles(inner):
        lane = low + lax.broadcasted_iota(jnp.int32, (1, high - low), 1)
        total = None
        for head, factor in enumerate(factors):
            start, stop = head * HEAD_DIM, (head + 1) * HEAD_DIM
            if stop <= low or start >= high:
                continue
            own = only((lane >= start) & (lane < stop), rows[:, low:high])
            part = lax.dot_general(
                factor[0], own, (((factor[1],), (0,)), ((), ())), preferred_element_type=F32
            )
            total = part if total is None else total + part
        pieces.append(total)
    return jnp.concatenate(pieces, axis=1)


def head_logits(query, key, allowed):
    logits = []
    for window in head_windows(query.shape[1]):
        start, stop, _ = window
        own = only(own_lanes(window), key[:, start:stop])
        logits.append(dot_nt(query[:, start:stop], own))
    return logits


def softmax_rows(logits, allowed):
    logits = jnp.where(allowed, logits * (1.0 / math.sqrt(HEAD_DIM)), NEGATIVE)
    powers = jnp.exp(logits - jnp.max(logits, axis=1, keepdims=True))
    return powers * (1.0 / jnp.sum(powers, axis=1, keepdims=True))


def attend_heads(query, key, value, allowed):
    logits = head_logits(query, key, allowed)
    probs = [softmax_rows(one, allowed).astype(BF16) for one in logits]
    return combine(query.shape[1], [(one, 1) for one in probs], value)


def attend_heads_back(query, key, value, out, out_grad, allowed):
    inner = query.shape[1]
    factor = 1.0 / math.sqrt(HEAD_DIM)
    logits = head_logits(query, key, allowed)
    slopes, deltas = [], []
    for window in head_windows(inner):
        start, stop, _ = window
        own = only(own_lanes(window), out_grad[:, start:stop])
        slopes.append(dot_nt(own, value[:, start:stop]))
        product = own.astype(F32) * out[:, start:stop].astype(F32)
        deltas.append(jnp.sum(product, axis=1, keepdims=True))
    halves, grads = [], []
    for one, slope, delta in zip(logits, slopes, deltas):
        probs = softmax_rows(one, allowed)
        halves.append(probs.astype(BF16))
        grads.append((probs * (slope - delta)).astype(BF16))
    q_grad = combine(inner, [(one, 1) for one in grads], key) * factor
    k_grad = combine(inner, [(one, 0) for one in grads], query) * factor
    v_grad = combine(inner, [(one, 0) for one in halves], out_grad)
    return jnp.concatenate(
        [q_grad.astype(BF16), k_grad.astype(BF16), v_grad.astype(BF16)], axis=1
    )


def slot_masks(info_ref, rows, slots):
    frames, limit, first = info_ref[0], info_ref[1], info_ref[2]
    group = pl.program_id(0)
    row = lax.broadcasted_iota(jnp.int32, (rows, 1), 0)
    slot = first + group * slots + row % slots
    token = (row // slots < frames) & (slot < limit)
    col = lax.broadcasted_iota(jnp.int32, (1, rows), 1)
    allowed = (row % slots == col % slots) & (col // slots < frames)
    return token.astype(F32), allowed


def normalised(mixed):
    values = mixed.astype(F32)
    centred = values - jnp.mean(values, axis=1, keepdims=True)
    inv_std = lax.rsqrt(jnp.mean(centred * centred, axis=1, keepdims=True) + EPSILON)
    return centred * inv_std, inv_std


def temporal_forward(
    info, mod, stream, out_s, w_spatial, w_qkv, mixed_ref, mod_ref, qkv_ref, out_ref, slots
):
    rows, width = mod_ref.shape[1:]
    inner = out_s.shape[-1]
    token, allowed = slot_masks(info, rows, slots)
    branch = dot_nt(out_s[...].reshape(rows, inner), w_spatial[...])
    mixed = (stream[...].reshape(rows, width).astype(F32) + token * branch).astype(BF16)
    mixed_ref[...] = mixed.reshape(mixed_ref.shape)
    normed, _ = normalised(mixed)
    modulated = (normed * (1.0 + mod[0, 1:2]) + mod[0, 0:1]).astype(BF16)
    mod_ref[...] = modulated.reshape(mod_ref.shape)
    qkv = dot_nt(modulated, w_qkv[...]).astype(BF16)
    qkv_ref[...] = qkv.reshape(qkv_ref.shape)
    out = attend_heads(qkv[:, :inner], qkv[:, inner : 2 * inner], qkv[:, 2 * inner :], allowed)
    out_ref[...] = out.astype(BF16).reshape(out_ref.shape)


def temporal_backward(
    info, mod, grad, mixed, out_s, qkv_ref, out_t, modulated, w_temporal, w_qkv, ln_ref, terms,
    sum_s, sum_t, sum_q, slots, y_count, x_count,
):
    rows, width = modulated.shape[1:]
    inner = out_s.shape[-1]
    token, allowed = slot_masks(info, rows, slots)

    @pl.when(pl.program_id(0) == 0)
    def _():
        for total in (sum_s, sum_t, sum_q):
            total[...] = jnp.zeros(total.shape, F32)

    grad_f = grad[...].reshape(rows, width).astype(F32)
    branch_grad = (token * mod[0, 2:3] * grad_f).astype(BF16)
    out_grad = dot_nn(branch_grad, w_temporal[...]).astype(BF16)
    qkv = qkv_ref[...].reshape(rows, 3 * inner)
    out = out_t[...].reshape(rows, inner)
    dqkv = attend_heads_back(
        qkv[:, :inner], qkv[:, inner : 2 * inner], qkv[:, 2 * inner :], out, out_grad, allowed
    )

    norm_grad = dot_nn(dqkv, w_qkv[...]) * (1.0 + mod[0, 1:2])
    normed, inv_std = normalised(mixed[...].reshape(rows, width))
    first = jnp.mean(norm_grad, axis=1, keepdims=True)
    second = jnp.mean(norm_grad * normed, axis=1, keepdims=True)
    ln_grad = (inv_std * (norm_grad - first - normed * second)).astype(BF16)
    ln_ref[...] = ln_grad.reshape(ln_ref.shape)
    hidden_grad = (grad_f + ln_grad.astype(F32)).astype(BF16)
    spatial_grad = (token * hidden_grad.astype(F32)).astype(BF16)

    sum_t[...] += dot_tn(out, branch_grad)
    sum_s[...] += dot_tn(out_s[...].reshape(rows, inner), spatial_grad)
    left = modulated[...].reshape(rows, width)
    step = width // (2 * y_count)
    for c in range(2):
        pieces = [left[:, (2 * y + c) * step : (2 * y + c + 1) * step] for y in range(y_count)]
        sum_q[c] += dot_tn(dqkv, jnp.concatenate(pieces, axis=1))

    @pl.when(pl.program_id(0) == pl.num_programs(0) - 1)
    def _():
        store_terms(sum_s, sum_t, sum_q, terms, y_count, x_count)


def term_rows(inner, width, y_count, x_count):
    tiles = -(-(width // 2) // LANES)
    return tiles * (3 * inner // x_count), width // LANES * (inner // y_count)


def store_terms(sum_s, sum_t, sum_q, terms, y_count, x_count):
    inner, width = sum_s.shape
    span, step = 3 * inner // x_count, inner // (2 * y_count)
    wide, pair = term_rows(inner, width, y_count, x_count)
    half = width // 2
    for c in range(2):
        for x in range(x_count):
            for tile in range(wide // span):
                low, high = tile * LANES, min((tile + 1) * LANES, half)
                block = sum_q[c, x * span : (x + 1) * span, low:high]
                if high - low < LANES:
                    rest = jnp.zeros((span, LANES - (high - low)), F32)
                    block = jnp.concatenate([block, rest], axis=1)
                start = x * wide + tile * span
                terms[c, start : start + span] = block.astype(BF16)
        for y in range(y_count):
            place = (2 * y + c) * step
            for tile in range(width // LANES):
                lanes = slice(tile * LANES, (tile + 1) * LANES)
                block = jnp.concatenate(
                    [sum_s[place : place + step, lanes], sum_t[place : place + step, lanes]],
                    axis=0,
                )
                start = x_count * wide + y * pair + tile * 2 * step
                terms[c, start : start + 2 * step] = block.astype(BF16)


def frame_keys(info_ref, rows):
    return lax.broadcasted_iota(jnp.int32, (1, rows), 1) < info_ref[1]


def frame_tokens(info_ref, rows):
    row = lax.broadcasted_iota(jnp.int32, (rows, 1), 0)
    alive = info_ref[3] + pl.program_id(0) < info_ref[0]
    return ((row < info_ref[1]) & alive).astype(F32)


def spatial_forward(info, qkv_ref, out_ref):
    rows, inner = out_ref.shape[1:]
    qkv = qkv_ref[0]
    out = attend_heads(
        qkv[:, :inner], qkv[:, inner : 2 * inner], qkv[:, 2 * inner :], frame_keys(info, rows)
    )
    out_ref[0] = out.astype(BF16)


def block_forward(info, mod, stream, out_s, out_t, w_spatial, w_temporal, block_ref):
    rows = stream.shape[1]
    token = frame_tokens(info, rows)
    spatial = dot_nt(out_s[0], w_spatial[...])
    mixed = (stream[0].astype(F32) + token * spatial).astype(BF16)
    branch = dot_nt(out_t[0], w_temporal[...])
    block_ref[0] = (mixed.astype(F32) + token * mod[0, 2:3] * branch).astype(BF16)


def spatial_backward(
    info, grad, ln_grad, qkv_ref, out_s, w_spatial, hidden_ref, dqkv_ref
):
    rows, inner = out_s.shape[1:]
    hidden_grad = (grad[0].astype(F32) + ln_grad[0].astype(F32)).astype(BF16)
    hidden_ref[0] = hidden_grad
    branch_grad = (frame_tokens(info, rows) * hidden_grad.astype(F32)).astype(BF16)
    out_grad = dot_nn(branch_grad, w_spatial[...]).astype(BF16)
    qkv = qkv_ref[0]
    dqkv_ref[0] = attend_heads_back(
        qkv[:, :inner], qkv[:, inner : 2 * inner], qkv[:, 2 * inner :], out_s[0], out_grad,
        frame_keys(info, rows),
    )


def whole(array):
    return pl.BlockSpec(
        array.shape, lambda step: (0,) * array.ndim, pipeline_mode=pl.Buffered(1)
    )


def per_frame(array):
    return pl.BlockSpec((1,) + array.shape[1:], lambda step: (step, 0, 0))


def per_group(array):
    return pl.BlockSpec(
        (array.shape[0], 1) + array.shape[2:], lambda step: (0, step, 0, 0)
    )


SCALARS = pl.BlockSpec(memory_space=pltpu.SMEM)


def run(body, steps, operands, specs, results, result_specs, scratch):
    return pl.pallas_call(
        body,
        grid=(steps,),
        in_specs=specs,
        out_specs=result_specs,
        out_shape=results,
        scratch_shapes=scratch,
        compiler_params=pltpu.CompilerParams(vmem_limit_bytes=VMEM_BYTES),
        cost_estimate=pl.CostEstimate(flops=1, bytes_accessed=1, transcendentals=0),
    )(*operands)


def shape_of(*dims, dtype=BF16):
    return jax.ShapeDtypeStruct(dims, dtype)


def exchange(rows, axes):
    return lax.all_to_all(rows, axes, 0, 0, tiled=True)


def shift(rows, axis, hops):
    count = lax.axis_size(axis)
    return lax.ppermute(rows, axis, [(at, (at + hops) % count) for at in range(count)])


def shift_both(rows, axis, hops):
    count = lax.axis_size(axis)
    pairs = []
    for at in range(count):
        pairs.append((2 * at, 2 * ((at - hops) % count)))
        pairs.append((2 * at + 1, 2 * ((at + hops) % count) + 1))
    return lax.ppermute(rows, (axis, "c"), pairs)


def swap(rows):
    return shift(rows, "c", 1)


def place_along_z(
    info, own, near, mid, far, last, near_p, mid_p, far_p, onward, kept, stack, flat, cut
):
    place, count = info[1], stack.shape[0]
    sign = 1 - 2 * info[3]
    stack[place] = own[...]
    stack[lax.rem(place + count // 2, count)] = last[...]
    for hops, mine, other in ((1, near, near_p), (2, mid, mid_p), (3, far, far_p)):
        stack[lax.rem(place + sign * hops + count, count)] = mine[...]
        stack[lax.rem(place - sign * hops + count, count)] = other[...]

    inner = flat.shape[1] // 2
    step = stack.shape[1] - 2 * cut
    for z in range(count):
        block = stack[z].astype(F32)
        side = 2 * z // count
        for number in range(2):
            for part in range(2):
                row = (2 * number * count + 4 * (z % (count // 2)) + 2 * part) * cut // 2
                flat[row : row + cut, side * inner : (side + 1) * inner] = block[
                    number * cut : (number + 1) * cut, part * inner : (part + 1) * inner
                ]
        row = 2 * count * cut + z * step
        flat[row : row + step] = block[2 * cut :]
    size = flat.shape[0] // 2
    lower, upper = flat[:size].astype(BF16), flat[size:].astype(BF16)

    @pl.when(info[3] == 0)
    def _():
        onward[...] = lower
        kept[...] = upper

    @pl.when(info[3] != 0)
    def _():
        onward[...] = upper
        kept[...] = lower


def place_along_x(
    info, own, own_k, near, near_k, near_p, near_pk, part, part_p, spatial, temporal, wide, out
):
    place, count = info[0], out.shape[0]
    half = part.shape[0]
    opposite = lax.rem(place + count // 2, count)

    def fill(index, first, second):
        out[index, :half] = first[...]
        out[index, half:] = second[...]

    @pl.when(info[3] == 0)
    def _():
        fill(place, own, own_k)
        fill(lax.rem(place + 1, count), near, near_k)
        fill(lax.rem(place - 1 + count, count), near_pk, near_p)
        fill(opposite, part, part_p)

    @pl.when(info[3] != 0)
    def _():
        fill(place, own_k, own)
        fill(lax.rem(place - 1 + count, count), near_k, near)
        fill(lax.rem(place + 1, count), near_p, near_pk)
        fill(opposite, part_p, part)

    cut, inner = out.shape[2] // count // 2, out.shape[2] // 2
    span = wide.shape[0] // count
    for x in range(count):
        for number, result in ((0, spatial), (1, temporal)):
            block = out[x, number * cut : (number + 1) * cut]
            result[2 * x * cut : (2 * x + 1) * cut] = block[:, :inner]
            result[(2 * x + 1) * cut : (2 * x + 2) * cut] = block[:, inner:]
        wide[x * span : (x + 1) * span] = out[x, 2 * cut :]


def in_vmem(body, info, blocks, results, scratch=()):
    vmem = pl.BlockSpec(memory_space=pltpu.VMEM)
    return pl.pallas_call(
        body,
        in_specs=[SCALARS] + [vmem] * len(blocks),
        out_specs=jax.tree.map(lambda _: vmem, results),
        out_shape=results,
        scratch_shapes=list(scratch),
        cost_estimate=pl.CostEstimate(flops=1, bytes_accessed=1, transcendentals=0),
        compiler_params=pltpu.CompilerParams(vmem_limit_bytes=VMEM_BYTES),
    )(info, *blocks)


def tie(*values):
    return lax.optimization_barrier(values)


def near_rows(out_spatial, qkv_temporal, out_temporal):
    half, narrow = out_spatial.shape
    packed = jnp.concatenate(
        [jnp.concatenate([out_spatial.T, out_temporal.T], axis=1), qkv_temporal.T], axis=0
    )
    near = jnp.transpose(lax.all_gather(packed, ("y", "c"), axis=0, tiled=False), (1, 0, 2))
    thin = near[:narrow, :, :half].reshape(narrow, -1)
    other = near[:narrow, :, half:].reshape(narrow, -1)
    wide = near[narrow:].reshape(near.shape[0] - narrow, -1)
    return (fold(thin), wide, fold(other))


def fold(rows):
    cut = rows.shape[-2] // 2
    return jnp.concatenate([rows[..., :cut, :], rows[..., cut:, :]], axis=-1)


def unfold(rows):
    cut = rows.shape[-1] // 2
    return jnp.concatenate([rows[..., :cut], rows[..., cut:]], axis=-2)


def gather_z(coords, rows, cut, beside):
    arrived = [shift_both(rows, "z", hops) for hops in (1, 2, 3)] + [shift(rows, "z", 4)]
    arrived, beside = tie(arrived, beside)
    swapped = [swap(block) for block in arrived[:3]]
    count, width = lax.axis_size("z"), rows.shape[1]
    half = shape_of(count * rows.shape[0] // 2, width)
    halves = in_vmem(
        functools.partial(place_along_z, cut=cut),
        coords,
        [rows] + arrived + swapped,
        (half, half),
        [pltpu.VMEM((count,) + rows.shape, BF16), pltpu.VMEM((2 * half.shape[0], width), F32)],
    )
    return halves, beside


def scatter(blocks, axis):
    count, place = lax.axis_size(axis), lax.axis_index(axis)
    arrived = []
    for hops in range(1, count):
        block = lax.dynamic_index_in_dim(blocks, (place + hops) % count, 0, keepdims=False)
        arrived.append(shift(block, axis, hops))
    return arrived


def sum_with_own(blocks, arrived, axis):
    place = lax.axis_index(axis)
    total = lax.dynamic_index_in_dim(blocks, place, 0, keepdims=False).astype(F32)
    for block in arrived:
        total = total + block.astype(F32)
    return total.astype(BF16)


def regroup_wide(info, blocks, first, second, third, out):
    y_count, span, lanes = out.shape
    total = blocks[info[0]].astype(F32)
    for block in (first, second, third):
        total = total + block[...].astype(F32)
    tiles = [total[at : at + span] for at in range(0, total.shape[0], span)]
    flat = jnp.concatenate(tiles, axis=1)
    step = (flat.shape[1] - LANES // 2) // y_count
    for y in range(y_count):
        block = flat[:, y * step : (y + 1) * step]
        rest = jnp.zeros((span, lanes - step), F32)
        out[y] = jnp.concatenate([block, rest], axis=1).astype(BF16)


def regroup_pair(info, blocks, first, second, third, out):
    x_count, span, lanes = out.shape
    total = blocks[info[2]].astype(F32)
    for block in (first, second, third):
        total = total + block[...].astype(F32)
    width = x_count * span
    step = total.shape[0] // (width // LANES)
    tiles = [total[at : at + step].T for at in range(0, total.shape[0], step)]
    flat = jnp.concatenate(tiles, axis=0)
    flat = jnp.concatenate([flat, jnp.zeros((width, lanes - step), F32)], axis=1)
    for x in range(x_count):
        out[x] = flat[x * span : (x + 1) * span].astype(BF16)


def reduce_start(coords, terms, inner, width, beside):
    x_count, y_count = lax.axis_size("x"), lax.axis_size("y")
    wide_rows, pair_rows = term_rows(inner, width, y_count, x_count)
    halves = exchange(terms, "c")
    cut = x_count * wide_rows

    def both(part):
        return (part[0].astype(F32) + part[1].astype(F32)).astype(BF16)

    wide = both(halves[:, :cut]).reshape(x_count, wide_rows, LANES)
    pair = both(halves[:, cut:]).reshape(y_count, pair_rows, LANES)
    arrived, pair_in, beside = tie(scatter(wide, "x"), scatter(pair, "y"), beside)
    wide = in_vmem(
        regroup_wide,
        coords,
        [wide] + arrived,
        shape_of(y_count, 3 * inner // x_count, 2 * LANES),
    )
    blocks = in_vmem(
        regroup_pair,
        coords,
        [pair] + pair_in,
        shape_of(x_count, width // x_count, 2 * LANES),
    )
    return (wide, blocks), beside


def reduce_end(reduced, inner, width, beside):
    wide, pair = reduced
    z_count = lax.axis_size("z")
    step = width // (2 * lax.axis_size("y"))
    wide_in, pair_in, beside = tie(scatter(wide, "y"), scatter(pair, "x"), beside)
    wide = sum_with_own(wide, wide_in, "y").reshape(z_count, -1, 2 * LANES)
    pair = sum_with_own(pair, pair_in, "x").reshape(z_count, -1, 2 * LANES)
    total = jnp.sum(exchange(jnp.concatenate([pair, wide], axis=1), "z").astype(F32), axis=0)
    narrow = pair.shape[1]
    half = step // 2
    summed = (total[:narrow, :half].T, total[narrow:, :step].T, total[:narrow, half:step].T)
    return summed, beside


def on_device(
    hidden,
    spatial_qkv,
    out_spatial,
    qkv_temporal,
    out_temporal,
    modulation,
    cotangent,
    frame_count,
    patch_height,
    patch_width,
):
    seq_count = lax.axis_size(("y", "c"))
    seq_place = lax.axis_index(("y", "c"))
    y_count = lax.axis_size("y")
    stream = hidden[0]
    grad_out = cotangent[0]
    packed_qkv = spatial_qkv[0]
    frame_dev, slot_total, width = stream.shape
    slot_dev = slot_total // seq_count
    inner = out_spatial.shape[0] * seq_count
    slots = 8
    groups = slot_dev // slots
    rows = frame_dev * seq_count * slots
    coords = jnp.stack([lax.axis_index(name) for name in ("x", "z", "y", "c")]).astype(jnp.int32)
    info = jnp.stack(
        [
            frame_count[0],
            patch_height[0] * patch_width[0],
            seq_place * slot_dev,
            seq_place * frame_dev,
        ]
    ).astype(jnp.int32)

    def to_slots(tokens):
        split = tokens.reshape(frame_dev, seq_count, groups, slots, -1)
        split = jnp.transpose(split, (1, 2, 0, 3, 4))
        return exchange(split.reshape(seq_count, groups, frame_dev * slots, -1), ("y", "c"))

    def to_frames(tokens):
        moved = exchange(tokens, ("y", "c")).reshape(seq_count, groups, frame_dev, slots, -1)
        return jnp.transpose(moved, (2, 0, 1, 3, 4)).reshape(frame_dev, slot_total, -1)

    out_s = shape_of(frame_dev, slot_total, inner)
    out_s = run(
        spatial_forward,
        frame_dev,
        [info, packed_qkv],
        [SCALARS, per_frame(packed_qkv)],
        out_s,
        per_frame(out_s),
        [],
    )
    thin, wide, other = near_rows(out_spatial, qkv_temporal, out_temporal)
    rows_z = jnp.concatenate([thin, other, wide], axis=0)
    cut = thin.shape[0]
    stream_tied, _ = tie(stream, rows_z)
    stream_s = to_slots(stream_tied)
    (onward, kept), (stream_s, out_s) = gather_z(coords, rows_z, cut, (stream_s, out_s))
    out_s_s = to_slots(out_s)
    grad_tied, _ = tie(grad_out, out_s_s)
    grad_s = to_slots(grad_tied)

    first = shift_both(onward, "x", 1)
    first_k = shift_both(kept, "x", 1)
    second = shift_both(first, "x", 1)
    second, out_s_s = tie(second, out_s_s)
    x_count = lax.axis_size("x")
    w_spatial, w_temporal, w_qkv = in_vmem(
        place_along_x,
        coords,
        [onward, kept, first, first_k, swap(first), swap(first_k), second, swap(second)],
        (shape_of(width, inner), shape_of(width, inner), shape_of(3 * inner, width)),
        [pltpu.VMEM((x_count, 2 * onward.shape[0], width), BF16)],
    )

    result = (
        shape_of(groups, rows, width),
        shape_of(groups, rows, width),
        shape_of(groups, rows, 3 * inner),
        shape_of(seq_count, groups, rows // seq_count, inner),
    )
    mixed_s, modulated, qkv_t, out_t = run(
        functools.partial(temporal_forward, slots=slots),
        groups,
        [info, modulation, stream_s, out_s_s, w_spatial, w_qkv],
        [SCALARS, whole(modulation), per_group(stream_s), per_group(out_s_s), whole(w_spatial), whole(w_qkv)],
        result,
        [per_frame(result[0]), per_frame(result[1]), per_frame(result[2]), per_group(result[3])],
        [],
    )
    out_t_tied, _ = tie(out_t, grad_s)
    out_t_f = to_frames(out_t_tied)

    wide_rows, pair_rows = term_rows(inner, width, y_count, x_count)
    result = (
        shape_of(seq_count, groups, rows // seq_count, width),
        shape_of(2, x_count * wide_rows + y_count * pair_rows, LANES),
    )
    total = pltpu.VMEM((inner, width), F32)
    ln_grad, terms = run(
        functools.partial(temporal_backward, slots=slots, y_count=y_count, x_count=x_count),
        groups,
        [info, modulation, grad_s, mixed_s, out_s_s, qkv_t, out_t, modulated, w_temporal, w_qkv],
        [
            SCALARS,
            whole(modulation),
            per_group(grad_s),
            per_frame(mixed_s),
            per_group(out_s_s),
            per_frame(qkv_t),
            per_group(out_t),
            per_frame(modulated),
            whole(w_temporal),
            whole(w_qkv),
        ],
        result,
        [per_group(result[0]), whole(result[1])],
        [total, total, pltpu.VMEM((2, 3 * inner, width // 2), F32)],
    )
    terms, out_t_f = lax.optimization_barrier((terms, out_t_f))
    block_out = shape_of(frame_dev, slot_total, width)
    block_out = run(
        block_forward,
        frame_dev,
        [info, modulation, stream, out_s, out_t_f, w_spatial, w_temporal],
        [
            SCALARS,
            whole(modulation),
            per_frame(stream),
            per_frame(out_s),
            per_frame(out_t_f),
            whole(w_spatial),
            whole(w_temporal),
        ],
        block_out,
        per_frame(block_out),
        [],
    )
    reduced, block_out = reduce_start(coords, terms, inner, width, block_out)
    ln_frames = to_frames(ln_grad)

    result = (shape_of(frame_dev, slot_total, width), shape_of(frame_dev, slot_total, 3 * inner))
    hidden_grad, qkv_s_grad = run(
        spatial_backward,
        frame_dev,
        [info, grad_out, ln_frames, packed_qkv, out_s, w_spatial],
        [
            SCALARS,
            per_frame(grad_out),
            per_frame(ln_frames),
            per_frame(packed_qkv),
            per_frame(out_s),
            whole(w_spatial),
        ],
        result,
        [per_frame(result[0]), per_frame(result[1])],
        [],
    )
    summed, qkv_s_grad = reduce_end(reduced, inner, width, qkv_s_grad)
    return (block_out[None], hidden_grad[None], qkv_s_grad[None], summed[0], summed[1], summed[2])


def solution(mesh):
    torus = Mesh(mesh.devices.reshape(4, 8, 4, 2), ("x", "z", "y", "c"))
    dp, seq = ("x", "z"), ("y", "c")
    tokens = P(dp, seq, None, None)
    weight = P(seq, dp)
    placed = (
        tokens,
        tokens,
        weight,
        weight,
        weight,
        P(dp, None, None),
        tokens,
        P(dp),
        P(dp),
        P(dp),
    )
    return jax.shard_map(
        on_device,
        mesh=torus,
        in_specs=placed,
        out_specs=(tokens, tokens, tokens, weight, weight, weight),
        check_vma=False,
    )
```

```python
import functools
import math

import jax
import jax.numpy as jnp
from jax import lax
from jax.experimental import pallas as pl
from jax.experimental.pallas import tpu as pltpu
from jax.sharding import Mesh
from jax.sharding import PartitionSpec as P

HEAD_DIM = 72
EPSILON = 1e-06
NEGATIVE = -1e30
LANES = 128
VMEM_BYTES = 56 * 1024 * 1024
F32 = jnp.float32
BF16 = jnp.bfloat16


def dot_nn(left, right):
    return lax.dot_general(left, right, (((1,), (0,)), ((), ())), preferred_element_type=F32)


def dot_nt(left, right):
    return lax.dot_general(left, right, (((1,), (1,)), ((), ())), preferred_element_type=F32)


def dot_tn(left, right):
    return lax.dot_general(left, right, (((0,), (0,)), ((), ())), preferred_element_type=F32)


def head_windows(inner):
    windows = []
    for head in range(inner // HEAD_DIM):
        low = head * HEAD_DIM
        start = low // LANES * LANES
        stop = min(-(-(low + HEAD_DIM) // LANES) * LANES, inner)
        windows.append((start, stop, low - start))
    return windows


def own_lanes(window):
    start, stop, offset = window
    lane = lax.broadcasted_iota(jnp.int32, (1, stop - start), 1)
    return (lane >= offset) & (lane < offset + HEAD_DIM)


def only(lanes, rows):
    return jnp.where(lanes, rows, jnp.zeros((), rows.dtype))


def lane_tiles(inner):
    return [(low, min(low + LANES, inner)) for low in range(0, inner, LANES)]


def combine(inner, factors, rows):
    pieces = []
    for low, high in lane_tiles(inner):
        lane = low + lax.broadcasted_iota(jnp.int32, (1, high - low), 1)
        total = None
        for head, factor in enumerate(factors):
            start, stop = head * HEAD_DIM, (head + 1) * HEAD_DIM
            if stop <= low or start >= high:
                continue
            own = only((lane >= start) & (lane < stop), rows[:, low:high])
            part = lax.dot_general(
                factor[0], own, (((factor[1],), (0,)), ((), ())), preferred_element_type=F32
            )
            total = part if total is None else total + part
        pieces.append(total)
    return jnp.concatenate(pieces, axis=1)


def head_logits(query, key, allowed):
    logits = []
    for window in head_windows(query.shape[1]):
        start, stop, _ = window
        own = only(own_lanes(window), key[:, start:stop])
        logits.append(dot_nt(query[:, start:stop], own))
    return logits


def softmax_rows(logits, allowed):
    logits = jnp.where(allowed, logits * (1.0 / math.sqrt(HEAD_DIM)), NEGATIVE)
    powers = jnp.exp(logits - jnp.max(logits, axis=1, keepdims=True))
    return powers * (1.0 / jnp.sum(powers, axis=1, keepdims=True))


def attend_heads(query, key, value, allowed):
    logits = head_logits(query, key, allowed)
    probs = [softmax_rows(one, allowed).astype(BF16) for one in logits]
    return combine(query.shape[1], [(one, 1) for one in probs], value)


def attend_heads_back(query, key, value, out, out_grad, allowed):
    inner = query.shape[1]
    factor = 1.0 / math.sqrt(HEAD_DIM)
    logits = head_logits(query, key, allowed)
    slopes, deltas = [], []
    for window in head_windows(inner):
        start, stop, _ = window
        own = only(own_lanes(window), out_grad[:, start:stop])
        slopes.append(dot_nt(own, value[:, start:stop]))
        product = own.astype(F32) * out[:, start:stop].astype(F32)
        deltas.append(jnp.sum(product, axis=1, keepdims=True))
    halves, grads = [], []
    for one, slope, delta in zip(logits, slopes, deltas):
        probs = softmax_rows(one, allowed)
        halves.append(probs.astype(BF16))
        grads.append((probs * (slope - delta)).astype(BF16))
    q_grad = combine(inner, [(one, 1) for one in grads], key) * factor
    k_grad = combine(inner, [(one, 0) for one in grads], query) * factor
    v_grad = combine(inner, [(one, 0) for one in halves], out_grad)
    return jnp.concatenate(
        [q_grad.astype(BF16), k_grad.astype(BF16), v_grad.astype(BF16)], axis=1
    )


def slot_masks(info_ref, rows, slots):
    frames, limit, first = info_ref[0], info_ref[1], info_ref[2]
    group = pl.program_id(0)
    row = lax.broadcasted_iota(jnp.int32, (rows, 1), 0)
    slot = first + group * slots + row % slots
    token = (row // slots < frames) & (slot < limit)
    col = lax.broadcasted_iota(jnp.int32, (1, rows), 1)
    allowed = (row % slots == col % slots) & (col // slots < frames)
    return token.astype(F32), allowed


def normalised(mixed):
    values = mixed.astype(F32)
    centred = values - jnp.mean(values, axis=1, keepdims=True)
    inv_std = lax.rsqrt(jnp.mean(centred * centred, axis=1, keepdims=True) + EPSILON)
    return centred * inv_std, inv_std


def temporal_forward(
    info, mod, stream, out_s, w_spatial, w_qkv, mixed_ref, mod_ref, qkv_ref, out_ref, slots
):
    rows, width = mod_ref.shape[1:]
    inner = out_s.shape[-1]
    token, allowed = slot_masks(info, rows, slots)
    branch = dot_nt(out_s[...].reshape(rows, inner), w_spatial[...])
    mixed = (stream[...].reshape(rows, width).astype(F32) + token * branch).astype(BF16)
    mixed_ref[...] = mixed.reshape(mixed_ref.shape)
    normed, _ = normalised(mixed)
    modulated = (normed * (1.0 + mod[0, 1:2]) + mod[0, 0:1]).astype(BF16)
    mod_ref[...] = modulated.reshape(mod_ref.shape)
    qkv = dot_nt(modulated, w_qkv[...]).astype(BF16)
    qkv_ref[...] = qkv.reshape(qkv_ref.shape)
    out = attend_heads(qkv[:, :inner], qkv[:, inner : 2 * inner], qkv[:, 2 * inner :], allowed)
    out_ref[...] = out.astype(BF16).reshape(out_ref.shape)


def temporal_backward(
    info, mod, grad, mixed, out_s, qkv_ref, out_t, modulated, w_temporal, w_qkv, ln_ref, terms,
    left_s, left_t, left_q, right_s, right_t, right_q, slots, y_count, x_count,
):
    rows, width = modulated.shape[1:]
    inner = out_s.shape[-1]
    token, allowed = slot_masks(info, rows, slots)

    grad_f = grad[...].reshape(rows, width).astype(F32)
    branch_grad = (token * mod[0, 2:3] * grad_f).astype(BF16)
    out_grad = dot_nn(branch_grad, w_temporal[...]).astype(BF16)
    qkv = qkv_ref[...].reshape(rows, 3 * inner)
    out = out_t[...].reshape(rows, inner)
    dqkv = attend_heads_back(
        qkv[:, :inner], qkv[:, inner : 2 * inner], qkv[:, 2 * inner :], out, out_grad, allowed
    )

    norm_grad = dot_nn(dqkv, w_qkv[...]) * (1.0 + mod[0, 1:2])
    normed, inv_std = normalised(mixed[...].reshape(rows, width))
    first = jnp.mean(norm_grad, axis=1, keepdims=True)
    second = jnp.mean(norm_grad * normed, axis=1, keepdims=True)
    ln_grad = (inv_std * (norm_grad - first - normed * second)).astype(BF16)
    ln_ref[...] = ln_grad.reshape(ln_ref.shape)
    hidden_grad = (grad_f + ln_grad.astype(F32)).astype(BF16)
    spatial_grad = (token * hidden_grad.astype(F32)).astype(BF16)

    step = width // (2 * y_count)
    normal = modulated[...].reshape(rows, width)
    place = pl.ds(pl.program_id(0) * rows, rows)
    left_s[place, :] = out_s[...].reshape(rows, inner)
    left_t[place, :] = out
    left_q[place, :] = dqkv
    right_s[place, :] = spatial_grad
    right_t[place, :] = branch_grad
    for c in range(2):
        pieces = [normal[:, (2 * y + c) * step : (2 * y + c + 1) * step] for y in range(y_count)]
        right_q[c, place, :] = jnp.concatenate(pieces, axis=1)

    @pl.when(pl.program_id(0) == pl.num_programs(0) - 1)
    def _():
        store_terms(left_s, left_t, left_q, right_s, right_t, right_q, terms, y_count, x_count)


def term_rows(inner, width, y_count, x_count):
    tiles = -(-(width // 2) // LANES)
    return tiles * (3 * inner // x_count), width // LANES * (inner // y_count)


def store_terms(left_s, left_t, left_q, right_s, right_t, right_q, terms, y_count, x_count):
    inner, width = left_s.shape[1], right_s.shape[1]
    span, step = 3 * inner // x_count, inner // (2 * y_count)
    wide, pair = term_rows(inner, width, y_count, x_count)
    half = width // 2
    for c in range(2):
        sum_q = dot_tn(left_q[...], right_q[c])
        for x in range(x_count):
            for tile in range(wide // span):
                low, high = tile * LANES, min((tile + 1) * LANES, half)
                block = sum_q[x * span : (x + 1) * span, low:high]
                if high - low < LANES:
                    rest = jnp.zeros((span, LANES - (high - low)), F32)
                    block = jnp.concatenate([block, rest], axis=1)
                start = x * wide + tile * span
                terms[c, start : start + span] = block.astype(BF16)
    sum_s = dot_tn(left_s[...], right_s[...])
    sum_t = dot_tn(left_t[...], right_t[...])
    for c in range(2):
        for y in range(y_count):
            place = (2 * y + c) * step
            for tile in range(width // LANES):
                lanes = slice(tile * LANES, (tile + 1) * LANES)
                block = jnp.concatenate(
                    [sum_s[place : place + step, lanes], sum_t[place : place + step, lanes]],
                    axis=0,
                )
                start = x_count * wide + y * pair + tile * 2 * step
                terms[c, start : start + 2 * step] = block.astype(BF16)


def frame_keys(info_ref, rows):
    return lax.broadcasted_iota(jnp.int32, (1, rows), 1) < info_ref[1]


def frame_tokens(info_ref, rows):
    row = lax.broadcasted_iota(jnp.int32, (rows, 1), 0)
    alive = info_ref[3] + pl.program_id(0) < info_ref[0]
    return ((row < info_ref[1]) & alive).astype(F32)


def spatial_forward(info, qkv_ref, out_ref):
    rows, inner = out_ref.shape[1:]
    qkv = qkv_ref[0]
    out = attend_heads(
        qkv[:, :inner], qkv[:, inner : 2 * inner], qkv[:, 2 * inner :], frame_keys(info, rows)
    )
    out_ref[0] = out.astype(BF16)


def block_forward(info, mod, stream, out_s, out_t, w_spatial, w_temporal, block_ref):
    rows = stream.shape[1]
    token = frame_tokens(info, rows)
    spatial = dot_nt(out_s[0], w_spatial[...])
    mixed = (stream[0].astype(F32) + token * spatial).astype(BF16)
    branch = dot_nt(out_t[0], w_temporal[...])
    block_ref[0] = (mixed.astype(F32) + token * mod[0, 2:3] * branch).astype(BF16)


def spatial_backward(
    info, grad, ln_grad, qkv_ref, out_s, w_spatial, hidden_ref, dqkv_ref
):
    rows, inner = out_s.shape[1:]
    hidden_grad = (grad[0].astype(F32) + ln_grad[0].astype(F32)).astype(BF16)
    hidden_ref[0] = hidden_grad
    branch_grad = (frame_tokens(info, rows) * hidden_grad.astype(F32)).astype(BF16)
    out_grad = dot_nn(branch_grad, w_spatial[...]).astype(BF16)
    qkv = qkv_ref[0]
    dqkv_ref[0] = attend_heads_back(
        qkv[:, :inner], qkv[:, inner : 2 * inner], qkv[:, 2 * inner :], out_s[0], out_grad,
        frame_keys(info, rows),
    )


def whole(array):
    return pl.BlockSpec(
        array.shape, lambda step: (0,) * array.ndim, pipeline_mode=pl.Buffered(1)
    )


def per_frame(array):
    return pl.BlockSpec((1,) + array.shape[1:], lambda step: (step, 0, 0))


def per_group(array):
    return pl.BlockSpec(
        (array.shape[0], 1) + array.shape[2:], lambda step: (0, step, 0, 0)
    )


SCALARS = pl.BlockSpec(memory_space=pltpu.SMEM)


def run(body, steps, operands, specs, results, result_specs, scratch):
    return pl.pallas_call(
        body,
        grid=(steps,),
        in_specs=specs,
        out_specs=result_specs,
        out_shape=results,
        scratch_shapes=scratch,
        compiler_params=pltpu.CompilerParams(vmem_limit_bytes=VMEM_BYTES),
        cost_estimate=pl.CostEstimate(flops=1, bytes_accessed=1, transcendentals=0),
    )(*operands)


def shape_of(*dims, dtype=BF16):
    return jax.ShapeDtypeStruct(dims, dtype)


def exchange(rows, axes):
    return lax.all_to_all(rows, axes, 0, 0, tiled=True)


def shift(rows, axis, hops):
    count = lax.axis_size(axis)
    return lax.ppermute(rows, axis, [(at, (at + hops) % count) for at in range(count)])


def shift_both(rows, axis, hops):
    count = lax.axis_size(axis)
    pairs = []
    for at in range(count):
        pairs.append((2 * at, 2 * ((at - hops) % count)))
        pairs.append((2 * at + 1, 2 * ((at + hops) % count) + 1))
    return lax.ppermute(rows, (axis, "c"), pairs)


def swap(rows):
    return shift(rows, "c", 1)


def place_along_z(
    info, own, near, mid, far, last, near_p, mid_p, far_p, onward, kept, stack, flat, cut
):
    place, count = info[1], stack.shape[0]
    sign = 1 - 2 * info[3]
    stack[place] = own[...]
    stack[lax.rem(place + count // 2, count)] = last[...]
    for hops, mine, other in ((1, near, near_p), (2, mid, mid_p), (3, far, far_p)):
        stack[lax.rem(place + sign * hops + count, count)] = mine[...]
        stack[lax.rem(place - sign * hops + count, count)] = other[...]

    inner = flat.shape[1] // 2
    step = stack.shape[1] - 2 * cut
    for z in range(count):
        block = stack[z].astype(F32)
        side = 2 * z // count
        for number in range(2):
            for part in range(2):
                row = (2 * number * count + 4 * (z % (count // 2)) + 2 * part) * cut // 2
                flat[row : row + cut, side * inner : (side + 1) * inner] = block[
                    number * cut : (number + 1) * cut, part * inner : (part + 1) * inner
                ]
        row = 2 * count * cut + z * step
        flat[row : row + step] = block[2 * cut :]
    size = flat.shape[0] // 2
    lower, upper = flat[:size].astype(BF16), flat[size:].astype(BF16)

    @pl.when(info[3] == 0)
    def _():
        onward[...] = lower
        kept[...] = upper

    @pl.when(info[3] != 0)
    def _():
        onward[...] = upper
        kept[...] = lower


def place_along_x(
    info, own, own_k, near, near_k, near_p, near_pk, part, part_p, spatial, temporal, wide, out
):
    place, count = info[0], out.shape[0]
    half = part.shape[0]
    opposite = lax.rem(place + count // 2, count)

    def fill(index, first, second):
        out[index, :half] = first[...]
        out[index, half:] = second[...]

    @pl.when(info[3] == 0)
    def _():
        fill(place, own, own_k)
        fill(lax.rem(place + 1, count), near, near_k)
        fill(lax.rem(place - 1 + count, count), near_pk, near_p)
        fill(opposite, part, part_p)

    @pl.when(info[3] != 0)
    def _():
        fill(place, own_k, own)
        fill(lax.rem(place - 1 + count, count), near_k, near)
        fill(lax.rem(place + 1, count), near_p, near_pk)
        fill(opposite, part_p, part)

    cut, inner = out.shape[2] // count // 2, out.shape[2] // 2
    span = wide.shape[0] // count
    for x in range(count):
        for number, result in ((0, spatial), (1, temporal)):
            block = out[x, number * cut : (number + 1) * cut]
            result[2 * x * cut : (2 * x + 1) * cut] = block[:, :inner]
            result[(2 * x + 1) * cut : (2 * x + 2) * cut] = block[:, inner:]
        wide[x * span : (x + 1) * span] = out[x, 2 * cut :]


def in_vmem(body, info, blocks, results, scratch=()):
    vmem = pl.BlockSpec(memory_space=pltpu.VMEM)
    return pl.pallas_call(
        body,
        in_specs=[SCALARS] + [vmem] * len(blocks),
        out_specs=jax.tree.map(lambda _: vmem, results),
        out_shape=results,
        scratch_shapes=list(scratch),
        cost_estimate=pl.CostEstimate(flops=1, bytes_accessed=1, transcendentals=0),
        compiler_params=pltpu.CompilerParams(vmem_limit_bytes=VMEM_BYTES),
    )(info, *blocks)


def tie(*values):
    return lax.optimization_barrier(values)


def near_rows(out_spatial, qkv_temporal, out_temporal):
    half, narrow = out_spatial.shape
    packed = jnp.concatenate(
        [jnp.concatenate([out_spatial.T, out_temporal.T], axis=1), qkv_temporal.T], axis=0
    )
    near = jnp.transpose(lax.all_gather(packed, ("y", "c"), axis=0, tiled=False), (1, 0, 2))
    thin = near[:narrow, :, :half].reshape(narrow, -1)
    other = near[:narrow, :, half:].reshape(narrow, -1)
    wide = near[narrow:].reshape(near.shape[0] - narrow, -1)
    return (fold(thin), wide, fold(other))


def fold(rows):
    cut = rows.shape[-2] // 2
    return jnp.concatenate([rows[..., :cut, :], rows[..., cut:, :]], axis=-1)


def unfold(rows):
    cut = rows.shape[-1] // 2
    return jnp.concatenate([rows[..., :cut], rows[..., cut:]], axis=-2)


def gather_z(coords, rows, cut, beside):
    arrived = [shift_both(rows, "z", hops) for hops in (2, 1, 3)]
    arrived = [arrived[1], arrived[0], arrived[2], shift_both(arrived[0], "z", 2)]
    arrived, beside = tie(arrived, beside)
    swapped = [swap(block) for block in arrived[:3]]
    count, width = lax.axis_size("z"), rows.shape[1]
    half = shape_of(count * rows.shape[0] // 2, width)
    halves = in_vmem(
        functools.partial(place_along_z, cut=cut),
        coords,
        [rows] + arrived + swapped,
        (half, half),
        [pltpu.VMEM((count,) + rows.shape, BF16), pltpu.VMEM((2 * half.shape[0], width), F32)],
    )
    return halves, beside


def scatter(blocks, axis):
    count, place = lax.axis_size(axis), lax.axis_index(axis)
    arrived = []
    for hops in range(1, count):
        block = lax.dynamic_index_in_dim(blocks, (place + hops) % count, 0, keepdims=False)
        arrived.append(shift(block, axis, hops))
    return arrived


def sum_with_own(blocks, arrived, axis):
    place = lax.axis_index(axis)
    total = lax.dynamic_index_in_dim(blocks, place, 0, keepdims=False).astype(F32)
    for block in arrived:
        total = total + block.astype(F32)
    return total.astype(BF16)


def regroup_wide(info, blocks, first, second, third, out):
    y_count, span, lanes = out.shape
    total = blocks[info[0]].astype(F32)
    for block in (first, second, third):
        total = total + block[...].astype(F32)
    tiles = [total[at : at + span] for at in range(0, total.shape[0], span)]
    flat = jnp.concatenate(tiles, axis=1)
    step = (flat.shape[1] - LANES // 2) // y_count
    for y in range(y_count):
        block = flat[:, y * step : (y + 1) * step]
        rest = jnp.zeros((span, lanes - step), F32)
        out[y] = jnp.concatenate([block, rest], axis=1).astype(BF16)


def regroup_pair(info, blocks, first, second, third, out):
    x_count, span, lanes = out.shape
    total = blocks[info[2]].astype(F32)
    for block in (first, second, third):
        total = total + block[...].astype(F32)
    width = x_count * span
    step = total.shape[0] // (width // LANES)
    tiles = [total[at : at + step].T for at in range(0, total.shape[0], step)]
    flat = jnp.concatenate(tiles, axis=0)
    flat = jnp.concatenate([flat, jnp.zeros((width, lanes - step), F32)], axis=1)
    for x in range(x_count):
        out[x] = flat[x * span : (x + 1) * span].astype(BF16)


def reduce_start(coords, terms, inner, width, beside):
    x_count, y_count = lax.axis_size("x"), lax.axis_size("y")
    wide_rows, pair_rows = term_rows(inner, width, y_count, x_count)
    halves = exchange(terms, "c")
    cut = x_count * wide_rows

    def both(part):
        return (part[0].astype(F32) + part[1].astype(F32)).astype(BF16)

    wide = both(halves[:, :cut]).reshape(x_count, wide_rows, LANES)
    pair = both(halves[:, cut:]).reshape(y_count, pair_rows, LANES)
    arrived, pair_in, beside = tie(scatter(wide, "x"), scatter(pair, "y"), beside)
    wide = in_vmem(
        regroup_wide,
        coords,
        [wide] + arrived,
        shape_of(y_count, 3 * inner // x_count, 2 * LANES),
    )
    blocks = in_vmem(
        regroup_pair,
        coords,
        [pair] + pair_in,
        shape_of(x_count, width // x_count, 2 * LANES),
    )
    return (wide, blocks), beside


def reduce_end(reduced, inner, width, beside):
    wide, pair = reduced
    z_count = lax.axis_size("z")
    step = width // (2 * lax.axis_size("y"))
    wide_in, pair_in, beside = tie(scatter(wide, "y"), scatter(pair, "x"), beside)
    wide = sum_with_own(wide, wide_in, "y").reshape(z_count, -1, 2 * LANES)
    pair = sum_with_own(pair, pair_in, "x").reshape(z_count, -1, 2 * LANES)
    total = jnp.sum(exchange(jnp.concatenate([pair, wide], axis=1), "z").astype(F32), axis=0)
    narrow = pair.shape[1]
    half = step // 2
    summed = (total[:narrow, :half].T, total[narrow:, :step].T, total[:narrow, half:step].T)
    return summed, beside


def on_device(
    hidden,
    spatial_qkv,
    out_spatial,
    qkv_temporal,
    out_temporal,
    modulation,
    cotangent,
    frame_count,
    patch_height,
    patch_width,
):
    seq_count = lax.axis_size(("y", "c"))
    seq_place = lax.axis_index(("y", "c"))
    y_count = lax.axis_size("y")
    stream = hidden[0]
    grad_out = cotangent[0]
    packed_qkv = spatial_qkv[0]
    frame_dev, slot_total, width = stream.shape
    slot_dev = slot_total // seq_count
    inner = out_spatial.shape[0] * seq_count
    slots = 8
    groups = slot_dev // slots
    rows = frame_dev * seq_count * slots
    coords = jnp.stack([lax.axis_index(name) for name in ("x", "z", "y", "c")]).astype(jnp.int32)
    info = jnp.stack(
        [
            frame_count[0],
            patch_height[0] * patch_width[0],
            seq_place * slot_dev,
            seq_place * frame_dev,
        ]
    ).astype(jnp.int32)

    def to_slots(tokens):
        split = tokens.reshape(frame_dev, seq_count, groups, slots, -1)
        split = jnp.transpose(split, (1, 2, 0, 3, 4))
        return exchange(split.reshape(seq_count, groups, frame_dev * slots, -1), ("y", "c"))

    def to_frames(tokens):
        moved = exchange(tokens, ("y", "c")).reshape(seq_count, groups, frame_dev, slots, -1)
        return jnp.transpose(moved, (2, 0, 1, 3, 4)).reshape(frame_dev, slot_total, -1)

    out_s = shape_of(frame_dev, slot_total, inner)
    out_s = run(
        spatial_forward,
        frame_dev,
        [info, packed_qkv],
        [SCALARS, per_frame(packed_qkv)],
        out_s,
        per_frame(out_s),
        [],
    )
    thin, wide, other = near_rows(out_spatial, qkv_temporal, out_temporal)
    rows_z = jnp.concatenate([thin, other, wide], axis=0)
    cut = thin.shape[0]
    stream_tied, _ = tie(stream, rows_z)
    stream_s = to_slots(stream_tied)
    (onward, kept), (stream_s, out_s) = gather_z(coords, rows_z, cut, (stream_s, out_s))
    grad_tied, _ = tie(grad_out, stream_s)
    grad_s = to_slots(grad_tied)
    out_s_tied, _ = tie(out_s, grad_s)
    out_s_s = to_slots(out_s_tied)

    first = shift_both(onward, "x", 1)
    first_k = shift_both(kept, "x", 1)
    second = shift_both(first, "x", 1)
    x_count = lax.axis_size("x")
    w_spatial, w_temporal, w_qkv = in_vmem(
        place_along_x,
        coords,
        [onward, kept, first, first_k, swap(first), swap(first_k), second, swap(second)],
        (shape_of(width, inner), shape_of(width, inner), shape_of(3 * inner, width)),
        [pltpu.VMEM((x_count, 2 * onward.shape[0], width), BF16)],
    )

    result = (
        shape_of(groups, rows, width),
        shape_of(groups, rows, width),
        shape_of(groups, rows, 3 * inner),
        shape_of(seq_count, groups, rows // seq_count, inner),
    )
    mixed_s, modulated, qkv_t, out_t = run(
        functools.partial(temporal_forward, slots=slots),
        groups,
        [info, modulation, stream_s, out_s_s, w_spatial, w_qkv],
        [SCALARS, whole(modulation), per_group(stream_s), per_group(out_s_s), whole(w_spatial), whole(w_qkv)],
        result,
        [per_frame(result[0]), per_frame(result[1]), per_frame(result[2]), per_group(result[3])],
        [],
    )
    out_t_f = to_frames(out_t)

    wide_rows, pair_rows = term_rows(inner, width, y_count, x_count)
    result = (
        shape_of(seq_count, groups, rows // seq_count, width),
        shape_of(2, x_count * wide_rows + y_count * pair_rows, LANES),
    )
    tokens = groups * rows
    kept = [(inner,), (inner,), (3 * inner,), (width,), (width,)]
    kept = [pltpu.VMEM((tokens,) + shape, BF16) for shape in kept]
    kept.append(pltpu.VMEM((2, tokens, width // 2), BF16))
    ln_grad, terms = run(
        functools.partial(temporal_backward, slots=slots, y_count=y_count, x_count=x_count),
        groups,
        [info, modulation, grad_s, mixed_s, out_s_s, qkv_t, out_t, modulated, w_temporal, w_qkv],
        [
            SCALARS,
            whole(modulation),
            per_group(grad_s),
            per_frame(mixed_s),
            per_group(out_s_s),
            per_frame(qkv_t),
            per_group(out_t),
            per_frame(modulated),
            whole(w_temporal),
            whole(w_qkv),
        ],
        result,
        [per_group(result[0]), whole(result[1])],
        kept,
    )
    terms, out_t_f = lax.optimization_barrier((terms, out_t_f))
    block_out = shape_of(frame_dev, slot_total, width)
    block_out = run(
        block_forward,
        frame_dev,
        [info, modulation, stream, out_s, out_t_f, w_spatial, w_temporal],
        [
            SCALARS,
            whole(modulation),
            per_frame(stream),
            per_frame(out_s),
            per_frame(out_t_f),
            whole(w_spatial),
            whole(w_temporal),
        ],
        block_out,
        per_frame(block_out),
        [],
    )
    reduced, block_out = reduce_start(coords, terms, inner, width, block_out)
    ln_frames = to_frames(ln_grad)

    result = (shape_of(frame_dev, slot_total, width), shape_of(frame_dev, slot_total, 3 * inner))
    hidden_grad, qkv_s_grad = run(
        spatial_backward,
        frame_dev,
        [info, grad_out, ln_frames, packed_qkv, out_s, w_spatial],
        [
            SCALARS,
            per_frame(grad_out),
            per_frame(ln_frames),
            per_frame(packed_qkv),
            per_frame(out_s),
            whole(w_spatial),
        ],
        result,
        [per_frame(result[0]), per_frame(result[1])],
        [],
    )
    summed, qkv_s_grad = reduce_end(reduced, inner, width, qkv_s_grad)
    return (block_out[None], hidden_grad[None], qkv_s_grad[None], summed[0], summed[1], summed[2])


def solution(mesh):
    torus = Mesh(mesh.devices.reshape(4, 8, 4, 2), ("x", "z", "y", "c"))
    dp, seq = ("x", "z"), ("y", "c")
    tokens = P(dp, seq, None, None)
    weight = P(seq, dp)
    placed = (
        tokens,
        tokens,
        weight,
        weight,
        weight,
        P(dp, None, None),
        tokens,
        P(dp),
        P(dp),
        P(dp),
    )
    return jax.shard_map(
        on_device,
        mesh=torus,
        in_specs=placed,
        out_specs=(tokens, tokens, tokens, weight, weight, weight),
        check_vma=False,
    )
```

```python
import functools
import math

import jax
import jax.numpy as jnp
from jax import lax
from jax.experimental import pallas as pl
from jax.experimental.pallas import tpu as pltpu
from jax.sharding import Mesh
from jax.sharding import PartitionSpec as P

HEAD_DIM = 72
EPSILON = 1e-06
NEGATIVE = -1e30
LANES = 128
VMEM_BYTES = 56 * 1024 * 1024
F32 = jnp.float32
BF16 = jnp.bfloat16


def dot_nn(left, right):
    return lax.dot_general(left, right, (((1,), (0,)), ((), ())), preferred_element_type=F32)


def dot_nt(left, right):
    return lax.dot_general(left, right, (((1,), (1,)), ((), ())), preferred_element_type=F32)


def dot_tn(left, right):
    return lax.dot_general(left, right, (((0,), (0,)), ((), ())), preferred_element_type=F32)


def head_windows(inner):
    windows = []
    for head in range(inner // HEAD_DIM):
        low = head * HEAD_DIM
        start = low // LANES * LANES
        stop = min(-(-(low + HEAD_DIM) // LANES) * LANES, inner)
        windows.append((start, stop, low - start))
    return windows


def own_lanes(window):
    start, stop, offset = window
    lane = lax.broadcasted_iota(jnp.int32, (1, stop - start), 1)
    return (lane >= offset) & (lane < offset + HEAD_DIM)


def only(lanes, rows):
    return jnp.where(lanes, rows, jnp.zeros((), rows.dtype))


def lane_tiles(inner):
    return [(low, min(low + LANES, inner)) for low in range(0, inner, LANES)]


def combine(inner, factors, rows):
    pieces = []
    for low, high in lane_tiles(inner):
        lane = low + lax.broadcasted_iota(jnp.int32, (1, high - low), 1)
        total = None
        for head, factor in enumerate(factors):
            start, stop = head * HEAD_DIM, (head + 1) * HEAD_DIM
            if stop <= low or start >= high:
                continue
            own = only((lane >= start) & (lane < stop), rows[:, low:high])
            part = lax.dot_general(
                factor[0], own, (((factor[1],), (0,)), ((), ())), preferred_element_type=F32
            )
            total = part if total is None else total + part
        pieces.append(total)
    return jnp.concatenate(pieces, axis=1)


def head_logits(query, key, allowed):
    logits = []
    for window in head_windows(query.shape[1]):
        start, stop, _ = window
        own = only(own_lanes(window), key[:, start:stop])
        logits.append(dot_nt(query[:, start:stop], own))
    return logits


def softmax_rows(logits, allowed):
    logits = jnp.where(allowed, logits * (1.0 / math.sqrt(HEAD_DIM)), NEGATIVE)
    powers = jnp.exp(logits - jnp.max(logits, axis=1, keepdims=True))
    return powers * (1.0 / jnp.sum(powers, axis=1, keepdims=True))


def attend_heads(query, key, value, allowed):
    logits = head_logits(query, key, allowed)
    probs = [softmax_rows(one, allowed).astype(BF16) for one in logits]
    return combine(query.shape[1], [(one, 1) for one in probs], value)


def attend_heads_back(query, key, value, out, out_grad, allowed):
    inner = query.shape[1]
    factor = 1.0 / math.sqrt(HEAD_DIM)
    logits = head_logits(query, key, allowed)
    slopes, deltas = [], []
    for window in head_windows(inner):
        start, stop, _ = window
        own = only(own_lanes(window), out_grad[:, start:stop])
        slopes.append(dot_nt(own, value[:, start:stop]))
        product = own.astype(F32) * out[:, start:stop].astype(F32)
        deltas.append(jnp.sum(product, axis=1, keepdims=True))
    halves, grads = [], []
    for one, slope, delta in zip(logits, slopes, deltas):
        probs = softmax_rows(one, allowed)
        halves.append(probs.astype(BF16))
        grads.append((probs * (slope - delta)).astype(BF16))
    q_grad = combine(inner, [(one, 1) for one in grads], key) * factor
    k_grad = combine(inner, [(one, 0) for one in grads], query) * factor
    v_grad = combine(inner, [(one, 0) for one in halves], out_grad)
    return jnp.concatenate(
        [q_grad.astype(BF16), k_grad.astype(BF16), v_grad.astype(BF16)], axis=1
    )


def slot_masks(info_ref, rows, slots):
    frames, limit, first = info_ref[0], info_ref[1], info_ref[2]
    group = pl.program_id(0)
    row = lax.broadcasted_iota(jnp.int32, (rows, 1), 0)
    slot = first + group * slots + row % slots
    token = (row // slots < frames) & (slot < limit)
    col = lax.broadcasted_iota(jnp.int32, (1, rows), 1)
    allowed = (row % slots == col % slots) & (col // slots < frames)
    return token.astype(F32), allowed


def normalised(mixed):
    values = mixed.astype(F32)
    centred = values - jnp.mean(values, axis=1, keepdims=True)
    inv_std = lax.rsqrt(jnp.mean(centred * centred, axis=1, keepdims=True) + EPSILON)
    return centred * inv_std, inv_std


def temporal_forward(
    info, mod, stream, out_s, w_spatial, w_qkv, mixed_ref, mod_ref, qkv_ref, out_ref, slots
):
    rows, width = mod_ref.shape[1:]
    inner = out_s.shape[-1]
    token, allowed = slot_masks(info, rows, slots)
    branch = dot_nt(out_s[...].reshape(rows, inner), w_spatial[...])
    mixed = (stream[...].reshape(rows, width).astype(F32) + token * branch).astype(BF16)
    mixed_ref[...] = mixed.reshape(mixed_ref.shape)
    normed, _ = normalised(mixed)
    modulated = (normed * (1.0 + mod[0, 1:2]) + mod[0, 0:1]).astype(BF16)
    mod_ref[...] = modulated.reshape(mod_ref.shape)
    qkv = dot_nt(modulated, w_qkv[...]).astype(BF16)
    qkv_ref[...] = qkv.reshape(qkv_ref.shape)
    out = attend_heads(qkv[:, :inner], qkv[:, inner : 2 * inner], qkv[:, 2 * inner :], allowed)
    out_ref[...] = out.astype(BF16).reshape(out_ref.shape)


def temporal_backward(
    info, mod, grad, mixed, out_s, qkv_ref, out_t, modulated, w_temporal, w_qkv, ln_ref,
    wide_keep, pair_keep, wide_send, pair_send, left_s, left_t, left_q, right_s, right_t, right_q, slots, y_count,
):
    rows, width = modulated.shape[1:]
    inner = out_s.shape[-1]
    token, allowed = slot_masks(info, rows, slots)

    grad_f = grad[...].reshape(rows, width).astype(F32)
    branch_grad = (token * mod[0, 2:3] * grad_f).astype(BF16)
    out_grad = dot_nn(branch_grad, w_temporal[...]).astype(BF16)
    qkv = qkv_ref[...].reshape(rows, 3 * inner)
    out = out_t[...].reshape(rows, inner)
    dqkv = attend_heads_back(
        qkv[:, :inner], qkv[:, inner : 2 * inner], qkv[:, 2 * inner :], out, out_grad, allowed
    )

    norm_grad = dot_nn(dqkv, w_qkv[...]) * (1.0 + mod[0, 1:2])
    normed, inv_std = normalised(mixed[...].reshape(rows, width))
    first = jnp.mean(norm_grad, axis=1, keepdims=True)
    second = jnp.mean(norm_grad * normed, axis=1, keepdims=True)
    ln_grad = (inv_std * (norm_grad - first - normed * second)).astype(BF16)
    ln_ref[...] = ln_grad.reshape(ln_ref.shape)
    hidden_grad = (grad_f + ln_grad.astype(F32)).astype(BF16)
    spatial_grad = (token * hidden_grad.astype(F32)).astype(BF16)

    step = width // (2 * y_count)
    normal = modulated[...].reshape(rows, width)
    place = pl.ds(pl.program_id(0) * rows, rows)
    left_s[place, :] = out_s[...].reshape(rows, inner)
    left_t[place, :] = out
    left_q[place, :] = dqkv
    right_s[place, :] = spatial_grad
    right_t[place, :] = branch_grad
    for c in range(2):
        pieces = [normal[:, (2 * y + c) * step : (2 * y + c + 1) * step] for y in range(y_count)]
        right_q[c, place, :] = jnp.concatenate(pieces, axis=1)

    @pl.when(pl.program_id(0) == pl.num_programs(0) - 1)
    def _():
        core = info[4]
        for side, out in ((core, wide_keep), (1 - core, wide_send)):
            store_wide(dot_tn(left_q[...], right_q[side]), out)
        sum_s = dot_tn(left_s[...], right_s[...])
        sum_t = dot_tn(left_t[...], right_t[...])
        for keeper in range(2):

            @pl.when(core == keeper)
            def _():
                store_pair(sum_s, sum_t, keeper, pair_keep)
                store_pair(sum_s, sum_t, 1 - keeper, pair_send)


def term_rows(inner, width, y_count, x_count):
    tiles = -(-(width // 2) // LANES)
    return tiles * (3 * inner // x_count), width // LANES * (inner // y_count)


def store_wide(total, out):
    x_count, rows, _ = out.shape
    span = total.shape[0] // x_count
    for tile in range(rows // span):
        block = total[:, tile * LANES : (tile + 1) * LANES]
        if block.shape[1] < LANES:
            rest = jnp.zeros((block.shape[0], LANES - block.shape[1]), F32)
            block = jnp.concatenate([block, rest], axis=1)
        for x in range(x_count):
            piece = block[x * span : (x + 1) * span]
            out[x, tile * span : (tile + 1) * span] = piece.astype(BF16)


def store_pair(sum_s, sum_t, core, out):
    y_count = out.shape[0]
    inner, width = sum_s.shape
    step = inner // (2 * y_count)
    for y in range(y_count):
        place = (2 * y + core) * step
        for tile in range(width // LANES):
            lanes = slice(tile * LANES, (tile + 1) * LANES)
            parts = [sum_s[place : place + step, lanes], sum_t[place : place + step, lanes]]
            block = jnp.concatenate(parts, axis=0).astype(BF16)
            out[y, tile * 2 * step : (tile + 1) * 2 * step] = block


def frame_keys(info_ref, rows):
    return lax.broadcasted_iota(jnp.int32, (1, rows), 1) < info_ref[1]


def frame_tokens(info_ref, rows):
    row = lax.broadcasted_iota(jnp.int32, (rows, 1), 0)
    alive = info_ref[3] + pl.program_id(0) < info_ref[0]
    return ((row < info_ref[1]) & alive).astype(F32)


def spatial_forward(info, qkv_ref, out_ref):
    rows, inner = out_ref.shape[1:]
    qkv = qkv_ref[0]
    out = attend_heads(
        qkv[:, :inner], qkv[:, inner : 2 * inner], qkv[:, 2 * inner :], frame_keys(info, rows)
    )
    out_ref[0] = out.astype(BF16)


def block_forward(info, mod, stream, out_s, out_t, w_spatial, w_temporal, block_ref):
    rows = stream.shape[1]
    token = frame_tokens(info, rows)
    spatial = dot_nt(out_s[0], w_spatial[...])
    mixed = (stream[0].astype(F32) + token * spatial).astype(BF16)
    branch = dot_nt(out_t[0], w_temporal[...])
    block_ref[0] = (mixed.astype(F32) + token * mod[0, 2:3] * branch).astype(BF16)


def spatial_backward(
    info, grad, ln_grad, qkv_ref, out_s, w_spatial, hidden_ref, dqkv_ref
):
    rows, inner = out_s.shape[1:]
    hidden_grad = (grad[0].astype(F32) + ln_grad[0].astype(F32)).astype(BF16)
    hidden_ref[0] = hidden_grad
    branch_grad = (frame_tokens(info, rows) * hidden_grad.astype(F32)).astype(BF16)
    out_grad = dot_nn(branch_grad, w_spatial[...]).astype(BF16)
    qkv = qkv_ref[0]
    dqkv_ref[0] = attend_heads_back(
        qkv[:, :inner], qkv[:, inner : 2 * inner], qkv[:, 2 * inner :], out_s[0], out_grad,
        frame_keys(info, rows),
    )


def whole(array):
    return pl.BlockSpec(
        array.shape, lambda step: (0,) * array.ndim, pipeline_mode=pl.Buffered(1)
    )


def per_frame(array):
    return pl.BlockSpec((1,) + array.shape[1:], lambda step: (step, 0, 0))


def per_group(array):
    return pl.BlockSpec(
        (array.shape[0], 1) + array.shape[2:], lambda step: (0, step, 0, 0)
    )


SCALARS = pl.BlockSpec(memory_space=pltpu.SMEM)


def run(body, steps, operands, specs, results, result_specs, scratch):
    return pl.pallas_call(
        body,
        grid=(steps,),
        in_specs=specs,
        out_specs=result_specs,
        out_shape=results,
        scratch_shapes=scratch,
        compiler_params=pltpu.CompilerParams(vmem_limit_bytes=VMEM_BYTES),
        cost_estimate=pl.CostEstimate(flops=1, bytes_accessed=1, transcendentals=0),
    )(*operands)


def shape_of(*dims, dtype=BF16):
    return jax.ShapeDtypeStruct(dims, dtype)


def exchange(rows, axes):
    return lax.all_to_all(rows, axes, 0, 0, tiled=True)


def shift(rows, axis, hops):
    count = lax.axis_size(axis)
    return lax.ppermute(rows, axis, [(at, (at + hops) % count) for at in range(count)])


def shift_both(rows, axis, hops):
    count = lax.axis_size(axis)
    pairs = []
    for at in range(count):
        pairs.append((2 * at, 2 * ((at - hops) % count)))
        pairs.append((2 * at + 1, 2 * ((at + hops) % count) + 1))
    return lax.ppermute(rows, (axis, "c"), pairs)


def swap(rows):
    return shift(rows, "c", 1)


def place_along_z(
    info, own, near, mid, far, last, near_p, mid_p, far_p, onward, kept, stack, flat, cut
):
    place, count = info[1], stack.shape[0]
    sign = 1 - 2 * info[3]
    stack[place] = own[...]
    stack[lax.rem(place + count // 2, count)] = last[...]
    for hops, mine, other in ((1, near, near_p), (2, mid, mid_p), (3, far, far_p)):
        stack[lax.rem(place + sign * hops + count, count)] = mine[...]
        stack[lax.rem(place - sign * hops + count, count)] = other[...]

    inner = flat.shape[1] // 2
    step = stack.shape[1] - 2 * cut
    for z in range(count):
        block = stack[z].astype(F32)
        side = 2 * z // count
        for number in range(2):
            for part in range(2):
                row = (2 * number * count + 4 * (z % (count // 2)) + 2 * part) * cut // 2
                flat[row : row + cut, side * inner : (side + 1) * inner] = block[
                    number * cut : (number + 1) * cut, part * inner : (part + 1) * inner
                ]
        row = 2 * count * cut + z * step
        flat[row : row + step] = block[2 * cut :]
    size = flat.shape[0] // 2
    lower, upper = flat[:size].astype(BF16), flat[size:].astype(BF16)

    @pl.when(info[3] == 0)
    def _():
        onward[...] = lower
        kept[...] = upper

    @pl.when(info[3] != 0)
    def _():
        onward[...] = upper
        kept[...] = lower


def place_along_x(
    info, own, own_k, near, near_k, near_p, near_pk, part, part_p, spatial, temporal, wide, out
):
    place, count = info[0], out.shape[0]
    half = part.shape[0]
    opposite = lax.rem(place + count // 2, count)

    def fill(index, first, second):
        out[index, :half] = first[...]
        out[index, half:] = second[...]

    @pl.when(info[3] == 0)
    def _():
        fill(place, own, own_k)
        fill(lax.rem(place + 1, count), near, near_k)
        fill(lax.rem(place - 1 + count, count), near_pk, near_p)
        fill(opposite, part, part_p)

    @pl.when(info[3] != 0)
    def _():
        fill(place, own_k, own)
        fill(lax.rem(place - 1 + count, count), near_k, near)
        fill(lax.rem(place + 1, count), near_p, near_pk)
        fill(opposite, part_p, part)

    cut, inner = out.shape[2] // count // 2, out.shape[2] // 2
    span = wide.shape[0] // count
    for x in range(count):
        for number, result in ((0, spatial), (1, temporal)):
            block = out[x, number * cut : (number + 1) * cut]
            result[2 * x * cut : (2 * x + 1) * cut] = block[:, :inner]
            result[(2 * x + 1) * cut : (2 * x + 2) * cut] = block[:, inner:]
        wide[x * span : (x + 1) * span] = out[x, 2 * cut :]


def in_vmem(body, info, blocks, results, scratch=()):
    vmem = pl.BlockSpec(memory_space=pltpu.VMEM)
    return pl.pallas_call(
        body,
        in_specs=[SCALARS] + [vmem] * len(blocks),
        out_specs=jax.tree.map(lambda _: vmem, results),
        out_shape=results,
        scratch_shapes=list(scratch),
        cost_estimate=pl.CostEstimate(flops=1, bytes_accessed=1, transcendentals=0),
        compiler_params=pltpu.CompilerParams(vmem_limit_bytes=VMEM_BYTES),
    )(info, *blocks)


def tie(*values):
    return lax.optimization_barrier(values)


def near_rows(out_spatial, qkv_temporal, out_temporal):
    half, narrow = out_spatial.shape
    packed = jnp.concatenate(
        [jnp.concatenate([out_spatial.T, out_temporal.T], axis=1), qkv_temporal.T], axis=0
    )
    near = jnp.transpose(lax.all_gather(packed, ("y", "c"), axis=0, tiled=False), (1, 0, 2))
    thin = near[:narrow, :, :half].reshape(narrow, -1)
    other = near[:narrow, :, half:].reshape(narrow, -1)
    wide = near[narrow:].reshape(near.shape[0] - narrow, -1)
    return (fold(thin), wide, fold(other))


def fold(rows):
    cut = rows.shape[-2] // 2
    return jnp.concatenate([rows[..., :cut, :], rows[..., cut:, :]], axis=-1)


def unfold(rows):
    cut = rows.shape[-1] // 2
    return jnp.concatenate([rows[..., :cut], rows[..., cut:]], axis=-2)


def gather_z(coords, rows, cut, beside):
    arrived = [shift_both(rows, "z", hops) for hops in (2, 1, 3)]
    arrived = [arrived[1], arrived[0], arrived[2], shift_both(arrived[0], "z", 2)]
    arrived, beside = tie(arrived, beside)
    swapped = [swap(block) for block in arrived[:3]]
    count, width = lax.axis_size("z"), rows.shape[1]
    half = shape_of(count * rows.shape[0] // 2, width)
    halves = in_vmem(
        functools.partial(place_along_z, cut=cut),
        coords,
        [rows] + arrived + swapped,
        (half, half),
        [pltpu.VMEM((count,) + rows.shape, BF16), pltpu.VMEM((2 * half.shape[0], width), F32)],
    )
    return halves, beside


def scatter(blocks, axis):
    count, place = lax.axis_size(axis), lax.axis_index(axis)
    arrived = []
    for hops in range(1, count):
        block = lax.dynamic_index_in_dim(blocks, (place + hops) % count, 0, keepdims=False)
        arrived.append(shift(block, axis, hops))
    return arrived


def halves_summed(keep, send):
    return (keep.astype(F32) + swap(send).astype(F32)).astype(BF16)


def spread(blocks, place, turned, outs):
    count = len(blocks)
    for index, block in enumerate(blocks):
        turned[lax.rem(index - place + count, count)] = block.astype(BF16)
    for hops, out in enumerate(outs):
        out[...] = turned[hops]


def regroup_wide(info, blocks, first, second, third, *outs):
    outs, turned = outs[:-1], outs[-1]
    y_count, span, lanes = turned.shape
    total = blocks[info[0]].astype(F32)
    for block in (first, second, third):
        total = total + block[...].astype(F32)
    tiles = [total[at : at + span] for at in range(0, total.shape[0], span)]
    flat = jnp.concatenate(tiles, axis=1)
    step = (flat.shape[1] - LANES // 2) // y_count
    rest = jnp.zeros((span, lanes - step), F32)
    cuts = [flat[:, y * step : (y + 1) * step] for y in range(y_count)]
    spread([jnp.concatenate([one, rest], axis=1) for one in cuts], info[2], turned, outs)


def regroup_pair(info, blocks, first, second, third, *outs):
    outs, turned = outs[:-1], outs[-1]
    x_count, span, lanes = turned.shape
    total = blocks[info[2]].astype(F32)
    for block in (first, second, third):
        total = total + block[...].astype(F32)
    width = x_count * span
    step = total.shape[0] // (width // LANES)
    tiles = [total[at : at + step].T for at in range(0, total.shape[0], step)]
    flat = jnp.concatenate(tiles, axis=0)
    flat = jnp.concatenate([flat, jnp.zeros((width, lanes - step), F32)], axis=1)
    cuts = [flat[x * span : (x + 1) * span] for x in range(x_count)]
    spread(cuts, info[0], turned, outs)


def regrouped(body, coords, blocks, arrived, span, count):
    one = shape_of(span, 2 * LANES)
    turned = pltpu.VMEM((count, span, 2 * LANES), BF16)
    return in_vmem(body, coords, [blocks] + arrived, (one,) * count, [turned])


def send_ahead(blocks, axis):
    return [shift(block, axis, hops + 1) for hops, block in enumerate(blocks[1:])]


def added(own, arrived):
    total = own.astype(F32)
    for block in arrived:
        total = total + block.astype(F32)
    return total.astype(BF16)


def reduce_grads(coords, wide, pair, inner, width, beside):
    x_count, y_count, z_count = (lax.axis_size(axis) for axis in ("x", "y", "z"))
    arrived, pair_in, beside = tie(scatter(wide, "x"), scatter(pair, "y"), beside)
    wide = regrouped(regroup_wide, coords, wide, arrived, 3 * inner // x_count, y_count)
    pair = regrouped(regroup_pair, coords, pair, pair_in, width // x_count, x_count)
    wide = added(wide[0], send_ahead(wide, "y")).reshape(z_count, -1, 2 * LANES)
    pair = added(pair[0], send_ahead(pair, "x")).reshape(z_count, -1, 2 * LANES)
    step = width // (2 * y_count)
    total = jnp.sum(exchange(jnp.concatenate([pair, wide], axis=1), "z").astype(F32), axis=0)
    narrow = pair.shape[1]
    half = step // 2
    summed = (total[:narrow, :half].T, total[narrow:, :step].T, total[:narrow, half:step].T)
    return summed, beside


def on_device(
    hidden,
    spatial_qkv,
    out_spatial,
    qkv_temporal,
    out_temporal,
    modulation,
    cotangent,
    frame_count,
    patch_height,
    patch_width,
):
    seq_count = lax.axis_size(("y", "c"))
    seq_place = lax.axis_index(("y", "c"))
    y_count = lax.axis_size("y")
    stream = hidden[0]
    grad_out = cotangent[0]
    packed_qkv = spatial_qkv[0]
    frame_dev, slot_total, width = stream.shape
    slot_dev = slot_total // seq_count
    inner = out_spatial.shape[0] * seq_count
    slots = 8
    groups = slot_dev // slots
    rows = frame_dev * seq_count * slots
    coords = jnp.stack([lax.axis_index(name) for name in ("x", "z", "y", "c")]).astype(jnp.int32)
    info = jnp.stack(
        [
            frame_count[0],
            patch_height[0] * patch_width[0],
            seq_place * slot_dev,
            seq_place * frame_dev,
            coords[3],
        ]
    ).astype(jnp.int32)

    def to_slots(tokens):
        split = tokens.reshape(frame_dev, seq_count, groups, slots, -1)
        split = jnp.transpose(split, (1, 2, 0, 3, 4))
        return exchange(split.reshape(seq_count, groups, frame_dev * slots, -1), ("y", "c"))

    def to_frames(tokens):
        moved = exchange(tokens, ("y", "c")).reshape(seq_count, groups, frame_dev, slots, -1)
        return jnp.transpose(moved, (2, 0, 1, 3, 4)).reshape(frame_dev, slot_total, -1)

    out_s = shape_of(frame_dev, slot_total, inner)
    out_s = run(
        spatial_forward,
        frame_dev,
        [info, packed_qkv],
        [SCALARS, per_frame(packed_qkv)],
        out_s,
        per_frame(out_s),
        [],
    )
    thin, wide, other = near_rows(out_spatial, qkv_temporal, out_temporal)
    rows_z = jnp.concatenate([thin, other, wide], axis=0)
    cut = thin.shape[0]
    stream_tied, _ = tie(stream, rows_z)
    stream_s = to_slots(stream_tied)
    (onward, kept), (stream_s, out_s) = gather_z(coords, rows_z, cut, (stream_s, out_s))
    grad_tied, _ = tie(grad_out, stream_s)
    grad_s = to_slots(grad_tied)
    onward, kept, grad_s = tie(onward, kept, grad_s)
    out_s_tied, _ = tie(out_s, grad_s)
    out_s_s = to_slots(out_s_tied)

    first, out_s_s = tie(shift_both(onward, "x", 1), out_s_s)
    first_k = shift_both(kept, "x", 1)
    second = shift_both(first, "x", 1)
    x_count = lax.axis_size("x")
    w_spatial, w_temporal, w_qkv = in_vmem(
        place_along_x,
        coords,
        [onward, kept, first, first_k, swap(first), swap(first_k), second, swap(second)],
        (shape_of(width, inner), shape_of(width, inner), shape_of(3 * inner, width)),
        [pltpu.VMEM((x_count, 2 * onward.shape[0], width), BF16)],
    )

    result = (
        shape_of(groups, rows, width),
        shape_of(groups, rows, width),
        shape_of(groups, rows, 3 * inner),
        shape_of(seq_count, groups, rows // seq_count, inner),
    )
    mixed_s, modulated, qkv_t, out_t = run(
        functools.partial(temporal_forward, slots=slots),
        groups,
        [info, modulation, stream_s, out_s_s, w_spatial, w_qkv],
        [SCALARS, whole(modulation), per_group(stream_s), per_group(out_s_s), whole(w_spatial), whole(w_qkv)],
        result,
        [per_frame(result[0]), per_frame(result[1]), per_frame(result[2]), per_group(result[3])],
        [],
    )
    out_t_f = to_frames(out_t)

    wide_rows, pair_rows = term_rows(inner, width, y_count, x_count)
    result = (
        shape_of(seq_count, groups, rows // seq_count, width),
        shape_of(x_count, wide_rows, LANES),
        shape_of(y_count, pair_rows, LANES),
        shape_of(x_count, wide_rows, LANES),
        shape_of(y_count, pair_rows, LANES),
    )
    tokens = groups * rows
    kept = [(inner,), (inner,), (3 * inner,), (width,), (width,)]
    kept = [pltpu.VMEM((tokens,) + shape, BF16) for shape in kept]
    kept.append(pltpu.VMEM((2, tokens, width // 2), BF16))
    ln_grad, wide_keep, pair_keep, wide_send, pair_send = run(
        functools.partial(temporal_backward, slots=slots, y_count=y_count),
        groups,
        [info, modulation, grad_s, mixed_s, out_s_s, qkv_t, out_t, modulated, w_temporal, w_qkv],
        [
            SCALARS,
            whole(modulation),
            per_group(grad_s),
            per_frame(mixed_s),
            per_group(out_s_s),
            per_frame(qkv_t),
            per_group(out_t),
            per_frame(modulated),
            whole(w_temporal),
            whole(w_qkv),
        ],
        result,
        [per_group(result[0])] + [whole(part) for part in result[1:]],
        kept,
    )
    wide_send, out_t_f = tie(wide_send, out_t_f)
    wide = halves_summed(wide_keep, wide_send)
    pair = halves_summed(pair_keep, pair_send)
    ln_frames = to_frames(ln_grad)

    result = (shape_of(frame_dev, slot_total, width), shape_of(frame_dev, slot_total, 3 * inner))
    hidden_grad, qkv_s_grad = run(
        spatial_backward,
        frame_dev,
        [info, grad_out, ln_frames, packed_qkv, out_s, w_spatial],
        [
            SCALARS,
            per_frame(grad_out),
            per_frame(ln_frames),
            per_frame(packed_qkv),
            per_frame(out_s),
            whole(w_spatial),
        ],
        result,
        [per_frame(result[0]), per_frame(result[1])],
        [],
    )
    summed, qkv_s_grad = reduce_grads(coords, wide, pair, inner, width, qkv_s_grad)
    block_out = shape_of(frame_dev, slot_total, width)
    block_out = run(
        block_forward,
        frame_dev,
        [info, modulation, stream, out_s, out_t_f, w_spatial, w_temporal],
        [
            SCALARS,
            whole(modulation),
            per_frame(stream),
            per_frame(out_s),
            per_frame(out_t_f),
            whole(w_spatial),
            whole(w_temporal),
        ],
        block_out,
        per_frame(block_out),
        [],
    )
    return (block_out[None], hidden_grad[None], qkv_s_grad[None], summed[0], summed[1], summed[2])


def solution(mesh):
    torus = Mesh(mesh.devices.reshape(4, 8, 4, 2), ("x", "z", "y", "c"))
    dp, seq = ("x", "z"), ("y", "c")
    tokens = P(dp, seq, None, None)
    weight = P(seq, dp)
    placed = (
        tokens,
        tokens,
        weight,
        weight,
        weight,
        P(dp, None, None),
        tokens,
        P(dp),
        P(dp),
        P(dp),
    )
    return jax.shard_map(
        on_device,
        mesh=torus,
        in_specs=placed,
        out_specs=(tokens, tokens, tokens, weight, weight, weight),
        check_vma=False,
    )
```

```python
import functools
import math

import jax
import jax.numpy as jnp
from jax import lax
from jax.experimental import pallas as pl
from jax.experimental.pallas import tpu as pltpu
from jax.sharding import Mesh
from jax.sharding import PartitionSpec as P

HEAD_DIM = 72
EPSILON = 1e-06
NEGATIVE = -1e30
LANES = 128
VMEM_BYTES = 56 * 1024 * 1024
F32 = jnp.float32
BF16 = jnp.bfloat16


def dot_nn(left, right):
    return lax.dot_general(left, right, (((1,), (0,)), ((), ())), preferred_element_type=F32)


def dot_nt(left, right):
    return lax.dot_general(left, right, (((1,), (1,)), ((), ())), preferred_element_type=F32)


def dot_tn(left, right):
    return lax.dot_general(left, right, (((0,), (0,)), ((), ())), preferred_element_type=F32)


def head_windows(inner):
    windows = []
    for head in range(inner // HEAD_DIM):
        low = head * HEAD_DIM
        start = low // LANES * LANES
        stop = min(-(-(low + HEAD_DIM) // LANES) * LANES, inner)
        windows.append((start, stop, low - start))
    return windows


def own_lanes(window):
    start, stop, offset = window
    lane = lax.broadcasted_iota(jnp.int32, (1, stop - start), 1)
    return (lane >= offset) & (lane < offset + HEAD_DIM)


def only(lanes, rows):
    return jnp.where(lanes, rows, jnp.zeros((), rows.dtype))


def lane_tiles(inner):
    return [(low, min(low + LANES, inner)) for low in range(0, inner, LANES)]


def combine(inner, factors, rows):
    pieces = []
    for low, high in lane_tiles(inner):
        lane = low + lax.broadcasted_iota(jnp.int32, (1, high - low), 1)
        total = None
        for head, factor in enumerate(factors):
            start, stop = head * HEAD_DIM, (head + 1) * HEAD_DIM
            if stop <= low or start >= high:
                continue
            own = only((lane >= start) & (lane < stop), rows[:, low:high])
            part = lax.dot_general(
                factor[0], own, (((factor[1],), (0,)), ((), ())), preferred_element_type=F32
            )
            total = part if total is None else total + part
        pieces.append(total)
    return jnp.concatenate(pieces, axis=1)


def head_logits(query, key, allowed):
    logits = []
    for window in head_windows(query.shape[1]):
        start, stop, _ = window
        own = only(own_lanes(window), key[:, start:stop])
        logits.append(dot_nt(query[:, start:stop], own))
    return logits


def softmax_rows(logits, allowed):
    logits = jnp.where(allowed, logits * (1.0 / math.sqrt(HEAD_DIM)), NEGATIVE)
    powers = jnp.exp(logits - jnp.max(logits, axis=1, keepdims=True))
    return powers * (1.0 / jnp.sum(powers, axis=1, keepdims=True))


def attend_heads(query, key, value, allowed):
    logits = head_logits(query, key, allowed)
    probs = [softmax_rows(one, allowed).astype(BF16) for one in logits]
    return combine(query.shape[1], [(one, 1) for one in probs], value)


def attend_heads_back(query, key, value, out, out_grad, allowed):
    inner = query.shape[1]
    factor = 1.0 / math.sqrt(HEAD_DIM)
    logits = head_logits(query, key, allowed)
    slopes, deltas = [], []
    for window in head_windows(inner):
        start, stop, _ = window
        own = only(own_lanes(window), out_grad[:, start:stop])
        slopes.append(dot_nt(own, value[:, start:stop]))
        product = own.astype(F32) * out[:, start:stop].astype(F32)
        deltas.append(jnp.sum(product, axis=1, keepdims=True))
    halves, grads = [], []
    for one, slope, delta in zip(logits, slopes, deltas):
        probs = softmax_rows(one, allowed)
        halves.append(probs.astype(BF16))
        grads.append((probs * (slope - delta)).astype(BF16))
    q_grad = combine(inner, [(one, 1) for one in grads], key) * factor
    k_grad = combine(inner, [(one, 0) for one in grads], query) * factor
    v_grad = combine(inner, [(one, 0) for one in halves], out_grad)
    return jnp.concatenate(
        [q_grad.astype(BF16), k_grad.astype(BF16), v_grad.astype(BF16)], axis=1
    )


def slot_masks(info_ref, rows, slots):
    frames, limit, first = info_ref[0], info_ref[1], info_ref[2]
    group = pl.program_id(0)
    row = lax.broadcasted_iota(jnp.int32, (rows, 1), 0)
    slot = first + group * slots + row % slots
    token = (row // slots < frames) & (slot < limit)
    col = lax.broadcasted_iota(jnp.int32, (1, rows), 1)
    allowed = (row % slots == col % slots) & (col // slots < frames)
    return token.astype(F32), allowed


def normalised(mixed):
    values = mixed.astype(F32)
    centred = values - jnp.mean(values, axis=1, keepdims=True)
    inv_std = lax.rsqrt(jnp.mean(centred * centred, axis=1, keepdims=True) + EPSILON)
    return centred * inv_std, inv_std


def temporal_forward(
    info, mod, stream, out_s, w_spatial, w_qkv, mixed_ref, mod_ref, qkv_ref, out_ref, slots
):
    rows, width = mod_ref.shape[1:]
    inner = out_s.shape[-1]
    token, allowed = slot_masks(info, rows, slots)
    branch = dot_nt(out_s[...].reshape(rows, inner), w_spatial[...])
    mixed = (stream[...].reshape(rows, width).astype(F32) + token * branch).astype(BF16)
    mixed_ref[...] = mixed.reshape(mixed_ref.shape)
    normed, _ = normalised(mixed)
    modulated = (normed * (1.0 + mod[0, 1:2]) + mod[0, 0:1]).astype(BF16)
    mod_ref[...] = modulated.reshape(mod_ref.shape)
    qkv = dot_nt(modulated, w_qkv[...]).astype(BF16)
    qkv_ref[...] = qkv.reshape(qkv_ref.shape)
    out = attend_heads(qkv[:, :inner], qkv[:, inner : 2 * inner], qkv[:, 2 * inner :], allowed)
    out_ref[...] = out.astype(BF16).reshape(out_ref.shape)


def temporal_backward(
    info, mod, grad, mixed, out_s, qkv_ref, out_t, modulated, w_temporal, w_qkv, ln_ref,
    wide_keep, pair_keep, wide_send, pair_send, left_s, left_t, left_q, right_s, right_t, right_q, slots, y_count,
):
    rows, width = modulated.shape[1:]
    inner = out_s.shape[-1]
    token, allowed = slot_masks(info, rows, slots)

    grad_f = grad[...].reshape(rows, width).astype(F32)
    branch_grad = (token * mod[0, 2:3] * grad_f).astype(BF16)
    out_grad = dot_nn(branch_grad, w_temporal[...]).astype(BF16)
    qkv = qkv_ref[...].reshape(rows, 3 * inner)
    out = out_t[...].reshape(rows, inner)
    dqkv = attend_heads_back(
        qkv[:, :inner], qkv[:, inner : 2 * inner], qkv[:, 2 * inner :], out, out_grad, allowed
    )

    norm_grad = dot_nn(dqkv, w_qkv[...]) * (1.0 + mod[0, 1:2])
    normed, inv_std = normalised(mixed[...].reshape(rows, width))
    first = jnp.mean(norm_grad, axis=1, keepdims=True)
    second = jnp.mean(norm_grad * normed, axis=1, keepdims=True)
    ln_grad = (inv_std * (norm_grad - first - normed * second)).astype(BF16)
    ln_ref[...] = ln_grad.reshape(ln_ref.shape)
    hidden_grad = (grad_f + ln_grad.astype(F32)).astype(BF16)
    spatial_grad = (token * hidden_grad.astype(F32)).astype(BF16)

    step = width // (2 * y_count)
    normal = modulated[...].reshape(rows, width)
    place = pl.ds(pl.program_id(0) * rows, rows)
    left_s[place, :] = out_s[...].reshape(rows, inner)
    left_t[place, :] = out
    left_q[place, :] = dqkv
    right_s[place, :] = spatial_grad
    right_t[place, :] = branch_grad
    for c in range(2):
        pieces = [normal[:, (2 * y + c) * step : (2 * y + c + 1) * step] for y in range(y_count)]
        right_q[c, place, :] = jnp.concatenate(pieces, axis=1)

    @pl.when(pl.program_id(0) == pl.num_programs(0) - 1)
    def _():
        core = info[4]
        for side, out in ((core, wide_keep), (1 - core, wide_send)):
            store_wide(dot_tn(left_q[...], right_q[side]), out)
        sum_s = dot_tn(left_s[...], right_s[...])
        sum_t = dot_tn(left_t[...], right_t[...])
        for keeper in range(2):

            @pl.when(core == keeper)
            def _():
                store_pair(sum_s, sum_t, keeper, pair_keep)
                store_pair(sum_s, sum_t, 1 - keeper, pair_send)


def term_rows(inner, width, y_count, x_count):
    tiles = -(-(width // 2) // LANES)
    return tiles * (3 * inner // x_count), width // LANES * (inner // y_count)


def store_wide(total, out):
    x_count, rows, _ = out.shape
    span = total.shape[0] // x_count
    for tile in range(rows // span):
        block = total[:, tile * LANES : (tile + 1) * LANES]
        if block.shape[1] < LANES:
            rest = jnp.zeros((block.shape[0], LANES - block.shape[1]), F32)
            block = jnp.concatenate([block, rest], axis=1)
        for x in range(x_count):
            piece = block[x * span : (x + 1) * span]
            out[x, tile * span : (tile + 1) * span] = piece.astype(BF16)


def store_pair(sum_s, sum_t, core, out):
    y_count = out.shape[0]
    inner, width = sum_s.shape
    step = inner // (2 * y_count)
    for y in range(y_count):
        place = (2 * y + core) * step
        for tile in range(width // LANES):
            lanes = slice(tile * LANES, (tile + 1) * LANES)
            parts = [sum_s[place : place + step, lanes], sum_t[place : place + step, lanes]]
            block = jnp.concatenate(parts, axis=0).astype(BF16)
            out[y, tile * 2 * step : (tile + 1) * 2 * step] = block


def frame_keys(info_ref, rows):
    return lax.broadcasted_iota(jnp.int32, (1, rows), 1) < info_ref[1]


def frame_tokens(info_ref, rows):
    row = lax.broadcasted_iota(jnp.int32, (rows, 1), 0)
    alive = info_ref[3] + pl.program_id(0) < info_ref[0]
    return ((row < info_ref[1]) & alive).astype(F32)


def spatial_forward(info, qkv_ref, out_ref):
    rows, inner = out_ref.shape[1:]
    qkv = qkv_ref[0]
    out = attend_heads(
        qkv[:, :inner], qkv[:, inner : 2 * inner], qkv[:, 2 * inner :], frame_keys(info, rows)
    )
    out_ref[0] = out.astype(BF16)


def block_forward(info, mod, stream, out_s, out_t, w_spatial, w_temporal, block_ref):
    rows = stream.shape[1]
    token = frame_tokens(info, rows)
    spatial = dot_nt(out_s[0], w_spatial[...])
    mixed = (stream[0].astype(F32) + token * spatial).astype(BF16)
    branch = dot_nt(out_t[0], w_temporal[...])
    block_ref[0] = (mixed.astype(F32) + token * mod[0, 2:3] * branch).astype(BF16)


def spatial_backward(
    info, grad, ln_grad, qkv_ref, out_s, w_spatial, hidden_ref, dqkv_ref
):
    rows, inner = out_s.shape[1:]
    hidden_grad = (grad[0].astype(F32) + ln_grad[0].astype(F32)).astype(BF16)
    hidden_ref[0] = hidden_grad
    branch_grad = (frame_tokens(info, rows) * hidden_grad.astype(F32)).astype(BF16)
    out_grad = dot_nn(branch_grad, w_spatial[...]).astype(BF16)
    qkv = qkv_ref[0]
    dqkv_ref[0] = attend_heads_back(
        qkv[:, :inner], qkv[:, inner : 2 * inner], qkv[:, 2 * inner :], out_s[0], out_grad,
        frame_keys(info, rows),
    )


def whole(array):
    return pl.BlockSpec(
        array.shape, lambda step: (0,) * array.ndim, pipeline_mode=pl.Buffered(1)
    )


def per_frame(array):
    return pl.BlockSpec((1,) + array.shape[1:], lambda step: (step, 0, 0))


def per_group(array):
    return pl.BlockSpec(
        (array.shape[0], 1) + array.shape[2:], lambda step: (0, step, 0, 0)
    )


SCALARS = pl.BlockSpec(memory_space=pltpu.SMEM)


def run(body, steps, operands, specs, results, result_specs, scratch):
    return pl.pallas_call(
        body,
        grid=(steps,),
        in_specs=specs,
        out_specs=result_specs,
        out_shape=results,
        scratch_shapes=scratch,
        compiler_params=pltpu.CompilerParams(vmem_limit_bytes=VMEM_BYTES),
        cost_estimate=pl.CostEstimate(flops=1, bytes_accessed=1, transcendentals=0),
    )(*operands)


def shape_of(*dims, dtype=BF16):
    return jax.ShapeDtypeStruct(dims, dtype)


def exchange(rows, axes):
    return lax.all_to_all(rows, axes, 0, 0, tiled=True)


def shift(rows, axis, hops):
    count = lax.axis_size(axis)
    return lax.ppermute(rows, axis, [(at, (at + hops) % count) for at in range(count)])


def shift_both(rows, axis, hops):
    count = lax.axis_size(axis)
    pairs = []
    for at in range(count):
        pairs.append((2 * at, 2 * ((at - hops) % count)))
        pairs.append((2 * at + 1, 2 * ((at + hops) % count) + 1))
    return lax.ppermute(rows, (axis, "c"), pairs)


def swap(rows):
    return shift(rows, "c", 1)


def place_along_z(
    info, own, near, mid, far, last, near_p, mid_p, far_p, onward, kept, stack, flat, cut
):
    place, count = info[1], stack.shape[0]
    sign = 1 - 2 * info[3]
    stack[place] = own[...]
    stack[lax.rem(place + count // 2, count)] = last[...]
    for hops, mine, other in ((1, near, near_p), (2, mid, mid_p), (3, far, far_p)):
        stack[lax.rem(place + sign * hops + count, count)] = mine[...]
        stack[lax.rem(place - sign * hops + count, count)] = other[...]

    inner = flat.shape[1] // 2
    step = stack.shape[1] - 2 * cut
    for z in range(count):
        block = stack[z].astype(F32)
        side = 2 * z // count
        for number in range(2):
            for part in range(2):
                row = (2 * number * count + 4 * (z % (count // 2)) + 2 * part) * cut // 2
                flat[row : row + cut, side * inner : (side + 1) * inner] = block[
                    number * cut : (number + 1) * cut, part * inner : (part + 1) * inner
                ]
        row = 2 * count * cut + z * step
        flat[row : row + step] = block[2 * cut :]
    size = flat.shape[0] // 2
    lower, upper = flat[:size].astype(BF16), flat[size:].astype(BF16)

    @pl.when(info[3] == 0)
    def _():
        onward[...] = lower
        kept[...] = upper

    @pl.when(info[3] != 0)
    def _():
        onward[...] = upper
        kept[...] = lower


def place_along_x(
    info, own, own_k, near, near_k, near_p, near_pk, part, part_p, spatial, temporal, wide, out
):
    place, count = info[0], out.shape[0]
    half = part.shape[0]
    opposite = lax.rem(place + count // 2, count)

    def fill(index, first, second):
        out[index, :half] = first[...]
        out[index, half:] = second[...]

    @pl.when(info[3] == 0)
    def _():
        fill(place, own, own_k)
        fill(lax.rem(place + 1, count), near, near_k)
        fill(lax.rem(place - 1 + count, count), near_pk, near_p)
        fill(opposite, part, part_p)

    @pl.when(info[3] != 0)
    def _():
        fill(place, own_k, own)
        fill(lax.rem(place - 1 + count, count), near_k, near)
        fill(lax.rem(place + 1, count), near_p, near_pk)
        fill(opposite, part_p, part)

    cut, inner = out.shape[2] // count // 2, out.shape[2] // 2
    span = wide.shape[0] // count
    for x in range(count):
        for number, result in ((0, spatial), (1, temporal)):
            block = out[x, number * cut : (number + 1) * cut]
            result[2 * x * cut : (2 * x + 1) * cut] = block[:, :inner]
            result[(2 * x + 1) * cut : (2 * x + 2) * cut] = block[:, inner:]
        wide[x * span : (x + 1) * span] = out[x, 2 * cut :]


def in_vmem(body, info, blocks, results, scratch=()):
    vmem = pl.BlockSpec(memory_space=pltpu.VMEM)
    return pl.pallas_call(
        body,
        in_specs=[SCALARS] + [vmem] * len(blocks),
        out_specs=jax.tree.map(lambda _: vmem, results),
        out_shape=results,
        scratch_shapes=list(scratch),
        cost_estimate=pl.CostEstimate(flops=1, bytes_accessed=1, transcendentals=0),
        compiler_params=pltpu.CompilerParams(vmem_limit_bytes=VMEM_BYTES),
    )(info, *blocks)


def tie(*values):
    return lax.optimization_barrier(values)


def near_rows(out_spatial, qkv_temporal, out_temporal):
    half, narrow = out_spatial.shape
    packed = jnp.concatenate(
        [jnp.concatenate([out_spatial.T, out_temporal.T], axis=1), qkv_temporal.T], axis=0
    )
    near = jnp.transpose(lax.all_gather(packed, ("y", "c"), axis=0, tiled=False), (1, 0, 2))
    thin = near[:narrow, :, :half].reshape(narrow, -1)
    other = near[:narrow, :, half:].reshape(narrow, -1)
    wide = near[narrow:].reshape(near.shape[0] - narrow, -1)
    return (fold(thin), wide, fold(other))


def fold(rows):
    cut = rows.shape[-2] // 2
    return jnp.concatenate([rows[..., :cut, :], rows[..., cut:, :]], axis=-1)


def unfold(rows):
    cut = rows.shape[-1] // 2
    return jnp.concatenate([rows[..., :cut], rows[..., cut:]], axis=-2)


def gather_z(coords, rows, cut, beside):
    arrived = [shift_both(rows, "z", hops) for hops in (2, 1, 3)]
    arrived = [arrived[1], arrived[0], arrived[2], shift_both(arrived[0], "z", 2)]
    arrived, beside = tie(arrived, beside)
    swapped = [swap(block) for block in arrived[:3]]
    count, width = lax.axis_size("z"), rows.shape[1]
    half = shape_of(count * rows.shape[0] // 2, width)
    halves = in_vmem(
        functools.partial(place_along_z, cut=cut),
        coords,
        [rows] + arrived + swapped,
        (half, half),
        [pltpu.VMEM((count,) + rows.shape, BF16), pltpu.VMEM((2 * half.shape[0], width), F32)],
    )
    return halves, beside


def scatter(blocks, axis):
    count, place = lax.axis_size(axis), lax.axis_index(axis)
    arrived = []
    for hops in range(1, count):
        block = lax.dynamic_index_in_dim(blocks, (place + hops) % count, 0, keepdims=False)
        arrived.append(shift(block, axis, hops))
    return arrived


def halves_summed(keep, send):
    return (keep.astype(F32) + swap(send).astype(F32)).astype(BF16)


def spread(blocks, place, turned, outs):
    count = len(blocks)
    for index, block in enumerate(blocks):
        turned[lax.rem(index - place + count, count)] = block.astype(BF16)
    for hops, out in enumerate(outs):
        out[...] = turned[hops]


def regroup_wide(info, blocks, first, second, third, *outs):
    outs, turned = outs[:-1], outs[-1]
    y_count, span, lanes = turned.shape
    total = blocks[info[0]].astype(F32)
    for block in (first, second, third):
        total = total + block[...].astype(F32)
    tiles = [total[at : at + span] for at in range(0, total.shape[0], span)]
    flat = jnp.concatenate(tiles, axis=1)
    step = (flat.shape[1] - LANES // 2) // y_count
    rest = jnp.zeros((span, lanes - step), F32)
    cuts = [flat[:, y * step : (y + 1) * step] for y in range(y_count)]
    spread([jnp.concatenate([one, rest], axis=1) for one in cuts], info[2], turned, outs)


def regroup_pair(info, blocks, first, second, third, *outs):
    outs, turned = outs[:-1], outs[-1]
    x_count, span, lanes = turned.shape
    total = blocks[info[2]].astype(F32)
    for block in (first, second, third):
        total = total + block[...].astype(F32)
    width = x_count * span
    step = total.shape[0] // (width // LANES)
    tiles = [total[at : at + step].T for at in range(0, total.shape[0], step)]
    flat = jnp.concatenate(tiles, axis=0)
    flat = jnp.concatenate([flat, jnp.zeros((width, lanes - step), F32)], axis=1)
    cuts = [flat[x * span : (x + 1) * span] for x in range(x_count)]
    spread(cuts, info[0], turned, outs)


def regrouped(body, coords, blocks, arrived, span, count):
    one = shape_of(span, 2 * LANES)
    turned = pltpu.VMEM((count, span, 2 * LANES), BF16)
    return in_vmem(body, coords, [blocks] + arrived, (one,) * count, [turned])


def send_ahead(blocks, axis):
    return [shift(block, axis, hops + 1) for hops, block in enumerate(blocks[1:])]


def added(own, arrived):
    total = own.astype(F32)
    for block in arrived:
        total = total + block.astype(F32)
    return total.astype(BF16)


def reduce_grads(coords, wide, pair, inner, width, beside):
    x_count, y_count, z_count = (lax.axis_size(axis) for axis in ("x", "y", "z"))
    arrived, pair_in, beside = tie(scatter(wide, "x"), scatter(pair, "y"), beside)
    wide = regrouped(regroup_wide, coords, wide, arrived, 3 * inner // x_count, y_count)
    pair = regrouped(regroup_pair, coords, pair, pair_in, width // x_count, x_count)
    wide = added(wide[0], send_ahead(wide, "y")).reshape(z_count, -1, 2 * LANES)
    pair = added(pair[0], send_ahead(pair, "x")).reshape(z_count, -1, 2 * LANES)
    step = width // (2 * y_count)
    total = jnp.sum(exchange(jnp.concatenate([pair, wide], axis=1), "z").astype(F32), axis=0)
    narrow = pair.shape[1]
    half = step // 2
    summed = (total[:narrow, :half].T, total[narrow:, :step].T, total[:narrow, half:step].T)
    return summed, beside


def on_device(
    hidden,
    spatial_qkv,
    out_spatial,
    qkv_temporal,
    out_temporal,
    modulation,
    cotangent,
    frame_count,
    patch_height,
    patch_width,
):
    seq_count = lax.axis_size(("y", "c"))
    seq_place = lax.axis_index(("y", "c"))
    y_count = lax.axis_size("y")
    stream = hidden[0]
    grad_out = cotangent[0]
    packed_qkv = spatial_qkv[0]
    frame_dev, slot_total, width = stream.shape
    slot_dev = slot_total // seq_count
    inner = out_spatial.shape[0] * seq_count
    slots = 8
    groups = slot_dev // slots
    rows = frame_dev * seq_count * slots
    coords = jnp.stack([lax.axis_index(name) for name in ("x", "z", "y", "c")]).astype(jnp.int32)
    info = jnp.stack(
        [
            frame_count[0],
            patch_height[0] * patch_width[0],
            seq_place * slot_dev,
            seq_place * frame_dev,
            coords[3],
        ]
    ).astype(jnp.int32)

    def to_slots(tokens):
        split = tokens.reshape(frame_dev, seq_count, groups, slots, -1)
        split = jnp.transpose(split, (1, 2, 0, 3, 4))
        return exchange(split.reshape(seq_count, groups, frame_dev * slots, -1), ("y", "c"))

    def to_frames(tokens):
        moved = exchange(tokens, ("y", "c")).reshape(seq_count, groups, frame_dev, slots, -1)
        return jnp.transpose(moved, (2, 0, 1, 3, 4)).reshape(frame_dev, slot_total, -1)

    out_s = shape_of(frame_dev, slot_total, inner)
    out_s = run(
        spatial_forward,
        frame_dev,
        [info, packed_qkv],
        [SCALARS, per_frame(packed_qkv)],
        out_s,
        per_frame(out_s),
        [],
    )
    thin, wide, other = near_rows(out_spatial, qkv_temporal, out_temporal)
    rows_z = jnp.concatenate([thin, other, wide], axis=0)
    cut = thin.shape[0]
    stream_tied, _ = tie(stream, rows_z)
    stream_s = to_slots(stream_tied)
    (onward, kept), (stream_s, out_s) = gather_z(coords, rows_z, cut, (stream_s, out_s))
    out_s_s = to_slots(out_s)
    first = shift_both(onward, "x", 1)
    first_k, out_s_s = tie(shift_both(kept, "x", 1), out_s_s)
    second = shift_both(first, "x", 1)
    second_p = swap(second)
    grad_tied, second_p = tie(grad_out, second_p)
    grad_s = to_slots(grad_tied)
    x_count = lax.axis_size("x")
    w_spatial, w_temporal, w_qkv = in_vmem(
        place_along_x,
        coords,
        [onward, kept, first, first_k, swap(first), swap(first_k), second, second_p],
        (shape_of(width, inner), shape_of(width, inner), shape_of(3 * inner, width)),
        [pltpu.VMEM((x_count, 2 * onward.shape[0], width), BF16)],
    )

    result = (
        shape_of(groups, rows, width),
        shape_of(groups, rows, width),
        shape_of(groups, rows, 3 * inner),
        shape_of(seq_count, groups, rows // seq_count, inner),
    )
    mixed_s, modulated, qkv_t, out_t = run(
        functools.partial(temporal_forward, slots=slots),
        groups,
        [info, modulation, stream_s, out_s_s, w_spatial, w_qkv],
        [SCALARS, whole(modulation), per_group(stream_s), per_group(out_s_s), whole(w_spatial), whole(w_qkv)],
        result,
        [per_frame(result[0]), per_frame(result[1]), per_frame(result[2]), per_group(result[3])],
        [],
    )
    out_t_f = to_frames(out_t)

    wide_rows, pair_rows = term_rows(inner, width, y_count, x_count)
    result = (
        shape_of(seq_count, groups, rows // seq_count, width),
        shape_of(x_count, wide_rows, LANES),
        shape_of(y_count, pair_rows, LANES),
        shape_of(x_count, wide_rows, LANES),
        shape_of(y_count, pair_rows, LANES),
    )
    tokens = groups * rows
    kept = [(inner,), (inner,), (3 * inner,), (width,), (width,)]
    kept = [pltpu.VMEM((tokens,) + shape, BF16) for shape in kept]
    kept.append(pltpu.VMEM((2, tokens, width // 2), BF16))
    ln_grad, wide_keep, pair_keep, wide_send, pair_send = run(
        functools.partial(temporal_backward, slots=slots, y_count=y_count),
        groups,
        [info, modulation, grad_s, mixed_s, out_s_s, qkv_t, out_t, modulated, w_temporal, w_qkv],
        [
            SCALARS,
            whole(modulation),
            per_group(grad_s),
            per_frame(mixed_s),
            per_group(out_s_s),
            per_frame(qkv_t),
            per_group(out_t),
            per_frame(modulated),
            whole(w_temporal),
            whole(w_qkv),
        ],
        result,
        [per_group(result[0])] + [whole(part) for part in result[1:]],
        kept,
    )
    wide_send, out_t_f = tie(wide_send, out_t_f)
    wide = halves_summed(wide_keep, wide_send)
    pair = halves_summed(pair_keep, pair_send)
    ln_frames = to_frames(ln_grad)

    result = (shape_of(frame_dev, slot_total, width), shape_of(frame_dev, slot_total, 3 * inner))
    hidden_grad, qkv_s_grad = run(
        spatial_backward,
        frame_dev,
        [info, grad_out, ln_frames, packed_qkv, out_s, w_spatial],
        [
            SCALARS,
            per_frame(grad_out),
            per_frame(ln_frames),
            per_frame(packed_qkv),
            per_frame(out_s),
            whole(w_spatial),
        ],
        result,
        [per_frame(result[0]), per_frame(result[1])],
        [],
    )
    summed, qkv_s_grad = reduce_grads(coords, wide, pair, inner, width, qkv_s_grad)
    block_out = shape_of(frame_dev, slot_total, width)
    block_out = run(
        block_forward,
        frame_dev,
        [info, modulation, stream, out_s, out_t_f, w_spatial, w_temporal],
        [
            SCALARS,
            whole(modulation),
            per_frame(stream),
            per_frame(out_s),
            per_frame(out_t_f),
            whole(w_spatial),
            whole(w_temporal),
        ],
        block_out,
        per_frame(block_out),
        [],
    )
    return (block_out[None], hidden_grad[None], qkv_s_grad[None], summed[0], summed[1], summed[2])


def solution(mesh):
    torus = Mesh(mesh.devices.reshape(4, 8, 4, 2), ("x", "z", "y", "c"))
    dp, seq = ("x", "z"), ("y", "c")
    tokens = P(dp, seq, None, None)
    weight = P(seq, dp)
    placed = (
        tokens,
        tokens,
        weight,
        weight,
        weight,
        P(dp, None, None),
        tokens,
        P(dp),
        P(dp),
        P(dp),
    )
    return jax.shard_map(
        on_device,
        mesh=torus,
        in_specs=placed,
        out_specs=(tokens, tokens, tokens, weight, weight, weight),
        check_vma=False,
    )
```

```python
import functools
import math

import jax
import jax.numpy as jnp
from jax import lax
from jax.experimental import pallas as pl
from jax.experimental.pallas import tpu as pltpu
from jax.sharding import Mesh
from jax.sharding import PartitionSpec as P

HEAD_DIM = 72
EPSILON = 1e-06
NEGATIVE = -1e30
LANES = 128
VMEM_BYTES = 56 * 1024 * 1024
F32 = jnp.float32
BF16 = jnp.bfloat16


def dot_nn(left, right):
    return lax.dot_general(left, right, (((1,), (0,)), ((), ())), preferred_element_type=F32)


def dot_nt(left, right):
    return lax.dot_general(left, right, (((1,), (1,)), ((), ())), preferred_element_type=F32)


def dot_tn(left, right):
    return lax.dot_general(left, right, (((0,), (0,)), ((), ())), preferred_element_type=F32)


def head_windows(inner):
    windows = []
    for head in range(inner // HEAD_DIM):
        low = head * HEAD_DIM
        start = low // LANES * LANES
        stop = min(-(-(low + HEAD_DIM) // LANES) * LANES, inner)
        windows.append((start, stop, low - start))
    return windows


def own_lanes(window):
    start, stop, offset = window
    lane = lax.broadcasted_iota(jnp.int32, (1, stop - start), 1)
    return (lane >= offset) & (lane < offset + HEAD_DIM)


def only(lanes, rows):
    return jnp.where(lanes, rows, jnp.zeros((), rows.dtype))


def lane_tiles(inner):
    return [(low, min(low + LANES, inner)) for low in range(0, inner, LANES)]


def combine(inner, factors, rows):
    pieces = []
    for low, high in lane_tiles(inner):
        lane = low + lax.broadcasted_iota(jnp.int32, (1, high - low), 1)
        total = None
        for head, factor in enumerate(factors):
            start, stop = head * HEAD_DIM, (head + 1) * HEAD_DIM
            if stop <= low or start >= high:
                continue
            own = only((lane >= start) & (lane < stop), rows[:, low:high])
            part = lax.dot_general(
                factor[0], own, (((factor[1],), (0,)), ((), ())), preferred_element_type=F32
            )
            total = part if total is None else total + part
        pieces.append(total)
    return jnp.concatenate(pieces, axis=1)


def head_logits(query, key, allowed):
    logits = []
    for window in head_windows(query.shape[1]):
        start, stop, _ = window
        own = only(own_lanes(window), key[:, start:stop])
        logits.append(dot_nt(query[:, start:stop], own))
    return logits


def softmax_rows(logits, allowed):
    logits = jnp.where(allowed, logits * (1.0 / math.sqrt(HEAD_DIM)), NEGATIVE)
    powers = jnp.exp(logits - jnp.max(logits, axis=1, keepdims=True))
    return powers * (1.0 / jnp.sum(powers, axis=1, keepdims=True))


def attend_heads(query, key, value, allowed):
    logits = head_logits(query, key, allowed)
    probs = [softmax_rows(one, allowed).astype(BF16) for one in logits]
    return combine(query.shape[1], [(one, 1) for one in probs], value)


def attend_heads_back(query, key, value, out, out_grad, allowed):
    inner = query.shape[1]
    factor = 1.0 / math.sqrt(HEAD_DIM)
    logits = head_logits(query, key, allowed)
    slopes, deltas = [], []
    for window in head_windows(inner):
        start, stop, _ = window
        own = only(own_lanes(window), out_grad[:, start:stop])
        slopes.append(dot_nt(own, value[:, start:stop]))
        product = own.astype(F32) * out[:, start:stop].astype(F32)
        deltas.append(jnp.sum(product, axis=1, keepdims=True))
    halves, grads = [], []
    for one, slope, delta in zip(logits, slopes, deltas):
        probs = softmax_rows(one, allowed)
        halves.append(probs.astype(BF16))
        grads.append((probs * (slope - delta)).astype(BF16))
    q_grad = combine(inner, [(one, 1) for one in grads], key) * factor
    k_grad = combine(inner, [(one, 0) for one in grads], query) * factor
    v_grad = combine(inner, [(one, 0) for one in halves], out_grad)
    return jnp.concatenate(
        [q_grad.astype(BF16), k_grad.astype(BF16), v_grad.astype(BF16)], axis=1
    )


def slot_masks(info_ref, rows, slots):
    frames, limit, first = info_ref[0], info_ref[1], info_ref[2]
    group = pl.program_id(0)
    row = lax.broadcasted_iota(jnp.int32, (rows, 1), 0)
    slot = first + group * slots + row % slots
    token = (row // slots < frames) & (slot < limit)
    col = lax.broadcasted_iota(jnp.int32, (1, rows), 1)
    allowed = (row % slots == col % slots) & (col // slots < frames)
    return token.astype(F32), allowed


def normalised(mixed):
    values = mixed.astype(F32)
    centred = values - jnp.mean(values, axis=1, keepdims=True)
    inv_std = lax.rsqrt(jnp.mean(centred * centred, axis=1, keepdims=True) + EPSILON)
    return centred * inv_std, inv_std


def temporal_forward(
    info, mod, stream, out_s, w_spatial, w_qkv, mixed_ref, mod_ref, qkv_ref, out_ref, slots
):
    rows, width = mod_ref.shape[1:]
    inner = out_s.shape[-1]
    token, allowed = slot_masks(info, rows, slots)
    branch = dot_nt(out_s[...].reshape(rows, inner), w_spatial[...])
    mixed = (stream[...].reshape(rows, width).astype(F32) + token * branch).astype(BF16)
    mixed_ref[...] = mixed.reshape(mixed_ref.shape)
    normed, _ = normalised(mixed)
    modulated = (normed * (1.0 + mod[0, 1:2]) + mod[0, 0:1]).astype(BF16)
    mod_ref[...] = modulated.reshape(mod_ref.shape)
    qkv = dot_nt(modulated, w_qkv[...]).astype(BF16)
    qkv_ref[...] = qkv.reshape(qkv_ref.shape)
    out = attend_heads(qkv[:, :inner], qkv[:, inner : 2 * inner], qkv[:, 2 * inner :], allowed)
    out_ref[...] = out.astype(BF16).reshape(out_ref.shape)


def temporal_backward(
    info, mod, grad, mixed, out_s, qkv_ref, out_t, modulated, w_temporal, w_qkv, ln_ref,
    wide_keep, pair_keep, wide_send, pair_send, left_s, left_t, left_q, right_s, right_t, right_q, slots, y_count,
):
    rows, width = modulated.shape[1:]
    inner = out_s.shape[-1]
    token, allowed = slot_masks(info, rows, slots)

    grad_f = grad[...].reshape(rows, width).astype(F32)
    branch_grad = (token * mod[0, 2:3] * grad_f).astype(BF16)
    out_grad = dot_nn(branch_grad, w_temporal[...]).astype(BF16)
    qkv = qkv_ref[...].reshape(rows, 3 * inner)
    out = out_t[...].reshape(rows, inner)
    dqkv = attend_heads_back(
        qkv[:, :inner], qkv[:, inner : 2 * inner], qkv[:, 2 * inner :], out, out_grad, allowed
    )

    norm_grad = dot_nn(dqkv, w_qkv[...]) * (1.0 + mod[0, 1:2])
    normed, inv_std = normalised(mixed[...].reshape(rows, width))
    first = jnp.mean(norm_grad, axis=1, keepdims=True)
    second = jnp.mean(norm_grad * normed, axis=1, keepdims=True)
    ln_grad = (inv_std * (norm_grad - first - normed * second)).astype(BF16)
    ln_ref[...] = ln_grad.reshape(ln_ref.shape)
    hidden_grad = (grad_f + ln_grad.astype(F32)).astype(BF16)
    spatial_grad = (token * hidden_grad.astype(F32)).astype(BF16)

    step = width // (2 * y_count)
    normal = modulated[...].reshape(rows, width)
    place = pl.ds(pl.program_id(0) * rows, rows)
    left_s[place, :] = out_s[...].reshape(rows, inner)
    left_t[place, :] = out
    left_q[place, :] = dqkv
    right_s[place, :] = spatial_grad
    right_t[place, :] = branch_grad
    for c in range(2):
        pieces = [normal[:, (2 * y + c) * step : (2 * y + c + 1) * step] for y in range(y_count)]
        right_q[c, place, :] = jnp.concatenate(pieces, axis=1)

    @pl.when(pl.program_id(0) == pl.num_programs(0) - 1)
    def _():
        core = info[4]
        for side, out in ((core, wide_keep), (1 - core, wide_send)):
            store_wide(dot_tn(left_q[...], right_q[side]), out)
        sum_s = dot_tn(left_s[...], right_s[...])
        sum_t = dot_tn(left_t[...], right_t[...])
        for keeper in range(2):

            @pl.when(core == keeper)
            def _():
                store_pair(sum_s, sum_t, keeper, pair_keep)
                store_pair(sum_s, sum_t, 1 - keeper, pair_send)


def term_rows(inner, width, y_count, x_count):
    tiles = -(-(width // 2) // LANES)
    return tiles * (3 * inner // x_count), width // LANES * (inner // y_count)


def store_wide(total, out):
    x_count, rows, _ = out.shape
    span = total.shape[0] // x_count
    for tile in range(rows // span):
        block = total[:, tile * LANES : (tile + 1) * LANES]
        if block.shape[1] < LANES:
            rest = jnp.zeros((block.shape[0], LANES - block.shape[1]), F32)
            block = jnp.concatenate([block, rest], axis=1)
        for x in range(x_count):
            piece = block[x * span : (x + 1) * span]
            out[x, tile * span : (tile + 1) * span] = piece.astype(BF16)


def store_pair(sum_s, sum_t, core, out):
    y_count = out.shape[0]
    inner, width = sum_s.shape
    step = inner // (2 * y_count)
    for y in range(y_count):
        place = (2 * y + core) * step
        for tile in range(width // LANES):
            lanes = slice(tile * LANES, (tile + 1) * LANES)
            parts = [sum_s[place : place + step, lanes], sum_t[place : place + step, lanes]]
            block = jnp.concatenate(parts, axis=0).astype(BF16)
            out[y, tile * 2 * step : (tile + 1) * 2 * step] = block


def frame_keys(info_ref, rows):
    return lax.broadcasted_iota(jnp.int32, (1, rows), 1) < info_ref[1]


def frame_tokens(info_ref, rows):
    row = lax.broadcasted_iota(jnp.int32, (rows, 1), 0)
    alive = info_ref[3] + pl.program_id(0) < info_ref[0]
    return ((row < info_ref[1]) & alive).astype(F32)


def spatial_forward(info, qkv_ref, out_ref):
    rows, inner = out_ref.shape[1:]
    qkv = qkv_ref[0]
    out = attend_heads(
        qkv[:, :inner], qkv[:, inner : 2 * inner], qkv[:, 2 * inner :], frame_keys(info, rows)
    )
    out_ref[0] = out.astype(BF16)


def block_forward(info, mod, stream, out_s, out_t, w_spatial, w_temporal, block_ref):
    rows = stream.shape[1]
    token = frame_tokens(info, rows)
    spatial = dot_nt(out_s[0], w_spatial[...])
    mixed = (stream[0].astype(F32) + token * spatial).astype(BF16)
    branch = dot_nt(out_t[0], w_temporal[...])
    block_ref[0] = (mixed.astype(F32) + token * mod[0, 2:3] * branch).astype(BF16)


def spatial_backward(
    info, grad, ln_grad, qkv_ref, out_s, w_spatial, hidden_ref, dqkv_ref
):
    rows, inner = out_s.shape[1:]
    hidden_grad = (grad[0].astype(F32) + ln_grad[0].astype(F32)).astype(BF16)
    hidden_ref[0] = hidden_grad
    branch_grad = (frame_tokens(info, rows) * hidden_grad.astype(F32)).astype(BF16)
    out_grad = dot_nn(branch_grad, w_spatial[...]).astype(BF16)
    qkv = qkv_ref[0]
    dqkv_ref[0] = attend_heads_back(
        qkv[:, :inner], qkv[:, inner : 2 * inner], qkv[:, 2 * inner :], out_s[0], out_grad,
        frame_keys(info, rows),
    )


def whole(array):
    return pl.BlockSpec(
        array.shape, lambda step: (0,) * array.ndim, pipeline_mode=pl.Buffered(1)
    )


def per_frame(array):
    return pl.BlockSpec((1,) + array.shape[1:], lambda step: (step, 0, 0))


def per_group(array):
    return pl.BlockSpec(
        (array.shape[0], 1) + array.shape[2:], lambda step: (0, step, 0, 0)
    )


SCALARS = pl.BlockSpec(memory_space=pltpu.SMEM)


def run(body, steps, operands, specs, results, result_specs, scratch):
    return pl.pallas_call(
        body,
        grid=(steps,),
        in_specs=specs,
        out_specs=result_specs,
        out_shape=results,
        scratch_shapes=scratch,
        compiler_params=pltpu.CompilerParams(vmem_limit_bytes=VMEM_BYTES),
        cost_estimate=pl.CostEstimate(flops=1, bytes_accessed=1, transcendentals=0),
    )(*operands)


def shape_of(*dims, dtype=BF16):
    return jax.ShapeDtypeStruct(dims, dtype)


def exchange(rows, axes):
    return lax.all_to_all(rows, axes, 0, 0, tiled=True)


def shift(rows, axis, hops):
    count = lax.axis_size(axis)
    return lax.ppermute(rows, axis, [(at, (at + hops) % count) for at in range(count)])


def shift_both(rows, axis, hops):
    count = lax.axis_size(axis)
    pairs = []
    for at in range(count):
        pairs.append((2 * at, 2 * ((at - hops) % count)))
        pairs.append((2 * at + 1, 2 * ((at + hops) % count) + 1))
    return lax.ppermute(rows, (axis, "c"), pairs)


def swap(rows):
    return shift(rows, "c", 1)


def place_along_z(
    info, own, near, mid, far, last, near_p, mid_p, far_p, onward, kept, stack, flat, cut
):
    place, count = info[1], stack.shape[0]
    sign = 1 - 2 * info[3]
    stack[place] = own[...]
    stack[lax.rem(place + count // 2, count)] = last[...]
    for hops, mine, other in ((1, near, near_p), (2, mid, mid_p), (3, far, far_p)):
        stack[lax.rem(place + sign * hops + count, count)] = mine[...]
        stack[lax.rem(place - sign * hops + count, count)] = other[...]

    inner = flat.shape[1] // 2
    step = stack.shape[1] - 2 * cut
    for z in range(count):
        block = stack[z].astype(F32)
        side = 2 * z // count
        for number in range(2):
            for part in range(2):
                row = (2 * number * count + 4 * (z % (count // 2)) + 2 * part) * cut // 2
                flat[row : row + cut, side * inner : (side + 1) * inner] = block[
                    number * cut : (number + 1) * cut, part * inner : (part + 1) * inner
                ]
        row = 2 * count * cut + z * step
        flat[row : row + step] = block[2 * cut :]
    size = flat.shape[0] // 2
    lower, upper = flat[:size].astype(BF16), flat[size:].astype(BF16)

    @pl.when(info[3] == 0)
    def _():
        onward[...] = lower
        kept[...] = upper

    @pl.when(info[3] != 0)
    def _():
        onward[...] = upper
        kept[...] = lower


def place_along_x(
    info, own, own_k, near, near_k, near_p, near_pk, part, part_p, spatial, temporal, wide, out
):
    place, count = info[0], out.shape[0]
    half = part.shape[0]
    opposite = lax.rem(place + count // 2, count)

    def fill(index, first, second):
        out[index, :half] = first[...]
        out[index, half:] = second[...]

    @pl.when(info[3] == 0)
    def _():
        fill(place, own, own_k)
        fill(lax.rem(place + 1, count), near, near_k)
        fill(lax.rem(place - 1 + count, count), near_pk, near_p)
        fill(opposite, part, part_p)

    @pl.when(info[3] != 0)
    def _():
        fill(place, own_k, own)
        fill(lax.rem(place - 1 + count, count), near_k, near)
        fill(lax.rem(place + 1, count), near_p, near_pk)
        fill(opposite, part_p, part)

    cut, inner = out.shape[2] // count // 2, out.shape[2] // 2
    span = wide.shape[0] // count
    for x in range(count):
        for number, result in ((0, spatial), (1, temporal)):
            block = out[x, number * cut : (number + 1) * cut]
            result[2 * x * cut : (2 * x + 1) * cut] = block[:, :inner]
            result[(2 * x + 1) * cut : (2 * x + 2) * cut] = block[:, inner:]
        wide[x * span : (x + 1) * span] = out[x, 2 * cut :]


def in_vmem(body, info, blocks, results, scratch=()):
    vmem = pl.BlockSpec(memory_space=pltpu.VMEM)
    return pl.pallas_call(
        body,
        in_specs=[SCALARS] + [vmem] * len(blocks),
        out_specs=jax.tree.map(lambda _: vmem, results),
        out_shape=results,
        scratch_shapes=list(scratch),
        cost_estimate=pl.CostEstimate(flops=1, bytes_accessed=1, transcendentals=0),
        compiler_params=pltpu.CompilerParams(vmem_limit_bytes=VMEM_BYTES),
    )(info, *blocks)


def tie(*values):
    return lax.optimization_barrier(values)


def near_rows(out_spatial, qkv_temporal, out_temporal):
    half, narrow = out_spatial.shape
    packed = jnp.concatenate(
        [jnp.concatenate([out_spatial.T, out_temporal.T], axis=1), qkv_temporal.T], axis=0
    )
    near = jnp.transpose(lax.all_gather(packed, ("y", "c"), axis=0, tiled=False), (1, 0, 2))
    thin = near[:narrow, :, :half].reshape(narrow, -1)
    other = near[:narrow, :, half:].reshape(narrow, -1)
    wide = near[narrow:].reshape(near.shape[0] - narrow, -1)
    return (fold(thin), wide, fold(other))


def fold(rows):
    cut = rows.shape[-2] // 2
    return jnp.concatenate([rows[..., :cut, :], rows[..., cut:, :]], axis=-1)


def unfold(rows):
    cut = rows.shape[-1] // 2
    return jnp.concatenate([rows[..., :cut], rows[..., cut:]], axis=-2)


def gather_z(coords, rows, cut, beside):
    arrived = [shift_both(rows, "z", hops) for hops in (2, 1, 3)]
    arrived = [arrived[1], arrived[0], arrived[2], shift_both(arrived[0], "z", 2)]
    arrived, beside = tie(arrived, beside)
    swapped = [swap(block) for block in arrived[:3]]
    count, width = lax.axis_size("z"), rows.shape[1]
    half = shape_of(count * rows.shape[0] // 2, width)
    halves = in_vmem(
        functools.partial(place_along_z, cut=cut),
        coords,
        [rows] + arrived + swapped,
        (half, half),
        [pltpu.VMEM((count,) + rows.shape, BF16), pltpu.VMEM((2 * half.shape[0], width), F32)],
    )
    return halves, beside


def scatter(blocks, axis):
    count, place = lax.axis_size(axis), lax.axis_index(axis)
    arrived = []
    for hops in range(1, count):
        block = lax.dynamic_index_in_dim(blocks, (place + hops) % count, 0, keepdims=False)
        arrived.append(shift(block, axis, hops))
    return arrived


def halves_summed(keep, other):
    return (keep.astype(F32) + other.astype(F32)).astype(BF16)


def spread(blocks, place, turned, outs):
    count = len(blocks)
    for index, block in enumerate(blocks):
        turned[lax.rem(index - place + count, count)] = block.astype(BF16)
    for hops, out in enumerate(outs):
        out[...] = turned[hops]


def regroup_wide(info, blocks, first, second, third, *outs):
    outs, turned = outs[:-1], outs[-1]
    y_count, span, lanes = turned.shape
    total = blocks[info[0]].astype(F32)
    for block in (first, second, third):
        total = total + block[...].astype(F32)
    tiles = [total[at : at + span] for at in range(0, total.shape[0], span)]
    flat = jnp.concatenate(tiles, axis=1)
    step = (flat.shape[1] - LANES // 2) // y_count
    rest = jnp.zeros((span, lanes - step), F32)
    cuts = [flat[:, y * step : (y + 1) * step] for y in range(y_count)]
    spread([jnp.concatenate([one, rest], axis=1) for one in cuts], info[2], turned, outs)


def regroup_pair(info, blocks, first, second, third, *outs):
    outs, turned = outs[:-1], outs[-1]
    x_count, span, lanes = turned.shape
    total = blocks[info[2]].astype(F32)
    for block in (first, second, third):
        total = total + block[...].astype(F32)
    width = x_count * span
    step = total.shape[0] // (width // LANES)
    tiles = [total[at : at + step].T for at in range(0, total.shape[0], step)]
    flat = jnp.concatenate(tiles, axis=0)
    flat = jnp.concatenate([flat, jnp.zeros((width, lanes - step), F32)], axis=1)
    cuts = [flat[x * span : (x + 1) * span] for x in range(x_count)]
    spread(cuts, info[0], turned, outs)


def regrouped(body, coords, blocks, arrived, span, count):
    one = shape_of(span, 2 * LANES)
    turned = pltpu.VMEM((count, span, 2 * LANES), BF16)
    return in_vmem(body, coords, [blocks] + arrived, (one,) * count, [turned])


def send_ahead(blocks, axis):
    return [shift(block, axis, hops + 1) for hops, block in enumerate(blocks[1:])]


def added(own, arrived):
    total = own.astype(F32)
    for block in arrived:
        total = total + block.astype(F32)
    return total.astype(BF16)


def reduce_grads(coords, wide, pair, inner, width, beside):
    x_count, y_count, z_count = (lax.axis_size(axis) for axis in ("x", "y", "z"))
    arrived, pair_in = scatter(wide, "x"), scatter(pair, "y")
    wide = regrouped(regroup_wide, coords, wide, arrived, 3 * inner // x_count, y_count)
    pair = regrouped(regroup_pair, coords, pair, pair_in, width // x_count, x_count)
    arrived, pair_in, beside = tie(send_ahead(wide, "y"), send_ahead(pair, "x"), beside)
    wide = added(wide[0], arrived).reshape(z_count, -1, 2 * LANES)
    pair = added(pair[0], pair_in).reshape(z_count, -1, 2 * LANES)
    step = width // (2 * y_count)
    total = jnp.sum(exchange(jnp.concatenate([pair, wide], axis=1), "z").astype(F32), axis=0)
    narrow = pair.shape[1]
    half = step // 2
    summed = (total[:narrow, :half].T, total[narrow:, :step].T, total[:narrow, half:step].T)
    return summed, beside


def on_device(
    hidden,
    spatial_qkv,
    out_spatial,
    qkv_temporal,
    out_temporal,
    modulation,
    cotangent,
    frame_count,
    patch_height,
    patch_width,
):
    seq_count = lax.axis_size(("y", "c"))
    seq_place = lax.axis_index(("y", "c"))
    y_count = lax.axis_size("y")
    stream = hidden[0]
    grad_out = cotangent[0]
    packed_qkv = spatial_qkv[0]
    frame_dev, slot_total, width = stream.shape
    slot_dev = slot_total // seq_count
    inner = out_spatial.shape[0] * seq_count
    slots = 8
    groups = slot_dev // slots
    rows = frame_dev * seq_count * slots
    coords = jnp.stack([lax.axis_index(name) for name in ("x", "z", "y", "c")]).astype(jnp.int32)
    info = jnp.stack(
        [
            frame_count[0],
            patch_height[0] * patch_width[0],
            seq_place * slot_dev,
            seq_place * frame_dev,
            coords[3],
        ]
    ).astype(jnp.int32)

    def to_slots(tokens):
        split = tokens.reshape(frame_dev, seq_count, groups, slots, -1)
        split = jnp.transpose(split, (1, 2, 0, 3, 4))
        return exchange(split.reshape(seq_count, groups, frame_dev * slots, -1), ("y", "c"))

    def to_frames(tokens):
        moved = exchange(tokens, ("y", "c")).reshape(seq_count, groups, frame_dev, slots, -1)
        return jnp.transpose(moved, (2, 0, 1, 3, 4)).reshape(frame_dev, slot_total, -1)

    out_s = shape_of(frame_dev, slot_total, inner)
    out_s = run(
        spatial_forward,
        frame_dev,
        [info, packed_qkv],
        [SCALARS, per_frame(packed_qkv)],
        out_s,
        per_frame(out_s),
        [],
    )
    thin, wide, other = near_rows(out_spatial, qkv_temporal, out_temporal)
    rows_z = jnp.concatenate([thin, other, wide], axis=0)
    cut = thin.shape[0]
    stream_tied, _ = tie(stream, rows_z)
    stream_s = to_slots(stream_tied)
    (onward, kept), (stream_s, out_s) = gather_z(coords, rows_z, cut, (stream_s, out_s))
    out_s_s = to_slots(out_s)
    first = shift_both(onward, "x", 1)
    first_k = shift_both(kept, "x", 1)
    second = shift_both(first, "x", 1)
    second_p, out_s_s = tie(swap(second), out_s_s)
    grad_tied, second_p = tie(grad_out, second_p)
    grad_s = to_slots(grad_tied)
    x_count = lax.axis_size("x")
    w_spatial, w_temporal, w_qkv = in_vmem(
        place_along_x,
        coords,
        [onward, kept, first, first_k, swap(first), swap(first_k), second, second_p],
        (shape_of(width, inner), shape_of(width, inner), shape_of(3 * inner, width)),
        [pltpu.VMEM((x_count, 2 * onward.shape[0], width), BF16)],
    )

    result = (
        shape_of(groups, rows, width),
        shape_of(groups, rows, width),
        shape_of(groups, rows, 3 * inner),
        shape_of(seq_count, groups, rows // seq_count, inner),
    )
    mixed_s, modulated, qkv_t, out_t = run(
        functools.partial(temporal_forward, slots=slots),
        groups,
        [info, modulation, stream_s, out_s_s, w_spatial, w_qkv],
        [SCALARS, whole(modulation), per_group(stream_s), per_group(out_s_s), whole(w_spatial), whole(w_qkv)],
        result,
        [per_frame(result[0]), per_frame(result[1]), per_frame(result[2]), per_group(result[3])],
        [],
    )
    out_t_tied, _ = tie(out_t, grad_s)
    out_t_f = to_frames(out_t_tied)

    wide_rows, pair_rows = term_rows(inner, width, y_count, x_count)
    result = (
        shape_of(seq_count, groups, rows // seq_count, width),
        shape_of(x_count, wide_rows, LANES),
        shape_of(y_count, pair_rows, LANES),
        shape_of(x_count, wide_rows, LANES),
        shape_of(y_count, pair_rows, LANES),
    )
    tokens = groups * rows
    kept = [(inner,), (inner,), (3 * inner,), (width,), (width,)]
    kept = [pltpu.VMEM((tokens,) + shape, BF16) for shape in kept]
    kept.append(pltpu.VMEM((2, tokens, width // 2), BF16))
    ln_grad, wide_keep, pair_keep, wide_send, pair_send = run(
        functools.partial(temporal_backward, slots=slots, y_count=y_count),
        groups,
        [info, modulation, grad_s, mixed_s, out_s_s, qkv_t, out_t, modulated, w_temporal, w_qkv],
        [
            SCALARS,
            whole(modulation),
            per_group(grad_s),
            per_frame(mixed_s),
            per_group(out_s_s),
            per_frame(qkv_t),
            per_group(out_t),
            per_frame(modulated),
            whole(w_temporal),
            whole(w_qkv),
        ],
        result,
        [per_group(result[0])] + [whole(part) for part in result[1:]],
        kept,
    )
    wide_send, out_t_f = tie(wide_send, out_t_f)
    wide_in, pair_send = tie(swap(wide_send), pair_send)
    wide = halves_summed(wide_keep, wide_in)
    pair = halves_summed(pair_keep, swap(pair_send))
    ln_frames = to_frames(ln_grad)

    result = (shape_of(frame_dev, slot_total, width), shape_of(frame_dev, slot_total, 3 * inner))
    hidden_grad, qkv_s_grad = run(
        spatial_backward,
        frame_dev,
        [info, grad_out, ln_frames, packed_qkv, out_s, w_spatial],
        [
            SCALARS,
            per_frame(grad_out),
            per_frame(ln_frames),
            per_frame(packed_qkv),
            per_frame(out_s),
            whole(w_spatial),
        ],
        result,
        [per_frame(result[0]), per_frame(result[1])],
        [],
    )
    summed, qkv_s_grad = reduce_grads(coords, wide, pair, inner, width, qkv_s_grad)
    block_out = shape_of(frame_dev, slot_total, width)
    block_out = run(
        block_forward,
        frame_dev,
        [info, modulation, stream, out_s, out_t_f, w_spatial, w_temporal],
        [
            SCALARS,
            whole(modulation),
            per_frame(stream),
            per_frame(out_s),
            per_frame(out_t_f),
            whole(w_spatial),
            whole(w_temporal),
        ],
        block_out,
        per_frame(block_out),
        [],
    )
    return (block_out[None], hidden_grad[None], qkv_s_grad[None], summed[0], summed[1], summed[2])


def solution(mesh):
    torus = Mesh(mesh.devices.reshape(4, 8, 4, 2), ("x", "z", "y", "c"))
    dp, seq = ("x", "z"), ("y", "c")
    tokens = P(dp, seq, None, None)
    weight = P(seq, dp)
    placed = (
        tokens,
        tokens,
        weight,
        weight,
        weight,
        P(dp, None, None),
        tokens,
        P(dp),
        P(dp),
        P(dp),
    )
    return jax.shard_map(
        on_device,
        mesh=torus,
        in_specs=placed,
        out_specs=(tokens, tokens, tokens, weight, weight, weight),
        check_vma=False,
    )
```

```python
import functools
import math

import jax
import jax.numpy as jnp
from jax import lax
from jax.experimental import pallas as pl
from jax.experimental.pallas import tpu as pltpu
from jax.sharding import Mesh
from jax.sharding import PartitionSpec as P

HEAD_DIM = 72
EPSILON = 1e-06
NEGATIVE = -1e30
LANES = 128
VMEM_BYTES = 56 * 1024 * 1024
F32 = jnp.float32
BF16 = jnp.bfloat16


def dot_nn(left, right):
    return lax.dot_general(left, right, (((1,), (0,)), ((), ())), preferred_element_type=F32)


def dot_nt(left, right):
    return lax.dot_general(left, right, (((1,), (1,)), ((), ())), preferred_element_type=F32)


def dot_tn(left, right):
    return lax.dot_general(left, right, (((0,), (0,)), ((), ())), preferred_element_type=F32)


def head_windows(inner):
    windows = []
    for head in range(inner // HEAD_DIM):
        low = head * HEAD_DIM
        start = low // LANES * LANES
        stop = min(-(-(low + HEAD_DIM) // LANES) * LANES, inner)
        windows.append((start, stop, low - start))
    return windows


def own_lanes(window):
    start, stop, offset = window
    lane = lax.broadcasted_iota(jnp.int32, (1, stop - start), 1)
    return (lane >= offset) & (lane < offset + HEAD_DIM)


def only(lanes, rows):
    return jnp.where(lanes, rows, jnp.zeros((), rows.dtype))


def lane_tiles(inner):
    return [(low, min(low + LANES, inner)) for low in range(0, inner, LANES)]


def combine(inner, factors, rows):
    pieces = []
    for low, high in lane_tiles(inner):
        lane = low + lax.broadcasted_iota(jnp.int32, (1, high - low), 1)
        total = None
        for head, factor in enumerate(factors):
            start, stop = head * HEAD_DIM, (head + 1) * HEAD_DIM
            if stop <= low or start >= high:
                continue
            own = only((lane >= start) & (lane < stop), rows[:, low:high])
            part = lax.dot_general(
                factor[0], own, (((factor[1],), (0,)), ((), ())), preferred_element_type=F32
            )
            total = part if total is None else total + part
        pieces.append(total)
    return jnp.concatenate(pieces, axis=1)


def head_logits(query, key, allowed):
    logits = []
    for window in head_windows(query.shape[1]):
        start, stop, _ = window
        own = only(own_lanes(window), key[:, start:stop])
        logits.append(dot_nt(query[:, start:stop], own))
    return logits


def softmax_rows(logits, allowed):
    logits = jnp.where(allowed, logits * (1.0 / math.sqrt(HEAD_DIM)), NEGATIVE)
    powers = jnp.exp(logits - jnp.max(logits, axis=1, keepdims=True))
    return powers * (1.0 / jnp.sum(powers, axis=1, keepdims=True))


def attend_heads(query, key, value, allowed):
    logits = head_logits(query, key, allowed)
    probs = [softmax_rows(one, allowed).astype(BF16) for one in logits]
    return combine(query.shape[1], [(one, 1) for one in probs], value)


def attend_heads_back(query, key, value, out, out_grad, allowed):
    inner = query.shape[1]
    factor = 1.0 / math.sqrt(HEAD_DIM)
    logits = head_logits(query, key, allowed)
    slopes, deltas = [], []
    for window in head_windows(inner):
        start, stop, _ = window
        own = only(own_lanes(window), out_grad[:, start:stop])
        slopes.append(dot_nt(own, value[:, start:stop]))
        product = own.astype(F32) * out[:, start:stop].astype(F32)
        deltas.append(jnp.sum(product, axis=1, keepdims=True))
    halves, grads = [], []
    for one, slope, delta in zip(logits, slopes, deltas):
        probs = softmax_rows(one, allowed)
        halves.append(probs.astype(BF16))
        grads.append((probs * (slope - delta)).astype(BF16))
    q_grad = combine(inner, [(one, 1) for one in grads], key) * factor
    k_grad = combine(inner, [(one, 0) for one in grads], query) * factor
    v_grad = combine(inner, [(one, 0) for one in halves], out_grad)
    return jnp.concatenate(
        [q_grad.astype(BF16), k_grad.astype(BF16), v_grad.astype(BF16)], axis=1
    )


def slot_masks(info_ref, rows, slots):
    frames, limit, first = info_ref[0], info_ref[1], info_ref[2]
    group = pl.program_id(0)
    row = lax.broadcasted_iota(jnp.int32, (rows, 1), 0)
    slot = first + group * slots + row % slots
    token = (row // slots < frames) & (slot < limit)
    col = lax.broadcasted_iota(jnp.int32, (1, rows), 1)
    allowed = (row % slots == col % slots) & (col // slots < frames)
    return token.astype(F32), allowed


def normalised(mixed):
    values = mixed.astype(F32)
    centred = values - jnp.mean(values, axis=1, keepdims=True)
    inv_std = lax.rsqrt(jnp.mean(centred * centred, axis=1, keepdims=True) + EPSILON)
    return centred * inv_std, inv_std


def temporal_forward(
    info, mod, stream, out_s, w_spatial, w_qkv, mixed_ref, mod_ref, qkv_ref, out_ref, slots
):
    rows, width = mod_ref.shape[1:]
    inner = out_s.shape[-1]
    token, allowed = slot_masks(info, rows, slots)
    branch = dot_nt(out_s[...].reshape(rows, inner), w_spatial[...])
    mixed = (stream[...].reshape(rows, width).astype(F32) + token * branch).astype(BF16)
    mixed_ref[...] = mixed.reshape(mixed_ref.shape)
    normed, _ = normalised(mixed)
    modulated = (normed * (1.0 + mod[0, 1:2]) + mod[0, 0:1]).astype(BF16)
    mod_ref[...] = modulated.reshape(mod_ref.shape)
    qkv = dot_nt(modulated, w_qkv[...]).astype(BF16)
    qkv_ref[...] = qkv.reshape(qkv_ref.shape)
    out = attend_heads(qkv[:, :inner], qkv[:, inner : 2 * inner], qkv[:, 2 * inner :], allowed)
    out_ref[...] = out.astype(BF16).reshape(out_ref.shape)


def temporal_backward(
    info, mod, grad, mixed, out_s, qkv_ref, out_t, modulated, w_temporal, w_qkv, ln_ref,
    wide_keep, pair_keep, wide_send, pair_send, left_s, left_t, left_q, right_s, right_t, right_q, slots, y_count,
):
    rows, width = modulated.shape[1:]
    inner = out_s.shape[-1]
    token, allowed = slot_masks(info, rows, slots)

    grad_f = grad[...].reshape(rows, width).astype(F32)
    branch_grad = (token * mod[0, 2:3] * grad_f).astype(BF16)
    out_grad = dot_nn(branch_grad, w_temporal[...]).astype(BF16)
    qkv = qkv_ref[...].reshape(rows, 3 * inner)
    out = out_t[...].reshape(rows, inner)
    dqkv = attend_heads_back(
        qkv[:, :inner], qkv[:, inner : 2 * inner], qkv[:, 2 * inner :], out, out_grad, allowed
    )

    norm_grad = dot_nn(dqkv, w_qkv[...]) * (1.0 + mod[0, 1:2])
    normed, inv_std = normalised(mixed[...].reshape(rows, width))
    first = jnp.mean(norm_grad, axis=1, keepdims=True)
    second = jnp.mean(norm_grad * normed, axis=1, keepdims=True)
    ln_grad = (inv_std * (norm_grad - first - normed * second)).astype(BF16)
    ln_ref[...] = ln_grad.reshape(ln_ref.shape)
    hidden_grad = (grad_f + ln_grad.astype(F32)).astype(BF16)
    spatial_grad = (token * hidden_grad.astype(F32)).astype(BF16)

    step = width // (2 * y_count)
    normal = modulated[...].reshape(rows, width)
    place = pl.ds(pl.program_id(0) * rows, rows)
    left_s[place, :] = out_s[...].reshape(rows, inner)
    left_t[place, :] = out
    left_q[place, :] = dqkv
    right_s[place, :] = spatial_grad
    right_t[place, :] = branch_grad
    for c in range(2):
        pieces = [normal[:, (2 * y + c) * step : (2 * y + c + 1) * step] for y in range(y_count)]
        right_q[c, place, :] = jnp.concatenate(pieces, axis=1)

    @pl.when(pl.program_id(0) == pl.num_programs(0) - 1)
    def _():
        core = info[4]
        for side, out in ((core, wide_keep), (1 - core, wide_send)):
            store_wide(dot_tn(left_q[...], right_q[side]), out)
        sum_s = dot_tn(left_s[...], right_s[...])
        sum_t = dot_tn(left_t[...], right_t[...])
        for keeper in range(2):

            @pl.when(core == keeper)
            def _():
                store_pair(sum_s, sum_t, keeper, pair_keep)
                store_pair(sum_s, sum_t, 1 - keeper, pair_send)


def term_rows(inner, width, y_count, x_count):
    tiles = -(-(width // 2) // LANES)
    return tiles * (3 * inner // x_count), width // LANES * (inner // y_count)


def store_wide(total, out):
    x_count, rows, _ = out.shape
    span = total.shape[0] // x_count
    for tile in range(rows // span):
        block = total[:, tile * LANES : (tile + 1) * LANES]
        if block.shape[1] < LANES:
            rest = jnp.zeros((block.shape[0], LANES - block.shape[1]), F32)
            block = jnp.concatenate([block, rest], axis=1)
        for x in range(x_count):
            piece = block[x * span : (x + 1) * span]
            out[x, tile * span : (tile + 1) * span] = piece.astype(BF16)


def store_pair(sum_s, sum_t, core, out):
    y_count = out.shape[0]
    inner, width = sum_s.shape
    step = inner // (2 * y_count)
    for y in range(y_count):
        place = (2 * y + core) * step
        for tile in range(width // LANES):
            lanes = slice(tile * LANES, (tile + 1) * LANES)
            parts = [sum_s[place : place + step, lanes], sum_t[place : place + step, lanes]]
            block = jnp.concatenate(parts, axis=0).astype(BF16)
            out[y, tile * 2 * step : (tile + 1) * 2 * step] = block


def frame_keys(info_ref, rows):
    return lax.broadcasted_iota(jnp.int32, (1, rows), 1) < info_ref[1]


def frame_tokens(info_ref, rows):
    row = lax.broadcasted_iota(jnp.int32, (rows, 1), 0)
    alive = info_ref[3] + pl.program_id(0) < info_ref[0]
    return ((row < info_ref[1]) & alive).astype(F32)


def spatial_forward(info, qkv_ref, out_ref):
    rows, inner = out_ref.shape[1:]
    qkv = qkv_ref[0]
    out = attend_heads(
        qkv[:, :inner], qkv[:, inner : 2 * inner], qkv[:, 2 * inner :], frame_keys(info, rows)
    )
    out_ref[0] = out.astype(BF16)


def block_forward(info, mod, stream, out_s, out_t, w_spatial, w_temporal, block_ref):
    rows = stream.shape[1]
    token = frame_tokens(info, rows)
    spatial = dot_nt(out_s[0], w_spatial[...])
    mixed = (stream[0].astype(F32) + token * spatial).astype(BF16)
    branch = dot_nt(out_t[0], w_temporal[...])
    block_ref[0] = (mixed.astype(F32) + token * mod[0, 2:3] * branch).astype(BF16)


def spatial_backward(
    info, grad, ln_grad, qkv_ref, out_s, w_spatial, hidden_ref, dqkv_ref
):
    rows, inner = out_s.shape[1:]
    hidden_grad = (grad[0].astype(F32) + ln_grad[0].astype(F32)).astype(BF16)
    hidden_ref[0] = hidden_grad
    branch_grad = (frame_tokens(info, rows) * hidden_grad.astype(F32)).astype(BF16)
    out_grad = dot_nn(branch_grad, w_spatial[...]).astype(BF16)
    qkv = qkv_ref[0]
    dqkv_ref[0] = attend_heads_back(
        qkv[:, :inner], qkv[:, inner : 2 * inner], qkv[:, 2 * inner :], out_s[0], out_grad,
        frame_keys(info, rows),
    )


def whole(array):
    return pl.BlockSpec(
        array.shape, lambda step: (0,) * array.ndim, pipeline_mode=pl.Buffered(1)
    )


def per_frame(array):
    return pl.BlockSpec((1,) + array.shape[1:], lambda step: (step, 0, 0))


def per_group(array):
    return pl.BlockSpec(
        (array.shape[0], 1) + array.shape[2:], lambda step: (0, step, 0, 0)
    )


SCALARS = pl.BlockSpec(memory_space=pltpu.SMEM)


def run(body, steps, operands, specs, results, result_specs, scratch):
    return pl.pallas_call(
        body,
        grid=(steps,),
        in_specs=specs,
        out_specs=result_specs,
        out_shape=results,
        scratch_shapes=scratch,
        compiler_params=pltpu.CompilerParams(vmem_limit_bytes=VMEM_BYTES),
        cost_estimate=pl.CostEstimate(flops=1, bytes_accessed=1, transcendentals=0),
    )(*operands)


def shape_of(*dims, dtype=BF16):
    return jax.ShapeDtypeStruct(dims, dtype)


def exchange(rows, axes):
    return lax.all_to_all(rows, axes, 0, 0, tiled=True)


def shift(rows, axis, hops):
    count = lax.axis_size(axis)
    return lax.ppermute(rows, axis, [(at, (at + hops) % count) for at in range(count)])


def shift_both(rows, axis, hops):
    count = lax.axis_size(axis)
    pairs = []
    for at in range(count):
        pairs.append((2 * at, 2 * ((at - hops) % count)))
        pairs.append((2 * at + 1, 2 * ((at + hops) % count) + 1))
    return lax.ppermute(rows, (axis, "c"), pairs)


def swap(rows):
    return shift(rows, "c", 1)


def place_along_z(
    info, own, near, mid, far, last, near_p, mid_p, far_p, onward, kept, stack, flat, cut
):
    place, count = info[1], stack.shape[0]
    sign = 1 - 2 * info[3]
    stack[place] = own[...]
    stack[lax.rem(place + count // 2, count)] = last[...]
    for hops, mine, other in ((1, near, near_p), (2, mid, mid_p), (3, far, far_p)):
        stack[lax.rem(place + sign * hops + count, count)] = mine[...]
        stack[lax.rem(place - sign * hops + count, count)] = other[...]

    inner = flat.shape[1] // 2
    step = stack.shape[1] - 2 * cut
    for z in range(count):
        block = stack[z].astype(F32)
        side = 2 * z // count
        for number in range(2):
            for part in range(2):
                row = (2 * number * count + 4 * (z % (count // 2)) + 2 * part) * cut // 2
                flat[row : row + cut, side * inner : (side + 1) * inner] = block[
                    number * cut : (number + 1) * cut, part * inner : (part + 1) * inner
                ]
        row = 2 * count * cut + z * step
        flat[row : row + step] = block[2 * cut :]
    size = flat.shape[0] // 2
    lower, upper = flat[:size].astype(BF16), flat[size:].astype(BF16)

    @pl.when(info[3] == 0)
    def _():
        onward[...] = lower
        kept[...] = upper

    @pl.when(info[3] != 0)
    def _():
        onward[...] = upper
        kept[...] = lower


def place_along_x(
    info, own, own_k, near, near_k, near_p, near_pk, part, part_p, spatial, temporal, wide, out
):
    place, count = info[0], out.shape[0]
    half = part.shape[0]
    opposite = lax.rem(place + count // 2, count)

    def fill(index, first, second):
        out[index, :half] = first[...]
        out[index, half:] = second[...]

    @pl.when(info[3] == 0)
    def _():
        fill(place, own, own_k)
        fill(lax.rem(place + 1, count), near, near_k)
        fill(lax.rem(place - 1 + count, count), near_pk, near_p)
        fill(opposite, part, part_p)

    @pl.when(info[3] != 0)
    def _():
        fill(place, own_k, own)
        fill(lax.rem(place - 1 + count, count), near_k, near)
        fill(lax.rem(place + 1, count), near_p, near_pk)
        fill(opposite, part_p, part)

    cut, inner = out.shape[2] // count // 2, out.shape[2] // 2
    span = wide.shape[0] // count
    for x in range(count):
        for number, result in ((0, spatial), (1, temporal)):
            block = out[x, number * cut : (number + 1) * cut]
            result[2 * x * cut : (2 * x + 1) * cut] = block[:, :inner]
            result[(2 * x + 1) * cut : (2 * x + 2) * cut] = block[:, inner:]
        wide[x * span : (x + 1) * span] = out[x, 2 * cut :]


def in_vmem(body, info, blocks, results, scratch=()):
    vmem = pl.BlockSpec(memory_space=pltpu.VMEM)
    return pl.pallas_call(
        body,
        in_specs=[SCALARS] + [vmem] * len(blocks),
        out_specs=jax.tree.map(lambda _: vmem, results),
        out_shape=results,
        scratch_shapes=list(scratch),
        cost_estimate=pl.CostEstimate(flops=1, bytes_accessed=1, transcendentals=0),
        compiler_params=pltpu.CompilerParams(vmem_limit_bytes=VMEM_BYTES),
    )(info, *blocks)


def tie(*values):
    return lax.optimization_barrier(values)


def near_rows(out_spatial, qkv_temporal, out_temporal):
    half, narrow = out_spatial.shape
    packed = jnp.concatenate(
        [jnp.concatenate([out_spatial.T, out_temporal.T], axis=1), qkv_temporal.T], axis=0
    )
    near = jnp.transpose(lax.all_gather(packed, ("y", "c"), axis=0, tiled=False), (1, 0, 2))
    thin = near[:narrow, :, :half].reshape(narrow, -1)
    other = near[:narrow, :, half:].reshape(narrow, -1)
    wide = near[narrow:].reshape(near.shape[0] - narrow, -1)
    return (fold(thin), wide, fold(other))


def fold(rows):
    cut = rows.shape[-2] // 2
    return jnp.concatenate([rows[..., :cut, :], rows[..., cut:, :]], axis=-1)


def unfold(rows):
    cut = rows.shape[-1] // 2
    return jnp.concatenate([rows[..., :cut], rows[..., cut:]], axis=-2)


def gather_z(coords, rows, cut, beside):
    arrived = [shift_both(rows, "z", hops) for hops in (2, 1, 3)]
    arrived = [arrived[1], arrived[0], arrived[2], shift_both(arrived[0], "z", 2)]
    arrived, beside = tie(arrived, beside)
    swapped = [swap(block) for block in arrived[:3]]
    count, width = lax.axis_size("z"), rows.shape[1]
    half = shape_of(count * rows.shape[0] // 2, width)
    halves = in_vmem(
        functools.partial(place_along_z, cut=cut),
        coords,
        [rows] + arrived + swapped,
        (half, half),
        [pltpu.VMEM((count,) + rows.shape, BF16), pltpu.VMEM((2 * half.shape[0], width), F32)],
    )
    return halves, beside


def scatter(blocks, axis):
    count, place = lax.axis_size(axis), lax.axis_index(axis)
    arrived = []
    for hops in range(1, count):
        block = lax.dynamic_index_in_dim(blocks, (place + hops) % count, 0, keepdims=False)
        arrived.append(shift(block, axis, hops))
    return arrived


def halves_summed(keep, send):
    return (keep.astype(F32) + swap(send).astype(F32)).astype(BF16)


def spread(blocks, place, turned, outs):
    count = len(blocks)
    for index, block in enumerate(blocks):
        turned[lax.rem(index - place + count, count)] = block.astype(BF16)
    for hops, out in enumerate(outs):
        out[...] = turned[hops]


def regroup_wide(info, blocks, first, second, third, *outs):
    outs, turned = outs[:-1], outs[-1]
    y_count, span, lanes = turned.shape
    total = blocks[info[0]].astype(F32)
    for block in (first, second, third):
        total = total + block[...].astype(F32)
    tiles = [total[at : at + span] for at in range(0, total.shape[0], span)]
    flat = jnp.concatenate(tiles, axis=1)
    step = (flat.shape[1] - LANES // 2) // y_count
    rest = jnp.zeros((span, lanes - step), F32)
    cuts = [flat[:, y * step : (y + 1) * step] for y in range(y_count)]
    spread([jnp.concatenate([one, rest], axis=1) for one in cuts], info[2], turned, outs)


def regroup_pair(info, blocks, first, second, third, *outs):
    outs, turned = outs[:-1], outs[-1]
    x_count, span, lanes = turned.shape
    total = blocks[info[2]].astype(F32)
    for block in (first, second, third):
        total = total + block[...].astype(F32)
    width = x_count * span
    step = total.shape[0] // (width // LANES)
    tiles = [total[at : at + step].T for at in range(0, total.shape[0], step)]
    flat = jnp.concatenate(tiles, axis=0)
    flat = jnp.concatenate([flat, jnp.zeros((width, lanes - step), F32)], axis=1)
    cuts = [flat[x * span : (x + 1) * span] for x in range(x_count)]
    spread(cuts, info[0], turned, outs)


def regrouped(body, coords, blocks, arrived, span, count):
    one = shape_of(span, 2 * LANES)
    turned = pltpu.VMEM((count, span, 2 * LANES), BF16)
    return in_vmem(body, coords, [blocks] + arrived, (one,) * count, [turned])


def send_ahead(blocks, axis):
    return [shift(block, axis, hops + 1) for hops, block in enumerate(blocks[1:])]


def added(own, arrived):
    total = own.astype(F32)
    for block in arrived:
        total = total + block.astype(F32)
    return total.astype(BF16)


def reduce_grads(coords, wide, pair, inner, width, beside):
    x_count, y_count, z_count = (lax.axis_size(axis) for axis in ("x", "y", "z"))
    arrived, pair_in, beside = tie(scatter(wide, "x"), scatter(pair, "y"), beside)
    wide = regrouped(regroup_wide, coords, wide, arrived, 3 * inner // x_count, y_count)
    pair = regrouped(regroup_pair, coords, pair, pair_in, width // x_count, x_count)
    wide = added(wide[0], send_ahead(wide, "y")).reshape(z_count, -1, 2 * LANES)
    pair = added(pair[0], send_ahead(pair, "x")).reshape(z_count, -1, 2 * LANES)
    step = width // (2 * y_count)
    total = jnp.sum(exchange(jnp.concatenate([pair, wide], axis=1), "z").astype(F32), axis=0)
    narrow = pair.shape[1]
    half = step // 2
    summed = (total[:narrow, :half].T, total[narrow:, :step].T, total[:narrow, half:step].T)
    return summed, beside


def on_device(
    hidden,
    spatial_qkv,
    out_spatial,
    qkv_temporal,
    out_temporal,
    modulation,
    cotangent,
    frame_count,
    patch_height,
    patch_width,
):
    seq_count = lax.axis_size(("y", "c"))
    seq_place = lax.axis_index(("y", "c"))
    y_count = lax.axis_size("y")
    stream = hidden[0]
    grad_out = cotangent[0]
    packed_qkv = spatial_qkv[0]
    frame_dev, slot_total, width = stream.shape
    slot_dev = slot_total // seq_count
    inner = out_spatial.shape[0] * seq_count
    slots = 8
    groups = slot_dev // slots
    rows = frame_dev * seq_count * slots
    coords = jnp.stack([lax.axis_index(name) for name in ("x", "z", "y", "c")]).astype(jnp.int32)
    info = jnp.stack(
        [
            frame_count[0],
            patch_height[0] * patch_width[0],
            seq_place * slot_dev,
            seq_place * frame_dev,
            coords[3],
        ]
    ).astype(jnp.int32)

    def to_slots(tokens):
        split = tokens.reshape(frame_dev, seq_count, groups, slots, -1)
        split = jnp.transpose(split, (1, 2, 0, 3, 4))
        return exchange(split.reshape(seq_count, groups, frame_dev * slots, -1), ("y", "c"))

    def to_frames(tokens):
        moved = exchange(tokens, ("y", "c")).reshape(seq_count, groups, frame_dev, slots, -1)
        return jnp.transpose(moved, (2, 0, 1, 3, 4)).reshape(frame_dev, slot_total, -1)

    out_s = shape_of(frame_dev, slot_total, inner)
    out_s = run(
        spatial_forward,
        frame_dev,
        [info, packed_qkv],
        [SCALARS, per_frame(packed_qkv)],
        out_s,
        per_frame(out_s),
        [],
    )
    thin, wide, other = near_rows(out_spatial, qkv_temporal, out_temporal)
    rows_z = jnp.concatenate([thin, other, wide], axis=0)
    cut = thin.shape[0]
    stream_tied, _ = tie(stream, rows_z)
    stream_s = to_slots(stream_tied)
    (onward, kept), (stream_s, out_s) = gather_z(coords, rows_z, cut, (stream_s, out_s))
    out_s_s = to_slots(out_s)
    first = shift_both(onward, "x", 1)
    first_k, out_s_s = tie(shift_both(kept, "x", 1), out_s_s)
    second = shift_both(first, "x", 1)
    swapped = [swap(first), swap(first_k), swap(second)]
    grad_tied, swapped = tie(grad_out, swapped)
    grad_s = to_slots(grad_tied)
    x_count = lax.axis_size("x")
    w_spatial, w_temporal, w_qkv = in_vmem(
        place_along_x,
        coords,
        [onward, kept, first, first_k, swapped[0], swapped[1], second, swapped[2]],
        (shape_of(width, inner), shape_of(width, inner), shape_of(3 * inner, width)),
        [pltpu.VMEM((x_count, 2 * onward.shape[0], width), BF16)],
    )

    result = (
        shape_of(groups, rows, width),
        shape_of(groups, rows, width),
        shape_of(groups, rows, 3 * inner),
        shape_of(seq_count, groups, rows // seq_count, inner),
    )
    mixed_s, modulated, qkv_t, out_t = run(
        functools.partial(temporal_forward, slots=slots),
        groups,
        [info, modulation, stream_s, out_s_s, w_spatial, w_qkv],
        [SCALARS, whole(modulation), per_group(stream_s), per_group(out_s_s), whole(w_spatial), whole(w_qkv)],
        result,
        [per_frame(result[0]), per_frame(result[1]), per_frame(result[2]), per_group(result[3])],
        [],
    )
    out_t_tied, _ = tie(out_t, grad_s)
    out_t_f = to_frames(out_t_tied)

    wide_rows, pair_rows = term_rows(inner, width, y_count, x_count)
    result = (
        shape_of(seq_count, groups, rows // seq_count, width),
        shape_of(x_count, wide_rows, LANES),
        shape_of(y_count, pair_rows, LANES),
        shape_of(x_count, wide_rows, LANES),
        shape_of(y_count, pair_rows, LANES),
    )
    tokens = groups * rows
    kept = [(inner,), (inner,), (3 * inner,), (width,), (width,)]
    kept = [pltpu.VMEM((tokens,) + shape, BF16) for shape in kept]
    kept.append(pltpu.VMEM((2, tokens, width // 2), BF16))
    ln_grad, wide_keep, pair_keep, wide_send, pair_send = run(
        functools.partial(temporal_backward, slots=slots, y_count=y_count),
        groups,
        [info, modulation, grad_s, mixed_s, out_s_s, qkv_t, out_t, modulated, w_temporal, w_qkv],
        [
            SCALARS,
            whole(modulation),
            per_group(grad_s),
            per_frame(mixed_s),
            per_group(out_s_s),
            per_frame(qkv_t),
            per_group(out_t),
            per_frame(modulated),
            whole(w_temporal),
            whole(w_qkv),
        ],
        result,
        [per_group(result[0])] + [whole(part) for part in result[1:]],
        kept,
    )
    wide_send, out_t_f = tie(wide_send, out_t_f)
    wide = halves_summed(wide_keep, wide_send)
    pair = halves_summed(pair_keep, pair_send)
    ln_frames = to_frames(ln_grad)

    result = (shape_of(frame_dev, slot_total, width), shape_of(frame_dev, slot_total, 3 * inner))
    hidden_grad, qkv_s_grad = run(
        spatial_backward,
        frame_dev,
        [info, grad_out, ln_frames, packed_qkv, out_s, w_spatial],
        [
            SCALARS,
            per_frame(grad_out),
            per_frame(ln_frames),
            per_frame(packed_qkv),
            per_frame(out_s),
            whole(w_spatial),
        ],
        result,
        [per_frame(result[0]), per_frame(result[1])],
        [],
    )
    summed, qkv_s_grad = reduce_grads(coords, wide, pair, inner, width, qkv_s_grad)
    block_out = shape_of(frame_dev, slot_total, width)
    block_out = run(
        block_forward,
        frame_dev,
        [info, modulation, stream, out_s, out_t_f, w_spatial, w_temporal],
        [
            SCALARS,
            whole(modulation),
            per_frame(stream),
            per_frame(out_s),
            per_frame(out_t_f),
            whole(w_spatial),
            whole(w_temporal),
        ],
        block_out,
        per_frame(block_out),
        [],
    )
    return (block_out[None], hidden_grad[None], qkv_s_grad[None], summed[0], summed[1], summed[2])


def solution(mesh):
    torus = Mesh(mesh.devices.reshape(4, 8, 4, 2), ("x", "z", "y", "c"))
    dp, seq = ("x", "z"), ("y", "c")
    tokens = P(dp, seq, None, None)
    weight = P(seq, dp)
    placed = (
        tokens,
        tokens,
        weight,
        weight,
        weight,
        P(dp, None, None),
        tokens,
        P(dp),
        P(dp),
        P(dp),
    )
    return jax.shard_map(
        on_device,
        mesh=torus,
        in_specs=placed,
        out_specs=(tokens, tokens, tokens, weight, weight, weight),
        check_vma=False,
    )
```
